32 devices in a mesh: sens: 8 (over y, x, core), hour: 4 (over z).
Axes of the slice: x: 2, y: 2, z: 4, core: 2. Of those that a mesh axis runs over, the one named last changes fastest.
Arguments:
- sky: bfloat16 [512, 146], P('hour'), may hold values from 0.049804688 to 1
- sky_open: bfloat16 [146, 16384], P(None, 'sens'), may hold values from 0 to 0.013977051
- sky_closed: bfloat16 [146, 16384], P(None, 'sens'), may hold values from 0 to 0.0039978027
- sun_coef: bfloat16 [5165, 16384], P(None, ('sens', 'hour')), may hold values from 0 to 1
- sun_bins: int32 [512, 4], P('hour'), may hold values from 0 to 5164, as said below
- sun_rad: bfloat16 [512, 4], P('hour'), may hold values from 0.099609375 to 1
- target: bfloat16 [512, 16384], P('hour', 'sens'), may hold values from 0 to 2
- zone_of: int32 [8192, 1], P('sens'), may hold values from 0 to 7
- area: float32 [8192], P('sens'), may hold values from 0.5 to 4
- openness: float32 [8192], P('sens'), may hold values from 0 to 1
Outputs:
- illuminance: bfloat16 [512, 16384], P('hour', 'sens')
- new_openness: float32 [8192], P('sens')
The draws below stay inside these ranges and needn't reach their ends.
Inputs may be any that keep to these rules, and one draw needn't show every extreme that they name: `sun_bins`: the 4 bins of one hour are consecutive modulo 5165, hence distinct. `zone_of`: every zone has at least one window.
All inputs are finite; a program needn't handle non-finite values.
Results may differ from the reference program's by a relative error of at most 0.001.
Values may be sent and summed in bfloat16 or wider, within the bound.
No kernel may reach another device: no remote copies, remote signals or barrier semaphores. Data moves between devices by JAX's collectives and lax.ppermute only.
A program may use at most 128 MiB of HBM per device.

```python
import math
import jax
import jax.numpy as jnp
from jax import lax

NBINS = 5165
PATCHES = 146
KBINS = 4
HOURS = 512
SENS_BLK = 2048
SENSORS = 16384
ZONES = 8
WIN = 8192


def draw_sun_bins(key, part):
    start = jax.random.randint(key, (HOURS,), 0, NBINS)
    start = start.at[0].set(NBINS - KBINS).at[1].set(0)
    return ((start[:, None] + jnp.arange(KBINS)[None, :]) % NBINS).astype(jnp.int32)


def block_levels(own_key, dims, shards, low, largest):
    def one(dim, shards_of):
        heights = jax.random.uniform(jax.random.fold_in(jax.random.fold_in(own_key, 6), dim), (shards_of,), jnp.float32, low / len(shards), largest / len(shards))
        return jnp.repeat(jnp.exp(heights), dims[dim] // shards_of).reshape((-1,) + (1,) * (len(dims) - dim - 1))

    factor_of = one(*shards[0])
    for cut in shards[1:]:
        factor_of = factor_of * one(*cut)
    return factor_of


def different_ones(key, rows, count, top, lift):
    ranking = jax.random.permutation(jax.random.fold_in(key, 1), count)
    favour = ranking
    for power in range(3):
        favour = favour * favour // count
    favour = favour * lift // count
    chance = jax.random.randint(jax.random.fold_in(key, 2), (rows, count), 0, 4096) + favour
    sure = jax.random.permutation(jax.random.fold_in(key, 3), rows)[jnp.arange(count) % rows]
    chance = jnp.where(jnp.arange(rows)[:, None] == sure[None, :], 1 << 14, chance)
    merit = chance * count + jnp.arange(count)
    return lax.top_k(merit.astype(jnp.int32), top)[1].astype(jnp.int32)


def setup_inputs(seed: int = 0) -> dict:
    keys = jax.random.split(jax.random.key(seed), 11)
    return {
        "sky": jnp.clip(jnp.exp(math.log(1.0) - 2.9996462 * jax.random.uniform(keys[0], (HOURS, PATCHES), jnp.float32) ** block_levels(keys[0], (HOURS, PATCHES), ((0, 4),), -0.2, 0.2)), 0.049804688, 1.0).astype(jnp.bfloat16),
        "sky_open": jnp.clip(0.013977051 * jax.random.uniform(keys[1], (PATCHES, SENSORS), jnp.float32) ** block_levels(keys[1], (PATCHES, SENSORS), ((1, 8),), -0.2, 0.2), 0.0, 0.013977051).astype(jnp.bfloat16),
        "sky_closed": jnp.clip(0.0039978027 * jax.random.uniform(keys[2], (PATCHES, SENSORS), jnp.float32) ** block_levels(keys[2], (PATCHES, SENSORS), ((1, 8),), -0.2, 0.2), 0.0, 0.0039978027).astype(jnp.bfloat16),
        "sun_coef": jnp.clip(1.0 * jax.random.uniform(keys[3], (NBINS, SENSORS), jnp.float32) ** block_levels(keys[3], (NBINS, SENSORS), ((1, 32),), -0.2, 0.2), 0.0, 1.0).astype(jnp.bfloat16),
        "sun_bins": draw_sun_bins(jax.random.fold_in(keys[10], 71), 0),
        "sun_rad": jnp.clip(jnp.exp(math.log(1.0) - 2.306499 * jax.random.uniform(keys[5], (HOURS, KBINS), jnp.float32) ** block_levels(keys[5], (HOURS, KBINS), ((0, 4),), -0.2, 0.2)), 0.099609375, 1.0).astype(jnp.bfloat16),
        "target": jnp.clip(2.0 * jax.random.uniform(keys[6], (HOURS, SENSORS), jnp.float32) ** block_levels(keys[6], (HOURS, SENSORS), ((0, 4), (1, 8)), -0.2, 0.2), 0.0, 2.0).astype(jnp.bfloat16),
        "zone_of": different_ones(keys[7], WIN, ZONES, 1, 2048),
        "area": jnp.clip(jnp.exp(math.log(4.0) - 2.0794415 * jax.random.uniform(keys[8], (WIN,), jnp.float32) ** block_levels(keys[8], (WIN,), ((0, 8),), -0.2, 0.2)), 0.5, 4.0),
        "openness": jnp.clip(1.0 * jax.random.uniform(keys[9], (WIN,), jnp.float32) ** block_levels(keys[9], (WIN,), ((0, 8),), -0.2, 0.2), 0.0, 1.0),
    }


def reference(sky, sky_open, sky_closed, sun_coef, sun_bins, sun_rad, target, zone_of, area, openness):
    member = (zone_of[:, 0][:, None] == jnp.arange(ZONES, dtype=jnp.int32)[None, :]).astype(jnp.float32)
    stacked = jnp.stack([area * openness, area, area * area])
    sums = jnp.dot(stacked, member, precision=lax.Precision.HIGHEST)
    share = sums[0] / sums[1]
    op_part = jnp.dot(sky, sky_open, preferred_element_type=jnp.float32)
    cl_part = jnp.dot(sky, sky_closed, preferred_element_type=jnp.float32)
    picked = jnp.take(sun_coef, sun_bins.reshape(-1), axis=0).reshape(HOURS, KBINS, SENSORS)
    sun_part = jnp.einsum('hk,hks->hs', sun_rad.astype(jnp.float32), picked.astype(jnp.float32))
    cross = op_part - cl_part + sun_part
    share_s = jnp.repeat(share, SENS_BLK)
    lit = cl_part + share_s[None, :] * cross
    terms = lax.optimization_barrier(jnp.sum(2.0 * (lit - target.astype(jnp.float32)) * cross, axis=0))
    zone_grad = lax.optimization_barrier(jnp.sum(terms.reshape(ZONES, SENS_BLK), axis=1))
    ratio = zone_grad / sums[1]
    grad = area * jnp.dot(member, ratio, precision=lax.Precision.HIGHEST)
    rms = jnp.sqrt(jnp.sum(grad * grad) / WIN + 1e-06)
    new_openness = jnp.clip(openness - 0.25 * grad / rms, 0.0, 1.0)
    return (lit.astype(jnp.bfloat16), new_openness)
```

```python
import jax
import jax.numpy as jnp
from jax import lax
from jax.experimental import pallas as pl
from jax.experimental.pallas import tpu as pltpu
from jax.sharding import PartitionSpec as P

LANES = 128
CHUNK = 1024


def exchange(x, axis, mask):
    size = lax.axis_size(axis)
    return lax.ppermute(x, axis, [(i, i ^ mask) for i in range(size)])


def group_sum(x, axis):
    size = lax.axis_size(axis)
    assert size & (size - 1) == 0
    step = 1
    while step < size:
        radix = min(8, size // step)
        terms = [x] + [exchange(x, axis, m * step) for m in range(1, radix)]
        while len(terms) > 1:
            terms = [a + b for a, b in zip(terms[::2], terms[1::2])]
        x = terms[0]
        step *= radix
    return x


def lit_kernel(nbins, chunks, groups, kbins, patches):
    def kernel(place_ref, share_ref, *refs):
        packed = refs[:groups]
        open_ref, closed_ref, coef_ref = refs[groups : groups + 3]
        lits = refs[groups + 3 : 2 * groups + 3]
        cross_ref, own_ref, acc, pattern, block = refs[2 * groups + 3 :]
        rows = packed[0].shape[0]
        step = pl.program_id(0)

        @pl.when(step == 0)
        def _():
            lane = lax.broadcasted_iota(jnp.int32, (rows, LANES), 1)
            for g in range(groups):
                small = packed[g][:, patches : patches + 3 * kbins].astype(jnp.float32)
                value = jnp.zeros((rows, LANES), jnp.float32)
                where = jnp.zeros((rows, LANES), jnp.float32)
                for k in range(kbins):
                    low = small[:, 2 * kbins + k : 2 * kbins + k + 1].astype(jnp.int32)
                    hit = lane == low
                    value = jnp.where(hit, small[:, k : k + 1], value)
                    where = jnp.where(hit, small[:, kbins + k : kbins + k + 1], where)
                pattern[g * rows : (g + 1) * rows] = value
                block[g * rows : (g + 1) * rows] = where

        def weights(first, count):
            parts = []
            for c in range(count):
                here = block[:] == (first + c).astype(jnp.float32)
                parts.append(jnp.where(here, pattern[:], 0.0).astype(jnp.bfloat16))
            return jnp.concatenate(parts, axis=1) if count > 1 else parts[0]

        per = CHUNK // LANES
        last = nbins - (chunks - 1) * CHUNK
        last_parts = pl.cdiv(last, LANES)

        @pl.when(step < chunks - 1)
        def _():
            part = jnp.dot(weights(step * per, per), coef_ref[:], preferred_element_type=jnp.float32)

            @pl.when(step == 0)
            def _():
                acc[:] = part

            @pl.when(step > 0)
            def _():
                acc[:] = acc[:] + part

        @pl.when(step == chunks - 1)
        def _():
            tail = coef_ref[: last_parts * LANES]
            row = lax.broadcasted_iota(jnp.int32, tail.shape, 0)
            tail = jnp.where(row < last, tail, jnp.zeros_like(tail))
            part = jnp.dot(weights(step * per, last_parts), tail, preferred_element_type=jnp.float32)
            share = share_ref[0]
            total = jnp.zeros((8, acc.shape[1]), jnp.float32)
            for g in range(groups):
                sky = packed[g][:, :patches]
                at = slice(g * rows, (g + 1) * rows)
                op = jnp.dot(sky, open_ref[:], preferred_element_type=jnp.float32)
                cl = jnp.dot(sky, closed_ref[:], preferred_element_type=jnp.float32)
                cross = op - cl + (acc[at] + part[at])
                lit = cl + share * cross
                lits[g][:] = lit.astype(jnp.bfloat16)
                cross_ref[at] = cross
                total = total + jnp.sum((lit * cross).reshape(rows // 8, 8, -1), axis=0)
            own_ref[:] = total

    return kernel


def grad_kernel(groups):
    def kernel(own_ref, cross_ref, *refs):
        targets, out_ref = refs[:groups], refs[groups]
        rows = targets[0].shape[0]
        total = own_ref[:]
        for g in range(groups):
            term = targets[g][:].astype(jnp.float32) * cross_ref[g * rows : (g + 1) * rows]
            total = total - jnp.sum(term.reshape(rows // 8, 8, -1), axis=0)
        out_ref[:] = jnp.broadcast_to(2.0 * jnp.sum(total), out_ref.shape)

    return kernel


def place_kernel(groups):
    def kernel(me_ref, *refs):
        blocks, out_ref, sems = refs[:groups], refs[groups], refs[groups + 1]
        width = blocks[0].shape[1]
        copies = []
        for g in range(groups):
            at = pl.multiple_of((me_ref[0] ^ g) * width, LANES)
            copies.append(pltpu.make_async_copy(blocks[g], out_ref.at[:, pl.ds(at, width)], sems.at[g]))
        for c in copies:
            c.start()
        for c in copies:
            c.wait()

    return kernel


def local(sky, sky_open, sky_closed, sun_coef, sun_bins, sun_rad, target, zone_of, area, openness):
    zone_count = lax.axis_size("sens")
    groups = lax.axis_size("hour")
    assert groups & (groups - 1) == 0
    own_zone = lax.axis_index("sens")
    own_hour = lax.axis_index("hour").astype(jnp.int32)
    rows, patches = sky.shape
    kbins = sun_bins.shape[1]
    nbins, width = sun_coef.shape
    assert nbins < kbins or nbins % LANES == 0 or nbins % LANES >= 2 * kbins
    assert nbins <= 256 * LANES and width % LANES == 0

    packed = jnp.concatenate(
        [sky, sun_rad, (sun_bins // LANES).astype(jnp.bfloat16), (sun_bins % LANES).astype(jnp.bfloat16)], axis=1
    )
    packs = [packed] + [exchange(packed, "hour", m) for m in range(1, groups)]

    zones = jnp.arange(zone_count, dtype=jnp.int32)
    member = (zone_of[:, 0][:, None] == zones[None, :]).astype(jnp.float32)
    stacked = jnp.stack([area * openness, area, area * area])
    totals = group_sum(jnp.dot(stacked, member, precision=lax.Precision.HIGHEST), "sens")
    mine = lax.dynamic_slice_in_dim(totals, own_zone, 1, 1)[:, 0]
    share = mine[0] / mine[1]

    def column_block(x, m):
        return lax.dynamic_slice_in_dim(x, (own_hour ^ m) * width, width, 1)

    targets = [column_block(target, 0)]
    targets += [exchange(column_block(target, m), "hour", m) for m in range(1, groups)]

    chunks = pl.cdiv(nbins, CHUNK)
    hours = rows * groups
    whole = lambda shape: pl.BlockSpec(shape, lambda i, place, share: (0,) * len(shape))
    column = pl.BlockSpec((patches, width), lambda i, place, share: (0, place[0]))
    results = pl.pallas_call(
        lit_kernel(nbins, chunks, groups, kbins, patches),
        grid_spec=pltpu.PrefetchScalarGridSpec(
            num_scalar_prefetch=2,
            grid=(chunks,),
            in_specs=[whole(packed.shape)] * groups
            + [column, column, pl.BlockSpec((CHUNK, width), lambda i, place, share: (i, 0))],
            out_specs=[whole((rows, width))] * groups + [whole((hours, width)), whole((8, width))],
            scratch_shapes=[
                pltpu.VMEM((hours, width), jnp.float32),
                pltpu.VMEM((hours, LANES), jnp.float32),
                pltpu.VMEM((hours, LANES), jnp.float32),
            ],
        ),
        out_shape=[jax.ShapeDtypeStruct((rows, width), jnp.bfloat16)] * groups
        + [jax.ShapeDtypeStruct((hours, width), jnp.float32), jax.ShapeDtypeStruct((8, width), jnp.float32)],
        compiler_params=pltpu.CompilerParams(vmem_limit_bytes=32 * 1024 * 1024),
        cost_estimate=pl.CostEstimate(
            flops=2 * hours * (nbins + 2 * patches) * width, bytes_accessed=2 * nbins * width, transcendentals=0
        ),
        name="lit",
    )(own_hour[None], share[None], *packs, sky_open, sky_closed, sun_coef)
    lits, cross, own_sum = results[:groups], results[groups], results[groups + 1]
    sent = [lits[0]] + [exchange(lits[m], "hour", m) for m in range(1, groups)]

    local_grad = pl.pallas_call(
        grad_kernel(groups),
        out_shape=jax.ShapeDtypeStruct((1, LANES), jnp.float32),
        cost_estimate=pl.CostEstimate(flops=2 * hours * width, bytes_accessed=6 * hours * width, transcendentals=0),
        name="grad",
    )(own_sum, cross, *targets)[0, :1]
    zone_grad = group_sum(local_grad, "hour")
    ratio = group_sum(jnp.where(zones == own_zone, zone_grad / mine[1], 0.0), "sens")
    rms = jnp.sqrt(jnp.sum(ratio * ratio * totals[2]) / (area.shape[0] * zone_count) + 1e-06)
    grad = area * jnp.dot(member, ratio, precision=lax.Precision.HIGHEST)
    new_openness = jnp.clip(openness - 0.25 * grad / rms, 0.0, 1.0)

    illuminance = pl.pallas_call(
        place_kernel(groups),
        in_specs=[pl.BlockSpec(memory_space=pltpu.SMEM)] + [pl.BlockSpec(memory_space=pl.ANY)] * groups,
        out_specs=pl.BlockSpec(memory_space=pl.ANY),
        out_shape=jax.ShapeDtypeStruct((rows, groups * width), jnp.bfloat16),
        scratch_shapes=[pltpu.SemaphoreType.DMA((groups,))],
        name="place",
    )(own_hour[None], *sent)
    return (illuminance, new_openness)


def solution(mesh):
    in_specs = (
        P("hour", None),
        P(None, "sens"),
        P(None, "sens"),
        P(None, ("sens", "hour")),
        P("hour", None),
        P("hour", None),
        P("hour", "sens"),
        P("sens", None),
        P("sens"),
        P("sens"),
    )
    out_specs = (P("hour", "sens"), P("sens"))
    return jax.shard_map(local, mesh=mesh, in_specs=in_specs, out_specs=out_specs, check_vma=False)
```

```python
import jax
import jax.numpy as jnp
from jax import lax
from jax.experimental import pallas as pl
from jax.experimental.pallas import tpu as pltpu
from jax.sharding import PartitionSpec as P

LANES = 128
CHUNK = 1024
HEAD = 16
VMEM_BYTES = 32 * 1024 * 1024


def call(kernel, name, out_shape, flops=0, moved=0, **more):
    return pl.pallas_call(
        kernel,
        out_shape=out_shape,
        name=name,
        compiler_params=pltpu.CompilerParams(vmem_limit_bytes=VMEM_BYTES),
        cost_estimate=pl.CostEstimate(flops=flops, bytes_accessed=moved, transcendentals=0),
        **more,
    )


def pack_kernel(sky_ref, bins_ref, rad_ref, out_ref):
    bins = bins_ref[:]
    kbins = bins.shape[0]
    fill = jnp.zeros((HEAD - 3 * kbins, bins.shape[1]), jnp.float32)
    parts = [rad_ref[:].astype(jnp.float32), (bins // LANES).astype(jnp.float32), (bins % LANES).astype(jnp.float32)]
    head = jnp.concatenate(parts + [fill], axis=0).astype(jnp.bfloat16)
    for g in range(out_ref.shape[0]):
        out_ref[g, :HEAD] = head
        out_ref[g, HEAD:] = sky_ref[:]


def sums_kernel(zone_ref, area_ref, openness_ref, target_ref, sums_ref, split_ref):
    zone, area = zone_ref[:], area_ref[:]
    lane = lax.broadcasted_iota(jnp.int32, (1, LANES), 1)
    values = [area * openness_ref[:], area, area * area]
    for z in range(sums_ref.shape[0]):
        member = zone == z
        row = jnp.zeros((1, LANES), jnp.float32)
        for k, value in enumerate(values):
            row = jnp.where(lane == k, jnp.sum(jnp.where(member, value, 0.0), keepdims=True), row)
        sums_ref[z] = row
    width = split_ref.shape[2]
    for g in range(split_ref.shape[0]):
        split_ref[g] = target_ref[:, g * width : (g + 1) * width]


def lit_kernel(nbins, chunks, groups, kbins, patches):
    def kernel(place_ref, sums_ref, packed, open_ref, closed_ref, coef_ref, lits, cross_ref, own_ref, acc, pattern, block):
        rows = packed.shape[2]
        step = pl.program_id(0)

        @pl.when(step == 0)
        def _():
            lane = lax.broadcasted_iota(jnp.int32, (rows, LANES), 1)
            for g in range(groups):
                small = packed[g, :HEAD].astype(jnp.float32).T
                value = jnp.zeros((rows, LANES), jnp.float32)
                where = jnp.zeros((rows, LANES), jnp.float32)
                for k in range(kbins):
                    low = small[:, 2 * kbins + k : 2 * kbins + k + 1].astype(jnp.int32)
                    hit = lane == low
                    value = jnp.where(hit, small[:, k : k + 1], value)
                    where = jnp.where(hit, small[:, kbins + k : kbins + k + 1], where)
                pattern[g * rows : (g + 1) * rows] = value
                block[g * rows : (g + 1) * rows] = where

        def weights(first, count):
            parts = []
            for c in range(count):
                here = block[:] == (first + c).astype(jnp.float32)
                parts.append(jnp.where(here, pattern[:], 0.0).astype(jnp.bfloat16))
            return jnp.concatenate(parts, axis=1) if count > 1 else parts[0]

        per = CHUNK // LANES
        last = nbins - (chunks - 1) * CHUNK
        last_parts = pl.cdiv(last, LANES)

        @pl.when(step < chunks - 1)
        def _():
            part = jnp.dot(weights(step * per, per), coef_ref[:], preferred_element_type=jnp.float32)

            @pl.when(step == 0)
            def _():
                acc[:] = part

            @pl.when(step > 0)
            def _():
                acc[:] = acc[:] + part

        @pl.when(step == chunks - 1)
        def _():
            tail = coef_ref[: last_parts * LANES]
            row = lax.broadcasted_iota(jnp.int32, tail.shape, 0)
            tail = jnp.where(row < last, tail, jnp.zeros_like(tail))
            part = jnp.dot(weights(step * per, last_parts), tail, preferred_element_type=jnp.float32)
            mine = jnp.sum(sums_ref[:], axis=0)
            share = mine[:, 0:1] / mine[:, 1:2]
            total = jnp.zeros((8, acc.shape[1]), jnp.float32)
            for g in range(groups):
                sky = packed[g, HEAD:]
                at = slice(g * rows, (g + 1) * rows)
                over = (((0,), (0,)), ((), ()))
                op = lax.dot_general(sky, open_ref[:], over, preferred_element_type=jnp.float32)
                cl = lax.dot_general(sky, closed_ref[:], over, preferred_element_type=jnp.float32)
                cross = op - cl + (acc[at] + part[at])
                lit = cl + share * cross
                lits[g] = lit.astype(jnp.bfloat16)
                cross_ref[at] = cross
                total = total + jnp.sum((lit * cross).reshape(rows // 8, 8, -1), axis=0)
            own_ref[:] = total

    return kernel


def grad_kernel(sums_ref, own_ref, cross_ref, targets, out_ref):
    groups, rows, _ = targets.shape
    total = own_ref[:]
    for g in range(groups):
        term = targets[g].astype(jnp.float32) * cross_ref[g * rows : (g + 1) * rows]
        total = total - jnp.sum(term.reshape(rows // 8, 8, -1), axis=0)
    mine = jnp.sum(sums_ref[:], axis=0)
    lane = lax.broadcasted_iota(jnp.int32, (1, LANES), 1)
    ratio = 2.0 * jnp.sum(total, keepdims=True) / mine[:, 1:2]
    row = jnp.where(lane == 0, ratio, jnp.where(lane == 1, mine[:, 2:3], 0.0))
    out_ref[:] = jnp.broadcast_to(row[None], out_ref.shape)


def step_kernel(groups, windows):
    def kernel(heard_ref, zone_ref, area_ref, openness_ref, out_ref):
        zone = zone_ref[:]
        chosen = jnp.zeros(zone.shape, jnp.float32)
        square = jnp.zeros((1, 1), jnp.float32)
        for z in range(heard_ref.shape[0] // groups):
            heard = heard_ref[z * groups : (z + 1) * groups]
            ratio = jnp.sum(heard, axis=0)[:, 0:1]
            square = square + ratio * ratio * heard[0, :, 1:2]
            chosen = jnp.where(zone == z, ratio, chosen)
        rms = jnp.sqrt(square / windows + 1e-06)
        out_ref[:] = jnp.clip(openness_ref[:] - 0.25 * (area_ref[:] * chosen) / rms, 0.0, 1.0)

    return kernel


def place_kernel(blocks, out_ref):
    width = blocks.shape[2]
    for g in range(blocks.shape[0]):
        out_ref[:, g * width : (g + 1) * width] = blocks[g]


def local(sky, sky_open, sky_closed, sun_coef, sun_bins, sun_rad, target, zone_of, area, openness):
    zones = lax.axis_size("sens")
    groups = lax.axis_size("hour")
    own_hour = lax.axis_index("hour").astype(jnp.int32)
    rows, patches = sky.shape
    kbins = sun_bins.shape[1]
    nbins, width = sun_coef.shape
    hours = rows * groups
    windows = area.shape[0]
    assert nbins % LANES == 0 or nbins % LANES >= 2 * kbins
    assert nbins <= 256 * LANES and width % LANES == 0 and windows % LANES == 0 and 3 * kbins <= HEAD
    shape = jax.ShapeDtypeStruct
    f32, bf16 = jnp.float32, jnp.bfloat16

    packed = call(pack_kernel, "pack", shape((groups, HEAD + patches, rows), bf16))(sky.T, sun_bins.T, sun_rad.T)
    packs = lax.all_to_all(packed, "hour", 0, 0)

    tiles = (windows // LANES, LANES)
    zone2, area2, openness2 = zone_of.reshape(tiles), area.reshape(tiles), openness.reshape(tiles)
    zone_sums, split = call(
        sums_kernel,
        "sums",
        [shape((zones, 1, LANES), f32), shape((groups, rows, width), bf16)],
        moved=4 * hours * width,
    )(zone2, area2, openness2, target)
    mine = lax.all_to_all(zone_sums, "sens", 0, 0)
    targets = lax.all_to_all(split, "hour", 0, 0)

    chunks = pl.cdiv(nbins, CHUNK)
    whole = lambda dims: pl.BlockSpec(dims, lambda i, place: (0,) * len(dims))
    column = pl.BlockSpec((patches, width), lambda i, place: (0, place[0]))
    lits, cross, own_sum = call(
        lit_kernel(nbins, chunks, groups, kbins, patches),
        "lit",
        [shape((groups, rows, width), bf16), shape((hours, width), f32), shape((8, width), f32)],
        flops=2 * hours * (nbins + 2 * patches) * width,
        moved=2 * nbins * width,
        grid_spec=pltpu.PrefetchScalarGridSpec(
            num_scalar_prefetch=1,
            grid=(chunks,),
            in_specs=[whole(mine.shape), whole(packs.shape), column, column]
            + [pl.BlockSpec((CHUNK, width), lambda i, place: (i, 0))],
            out_specs=[whole((groups, rows, width)), whole((hours, width)), whole((8, width))],
            scratch_shapes=[
                pltpu.VMEM((hours, width), f32),
                pltpu.VMEM((hours, LANES), f32),
                pltpu.VMEM((hours, LANES), f32),
            ],
        ),
    )(own_hour[None], mine, packs, sky_open, sky_closed, sun_coef)
    placed = lax.all_to_all(lits, "hour", 0, 0)

    message = call(
        grad_kernel,
        "grad",
        shape((zones * groups, 1, LANES), f32),
        flops=2 * hours * width,
        moved=6 * hours * width,
    )(mine, own_sum, cross, targets)
    heard = lax.all_to_all(message, ("sens", "hour"), 0, 0)
    new_openness = call(step_kernel(groups, windows * zones), "step", shape(tiles, f32))(heard, zone2, area2, openness2)
    illuminance = call(place_kernel, "place", shape((rows, groups * width), bf16), moved=4 * hours * width)(placed)
    return (illuminance, new_openness.reshape(-1))


def solution(mesh):
    in_specs = (
        P("hour", None),
        P(None, "sens"),
        P(None, "sens"),
        P(None, ("sens", "hour")),
        P("hour", None),
        P("hour", None),
        P("hour", "sens"),
        P("sens", None),
        P("sens"),
        P("sens"),
    )
    out_specs = (P("hour", "sens"), P("sens"))
    return jax.shard_map(local, mesh=mesh, in_specs=in_specs, out_specs=out_specs, check_vma=False)
```

```python
import jax
import jax.numpy as jnp
from jax import lax
from jax.experimental import pallas as pl
from jax.experimental.pallas import tpu as pltpu
from jax.sharding import PartitionSpec as P

LANES = 128
CHUNK = 8
HEAD = 16
TAIL = 8
PATTERN = jnp.bfloat16
LEVELS = 65000.0
VMEM_BYTES = 40 * 1024 * 1024
HBM = pl.BlockSpec(memory_space=pltpu.HBM)
SMEM = pl.BlockSpec(memory_space=pltpu.SMEM)
VMEM = pl.BlockSpec(memory_space=pltpu.VMEM)


def call(kernel, name, out_shape, flops=0, moved=0, **more):
    return pl.pallas_call(
        kernel,
        out_shape=out_shape,
        name=name,
        compiler_params=pltpu.CompilerParams(vmem_limit_bytes=VMEM_BYTES),
        cost_estimate=pl.CostEstimate(flops=flops, bytes_accessed=moved, transcendentals=0),
        **more,
    )


def fetch(pairs, sems):
    copies = [pltpu.make_async_copy(source, place, sems.at[i]) for i, (source, place) in enumerate(pairs)]
    for c in copies:
        c.start()
    return copies


def pack_kernel(bins_hbm, rad_hbm, out_ref, bins_ref, rad_ref, sems):
    for c in fetch([(bins_hbm, bins_ref), (rad_hbm, rad_ref)], sems):
        c.wait()
    bins = bins_ref[:]
    kbins = bins.shape[0]
    fill = jnp.zeros((HEAD - 3 * kbins, bins.shape[1]), jnp.float32)
    parts = [rad_ref[:].astype(jnp.float32), (bins // LANES).astype(jnp.float32), (bins % LANES).astype(jnp.float32)]
    head = jnp.concatenate(parts + [fill], axis=0).astype(jnp.bfloat16)
    for g in range(out_ref.shape[0]):
        out_ref[g] = head


def sums_kernel(zones):
    def kernel(zone_hbm, area_hbm, openness_hbm, out_ref, zone_ref, area_ref, openness_ref, sems):
        for c in fetch([(zone_hbm, zone_ref), (area_hbm, area_ref), (openness_hbm, openness_ref)], sems):
            c.wait()
        zone, area = zone_ref[:], area_ref[:]
        lane = lax.broadcasted_iota(jnp.int32, (1, LANES), 1)
        values = [area * openness_ref[:], area, area * area]
        rows = [jnp.zeros((1, LANES), jnp.float32)] * len(values)
        for z in range(zones):
            member = zone == z
            for k, value in enumerate(values):
                rows[k] = jnp.where(lane == z, jnp.sum(jnp.where(member, value, 0.0), keepdims=True), rows[k])
        out_ref[:] = jnp.zeros_like(out_ref)
        for k, row in enumerate(rows):
            out_ref[k : k + 1] = row

    return kernel


def fetch_kernel(coef_hbm, tail_hbm, out_ref, sems):
    tail = tail_hbm.shape[0]
    whole = out_ref.shape[0] - tail
    pairs = [(coef_hbm.at[pl.ds(0, whole)], out_ref.at[pl.ds(0, whole)]), (tail_hbm, out_ref.at[pl.ds(whole, tail)])]
    for c in fetch(pairs, sems):
        c.wait()


def sun_kernel(groups, kbins):
    def kernel(heads, coef_ref, out_ref, acc, pattern, block):
        rows = heads.shape[2]
        lane = lax.broadcasted_iota(jnp.int32, (rows, LANES), 1)
        for g in range(groups):
            small = heads[g].astype(jnp.float32).T
            value = jnp.zeros((rows, LANES), jnp.float32)
            where = jnp.zeros((rows, LANES), jnp.float32)
            for k in range(kbins):
                low = small[:, 2 * kbins + k : 2 * kbins + k + 1].astype(jnp.int32)
                hit = lane == low
                value = jnp.where(hit, small[:, k : k + 1], value)
                where = jnp.where(hit, small[:, kbins + k : kbins + k + 1], where)
            pattern[g * rows : (g + 1) * rows] = value.astype(pattern.dtype)
            block[g * rows : (g + 1) * rows] = where.astype(block.dtype)

        blocks = coef_ref.shape[0] // LANES
        for first in range(0, blocks, CHUNK):
            count = min(CHUNK, blocks - first)
            parts = []
            for c in range(first, first + count):
                here = block[:] == jnp.asarray(c, block.dtype)
                parts.append(jnp.where(here, pattern[:], jnp.zeros_like(pattern)).astype(jnp.bfloat16))
            weights = jnp.concatenate(parts, axis=1) if count > 1 else parts[0]
            rows_at = slice(first * LANES, (first + count) * LANES)
            part = jnp.dot(weights, coef_ref[rows_at], preferred_element_type=jnp.float32)
            acc[:] = part if first == 0 else acc[:] + part

        for g in range(groups):
            sun = acc[g * rows : (g + 1) * rows]
            power = jnp.ceil(jnp.log2(jnp.maximum(jnp.max(sun, axis=0, keepdims=True), 1e-30)))
            code = jnp.round(sun * (LEVELS / jnp.exp2(power)) - 0.5 * LEVELS)
            out_ref[g, :rows] = code.astype(jnp.int32).astype(jnp.int16)
            power = jnp.broadcast_to(power, (TAIL, power.shape[1]))
            out_ref[g, rows:] = power.astype(jnp.int32).astype(jnp.int16)

    return kernel


def base_kernel(sky_ref, open_ref, closed_ref, cross_ref, closed_out):
    over = (((0,), (0,)), ((), ()))
    closed = lax.dot_general(sky_ref[:], closed_ref[:], over, preferred_element_type=jnp.float32)
    opened = lax.dot_general(sky_ref[:], open_ref[:], over, preferred_element_type=jnp.float32)
    closed_out[:] = closed
    cross_ref[:] = opened - closed


def own_sums(place_ref, sums_ref):
    sums = jnp.sum(sums_ref[:], axis=0)
    lane = lax.broadcasted_iota(jnp.int32, (1, LANES), 1)
    own = lane == place_ref[0]
    return [jnp.sum(jnp.where(own, sums[k : k + 1], 0.0), keepdims=True) for k in range(2)]


def cross_of(codes, base_ref, g):
    rows, width = base_ref.shape[0], codes.shape[2]
    scale = jnp.exp2(codes[g, rows:].astype(jnp.int32).astype(jnp.float32)[:1]) / LEVELS
    sun = (codes[g, :rows].astype(jnp.int32).astype(jnp.float32) + 0.5 * LEVELS) * scale
    return base_ref[:, g * width : (g + 1) * width] + sun


def grad_kernel(place_ref, sums_ref, codes, base_ref, closed_ref, target_ref, out_ref):
    num, den = own_sums(place_ref, sums_ref)
    share = num / den
    rows, width = base_ref.shape[0], codes.shape[2]
    total = jnp.zeros((8, width), jnp.float32)
    for g in range(codes.shape[0]):
        at = slice(g * width, (g + 1) * width)
        cross = cross_of(codes, base_ref, g)
        lit = closed_ref[:, at] + share * cross
        term = (lit - target_ref[:, at].astype(jnp.float32)) * cross
        total = total + jnp.sum(term.reshape(rows // 8, 8, width), axis=0)
    out_ref[:] = jnp.broadcast_to((2.0 * jnp.sum(total, keepdims=True))[None], out_ref.shape)


def lit_kernel(place_ref, sums_ref, codes, base_ref, closed_ref, out_ref):
    num, den = own_sums(place_ref, sums_ref)
    share = num / den
    width = codes.shape[2]
    for g in range(codes.shape[0]):
        at = slice(g * width, (g + 1) * width)
        out_ref[:, at] = (closed_ref[:, at] + share * cross_of(codes, base_ref, g)).astype(jnp.bfloat16)


def step_kernel(groups, zones, windows):
    def kernel(heard_ref, sums_ref, zone_hbm, area_hbm, openness_hbm, out_ref, zone_ref, area_ref, openness_ref, sems):
        copies = fetch([(zone_hbm, zone_ref), (area_hbm, area_ref), (openness_hbm, openness_ref)], sems)
        sums = jnp.sum(sums_ref[:], axis=0)
        ratios = []
        square = jnp.zeros((1, 1), jnp.float32)
        for z in range(zones):
            grads = jnp.sum(heard_ref[z * groups : (z + 1) * groups], axis=0)[:, 0:1]
            ratios.append(grads / sums[1:2, z : z + 1])
            square = square + ratios[z] * ratios[z] * sums[2:3, z : z + 1]
        rms = jnp.sqrt(square / windows + 1e-06)
        for c in copies:
            c.wait()
        zone = zone_ref[:]
        chosen = jnp.zeros(zone.shape, jnp.float32)
        for z in range(zones):
            chosen = jnp.where(zone == z, ratios[z], chosen)
        out_ref[:] = jnp.clip(openness_ref[:] - 0.25 * (area_ref[:] * chosen) / rms, 0.0, 1.0)

    return kernel


def local(sky, sky_open, sky_closed, sun_coef, sun_bins, sun_rad, target, zone_of, area, openness):
    zones = lax.axis_size("sens")
    groups = lax.axis_size("hour")
    own_zone = lax.axis_index("sens").astype(jnp.int32)[None]
    rows, patches = sky.shape
    kbins = sun_bins.shape[1]
    nbins, width = sun_coef.shape
    hours = rows * groups
    windows = area.shape[0]
    assert nbins % LANES == 0 or nbins % LANES >= 2 * kbins
    assert nbins <= 256 * LANES and width % LANES == 0 and windows % LANES == 0 and 3 * kbins <= HEAD
    assert zones <= LANES and rows % 16 == 0
    shape = jax.ShapeDtypeStruct
    f32, bf16 = jnp.float32, jnp.bfloat16
    dma = lambda n: pltpu.SemaphoreType.DMA((n,))

    packed = call(
        pack_kernel,
        "pack",
        shape((groups, HEAD, rows), bf16),
        in_specs=[HBM, HBM],
        scratch_shapes=[pltpu.VMEM((kbins, rows), jnp.int32), pltpu.VMEM((kbins, rows), bf16), dma(2)],
    )(sun_bins.T, sun_rad.T)
    heads = lax.all_to_all(packed, "hour", 0, 0)

    tiles = (windows // LANES, LANES)
    zone2, area2, openness2 = zone_of.reshape(tiles), area.reshape(tiles), openness.reshape(tiles)
    own_windows = [pltpu.VMEM(tiles, jnp.int32), pltpu.VMEM(tiles, f32), pltpu.VMEM(tiles, f32), dma(3)]
    zone_sums = call(
        sums_kernel(zones), "sums", shape((8, LANES), f32), in_specs=[HBM] * 3, scratch_shapes=own_windows
    )(zone2, area2, openness2)
    sums = lax.all_gather(zone_sums, "sens", axis=0)

    blocks = pl.cdiv(nbins, LANES)
    tail = jnp.pad(sun_coef[(blocks - 1) * LANES :], ((0, blocks * LANES - nbins), (0, 0)))
    coef = call(
        fetch_kernel,
        "coefficients",
        shape((blocks * LANES, width), bf16),
        moved=4 * nbins * width,
        in_specs=[HBM, HBM],
        out_specs=VMEM,
        scratch_shapes=[dma(2)],
    )(sun_coef, tail)

    codes = call(
        sun_kernel(groups, kbins),
        "sun",
        shape((groups, rows + TAIL, width), jnp.int16),
        flops=2 * hours * nbins * width,
        moved=2 * nbins * width,
        in_specs=[VMEM, VMEM],
        scratch_shapes=[
            pltpu.VMEM((hours, width), f32),
            pltpu.VMEM((hours, LANES), PATTERN),
            pltpu.VMEM((hours, LANES), PATTERN),
        ],
    )(heads, coef)
    codes = lax.all_to_all(codes, "hour", 0, 0)

    base, closed = call(
        base_kernel,
        "base",
        [shape((rows, groups * width), f32)] * 2,
        flops=4 * rows * patches * groups * width,
        moved=8 * rows * groups * width,
    )(sky.T, sky_open, sky_closed)
    message = call(
        grad_kernel,
        "grad",
        shape((zones * groups, 1, LANES), f32),
        in_specs=[SMEM] + [VMEM] * 5,
        flops=8 * hours * width,
        moved=12 * hours * width,
    )(own_zone, sums, codes, base, closed, target)
    heard = lax.all_to_all(message, ("sens", "hour"), 0, 0)
    illuminance = call(
        lit_kernel,
        "lit",
        shape((rows, groups * width), bf16),
        in_specs=[SMEM] + [VMEM] * 4,
        flops=4 * hours * width,
        moved=12 * hours * width,
    )(own_zone, sums, codes, base, closed)
    new_openness = call(
        step_kernel(groups, zones, windows * zones),
        "step",
        shape(tiles, f32),
        in_specs=[VMEM, VMEM] + [HBM] * 3,
        scratch_shapes=own_windows,
    )(heard, sums, zone2, area2, openness2)
    return (illuminance, new_openness.reshape(-1))


def solution(mesh):
    in_specs = (
        P("hour", None),
        P(None, "sens"),
        P(None, "sens"),
        P(None, ("sens", "hour")),
        P("hour", None),
        P("hour", None),
        P("hour", "sens"),
        P("sens", None),
        P("sens"),
        P("sens"),
    )
    out_specs = (P("hour", "sens"), P("sens"))
    return jax.shard_map(local, mesh=mesh, in_specs=in_specs, out_specs=out_specs, check_vma=False)
```

```python
import jax
import jax.numpy as jnp
from jax import lax
from jax.experimental import pallas as pl
from jax.experimental.pallas import tpu as pltpu
from jax.sharding import PartitionSpec as P

LANES = 128
CHUNK = 8
HEAD = 16
TAIL = 8
PATTERN = jnp.bfloat16
LEVELS = 65000.0
VMEM_BYTES = 40 * 1024 * 1024
ANY = pl.BlockSpec(memory_space=pl.ANY)
HBM = pl.BlockSpec(memory_space=pltpu.HBM)
SMEM = pl.BlockSpec(memory_space=pltpu.SMEM)
VMEM = pl.BlockSpec(memory_space=pltpu.VMEM)


def call(kernel, name, out_shape, flops=0, moved=0, **more):
    run = pl.pallas_call(
        kernel,
        out_shape=out_shape,
        name=name,
        compiler_params=pltpu.CompilerParams(vmem_limit_bytes=VMEM_BYTES),
        cost_estimate=pl.CostEstimate(flops=flops, bytes_accessed=moved, transcendentals=0),
        **more,
    )
    specs = more["in_specs"]
    return lambda *args: run(
        *[pltpu.with_memory_space_constraint(x, pltpu.HBM) if s is HBM else x for x, s in zip(args, specs)]
    )


def exchange(x, axis, mask):
    return lax.ppermute(x, axis, [(i, i ^ mask) for i in range(lax.axis_size(axis))])


def fetch(pairs, sems):
    copies = [pltpu.make_async_copy(source, place, sems.at[i]) for i, (source, place) in enumerate(pairs)]
    for c in copies:
        c.start()
    return copies


def pack_kernel(bins_hbm, rad_hbm, out_ref, bins_ref, rad_ref, sems):
    for c in fetch([(bins_hbm, bins_ref), (rad_hbm, rad_ref)], sems):
        c.wait()
    bins = bins_ref[:]
    kbins = bins.shape[0]
    fill = jnp.zeros((HEAD - 3 * kbins, bins.shape[1]), jnp.float32)
    parts = [rad_ref[:].astype(jnp.float32), (bins // LANES).astype(jnp.float32), (bins % LANES).astype(jnp.float32)]
    head = jnp.concatenate(parts + [fill], axis=0).astype(jnp.bfloat16)
    for g in range(out_ref.shape[0]):
        out_ref[g] = head


def sums_kernel(token, zone_hbm, area_hbm, openness_hbm, out_ref, zone_ref, area_ref, openness_ref, sems):
    for c in fetch([(zone_hbm, zone_ref), (area_hbm, area_ref), (openness_hbm, openness_ref)], sems):
        c.wait()
    zone, area = zone_ref[:], area_ref[:]
    lane = lax.broadcasted_iota(jnp.int32, (1, LANES), 1)
    values = [area * openness_ref[:], area, area * area]
    for z in range(out_ref.shape[0]):
        member = zone == z
        row = jnp.zeros((1, LANES), jnp.float32)
        for k, value in enumerate(values):
            row = jnp.where(lane == k, jnp.sum(jnp.where(member, value, 0.0), keepdims=True), row)
        out_ref[z] = row


def fetch_kernel(coef_hbm, out_ref, sems):
    for c in fetch([(coef_hbm, out_ref)], sems):
        c.wait()


def sun_kernel(masks, kbins):
    count = len(masks)

    def kernel(me_ref, heads, coef_ref, *refs):
        outs, (token, acc, pattern, block) = refs[:count], refs[count:]
        rows = heads.shape[2]
        nbins = coef_ref.shape[0]
        token[:] = jnp.zeros_like(token)
        lane = lax.broadcasted_iota(jnp.int32, (rows, LANES), 1)
        for g, mask in enumerate(masks):
            small = heads[me_ref[0] ^ mask].astype(jnp.float32).T
            value = jnp.zeros((rows, LANES), jnp.float32)
            where = jnp.zeros((rows, LANES), jnp.float32)
            for k in range(kbins):
                low = small[:, 2 * kbins + k : 2 * kbins + k + 1].astype(jnp.int32)
                hit = lane == low
                value = jnp.where(hit, small[:, k : k + 1], value)
                where = jnp.where(hit, small[:, kbins + k : kbins + k + 1], where)
            pattern[g * rows : (g + 1) * rows] = value.astype(pattern.dtype)
            block[g * rows : (g + 1) * rows] = where.astype(block.dtype)

        step = CHUNK * LANES
        for first in range(0, nbins, step):
            end = min(first + step, nbins)
            parts = []
            for c in range(first // LANES, pl.cdiv(end, LANES)):
                here = block[:] == jnp.asarray(c, block.dtype)
                parts.append(jnp.where(here, pattern[:], jnp.zeros_like(pattern)).astype(jnp.bfloat16))
            weights = jnp.concatenate(parts, axis=1) if len(parts) > 1 else parts[0]
            part = jnp.dot(weights[:, : end - first], coef_ref[first:end], preferred_element_type=jnp.float32)
            acc[:] = part if first == 0 else acc[:] + part

        for g in range(count):
            sun = acc[g * rows : (g + 1) * rows]
            power = jnp.ceil(jnp.log2(jnp.maximum(jnp.max(sun, axis=0, keepdims=True), 1e-30)))
            code = jnp.round(sun * (LEVELS / jnp.exp2(power)) - 0.5 * LEVELS)
            outs[g][:rows] = code.astype(jnp.int32).astype(jnp.int16)
            power = jnp.broadcast_to(power, (TAIL, power.shape[1]))
            outs[g][rows:] = power.astype(jnp.int32).astype(jnp.int16)

    return kernel


def base_kernel(
    token, sky_hbm, open_hbm, closed_hbm, target_hbm, cross_ref, closed_out, apart_ref, sky_ref, open_ref, closed_ref, target_ref, sems
):
    pairs = [(sky_hbm, sky_ref), (open_hbm, open_ref), (closed_hbm, closed_ref), (target_hbm, target_ref)]
    for c in fetch(pairs, sems):
        c.wait()
    over = (((0,), (0,)), ((), ()))
    closed = lax.dot_general(sky_ref[:], closed_ref[:], over, preferred_element_type=jnp.float32)
    opened = lax.dot_general(sky_ref[:], open_ref[:], over, preferred_element_type=jnp.float32)
    closed_out[:] = closed
    cross_ref[:] = opened - closed
    apart_ref[:] = closed - target_ref[:].astype(jnp.float32)


def own_sums(sums_ref):
    sums = jnp.sum(sums_ref[:], axis=0)
    return [sums[:, k : k + 1] for k in range(3)]


def place(me_ref, mask, width):
    return pl.ds(pl.multiple_of((me_ref[0] ^ mask) * width, LANES), width)


def cross_of(codes, base):
    rows = base.shape[0]
    scale = jnp.exp2(codes[rows:].astype(jnp.int32).astype(jnp.float32)[:1]) / LEVELS
    sun = (codes[:rows].astype(jnp.int32).astype(jnp.float32) + 0.5 * LEVELS) * scale
    return base + sun


def grad_kernel(groups):
    def kernel(me_ref, sums_ref, base_ref, apart_ref, *refs):
        codes, out_ref = refs[:groups], refs[groups]
        num, den, square = own_sums(sums_ref)
        share = num / den
        rows, width = base_ref.shape[0], codes[0].shape[1]
        total = jnp.zeros((8, width), jnp.float32)
        for mask in range(groups):
            at = place(me_ref, mask, width)
            cross = cross_of(codes[mask], base_ref[:, at])
            term = (apart_ref[:, at] + share * cross) * cross
            total = total + jnp.sum(term.reshape(rows // 8, 8, width), axis=0)
        lane = lax.broadcasted_iota(jnp.int32, (1, LANES), 1)
        ratio = 2.0 * jnp.sum(total, keepdims=True) / den
        row = jnp.where(lane == 0, ratio, jnp.where(lane == 1, square, 0.0))
        out_ref[:] = jnp.broadcast_to(row[None], out_ref.shape)

    return kernel


def lit_kernel(groups):
    def kernel(me_ref, sums_ref, base_ref, closed_ref, *refs):
        codes, out_ref = refs[:groups], refs[groups]
        num, den, _ = own_sums(sums_ref)
        share = num / den
        width = codes[0].shape[1]
        for mask in range(groups):
            at = place(me_ref, mask, width)
            lit = closed_ref[:, at] + share * cross_of(codes[mask], base_ref[:, at])
            out_ref[:, at] = lit.astype(jnp.bfloat16)

    return kernel


def step_kernel(groups, windows):
    def kernel(heard_ref, zone_hbm, area_hbm, openness_hbm, out_ref, zone_ref, area_ref, openness_ref, sems):
        copies = fetch([(zone_hbm, zone_ref), (area_hbm, area_ref), (openness_hbm, openness_ref)], sems)
        ratios = []
        square = jnp.zeros((1, 1), jnp.float32)
        for z in range(heard_ref.shape[0] // groups):
            heard = heard_ref[z * groups : (z + 1) * groups]
            ratios.append(jnp.sum(heard, axis=0)[:, 0:1])
            square = square + ratios[z] * ratios[z] * heard[0, :, 1:2]
        rms = jnp.sqrt(square / windows + 1e-06)
        for c in copies:
            c.wait()
        zone = zone_ref[:]
        chosen = jnp.zeros(zone.shape, jnp.float32)
        for z, ratio in enumerate(ratios):
            chosen = jnp.where(zone == z, ratio, chosen)
        out_ref[:] = jnp.clip(openness_ref[:] - 0.25 * (area_ref[:] * chosen) / rms, 0.0, 1.0)

    return kernel


def local(sky, sky_open, sky_closed, sun_coef, sun_bins, sun_rad, target, zone_of, area, openness):
    zones = lax.axis_size("sens")
    groups = lax.axis_size("hour")
    me = lax.axis_index("hour").astype(jnp.int32)[None]
    rows, patches = sky.shape
    kbins = sun_bins.shape[1]
    nbins, width = sun_coef.shape
    hours = rows * groups
    sensors = groups * width
    windows = area.shape[0]
    assert nbins % LANES == 0 or nbins % LANES >= 2 * kbins
    assert nbins <= 256 * LANES and width % LANES == 0 and windows % LANES == 0 and 3 * kbins <= HEAD
    assert groups & (groups - 1) == 0 and groups > 1 and rows % 16 == 0
    shape = jax.ShapeDtypeStruct
    f32, bf16 = jnp.float32, jnp.bfloat16
    dma = lambda n: pltpu.SemaphoreType.DMA((n,))

    packed = call(
        pack_kernel,
        "pack",
        shape((groups, HEAD, rows), bf16),
        in_specs=[HBM, HBM],
        scratch_shapes=[pltpu.VMEM((kbins, rows), jnp.int32), pltpu.VMEM((kbins, rows), bf16), dma(2)],
    )(sun_bins.T, sun_rad.T)
    heads = lax.all_to_all(packed, "hour", 0, 0)
    coef = call(
        fetch_kernel,
        "coefficients",
        shape((nbins, width), bf16),
        moved=4 * nbins * width,
        in_specs=[HBM],
        out_specs=VMEM,
        scratch_shapes=[dma(1)],
    )(sun_coef)

    def sun(masks):
        count = len(masks)
        found = call(
            sun_kernel(masks, kbins),
            "sun",
            [shape((rows + TAIL, width), jnp.int16)] * count + [shape((8, LANES), f32)],
            flops=2 * count * rows * nbins * width,
            moved=2 * nbins * width,
            in_specs=[SMEM, VMEM, VMEM],
            scratch_shapes=[
                pltpu.VMEM((count * rows, width), f32),
                pltpu.VMEM((count * rows, LANES), PATTERN),
                pltpu.VMEM((count * rows, LANES), PATTERN),
            ],
        )(me, heads, coef)
        return dict(zip(masks, found)), found[count]

    order = list(range(groups))[::-1]
    far, token = sun(order[: groups // 2])
    codes = {mask: exchange(x, "hour", mask) for mask, x in far.items()}
    near, _ = sun(order[groups // 2 :])
    codes |= {mask: exchange(x, "hour", mask) if mask else x for mask, x in near.items()}
    codes = [codes[mask] for mask in range(groups)]

    tiles = (windows // LANES, LANES)
    zone2, area2, openness2 = zone_of.reshape(tiles), area.reshape(tiles), openness.reshape(tiles)
    own_windows = [pltpu.VMEM(tiles, jnp.int32), pltpu.VMEM(tiles, f32), pltpu.VMEM(tiles, f32), dma(3)]
    zone_sums = call(
        sums_kernel, "sums", shape((zones, 1, LANES), f32), in_specs=[ANY] + [HBM] * 3, scratch_shapes=own_windows
    )(token, zone2, area2, openness2)
    sums = lax.all_to_all(zone_sums, "sens", 0, 0)

    base, closed, apart = call(
        base_kernel,
        "base",
        [shape((rows, sensors), f32)] * 3,
        flops=4 * rows * patches * sensors,
        moved=8 * rows * sensors,
        in_specs=[ANY] + [HBM] * 4,
        scratch_shapes=[
            pltpu.VMEM((patches, rows), bf16),
            pltpu.VMEM((patches, sensors), bf16),
            pltpu.VMEM((patches, sensors), bf16),
            pltpu.VMEM((rows, sensors), bf16),
            dma(4),
        ],
    )(token, sky.T, sky_open, sky_closed, target)
    message = call(
        grad_kernel(groups),
        "grad",
        shape((zones * groups, 1, LANES), f32),
        in_specs=[SMEM] + [VMEM] * (3 + groups),
        flops=8 * hours * width,
        moved=12 * hours * width,
    )(me, sums, base, apart, *codes)
    heard = lax.all_to_all(message, ("sens", "hour"), 0, 0)
    illuminance = call(
        lit_kernel(groups),
        "lit",
        shape((rows, sensors), bf16),
        in_specs=[SMEM] + [VMEM] * (3 + groups),
        flops=4 * hours * width,
        moved=12 * hours * width,
    )(me, sums, base, closed, *codes)
    new_openness = call(
        step_kernel(groups, windows * zones),
        "step",
        shape(tiles, f32),
        in_specs=[VMEM] + [HBM] * 3,
        scratch_shapes=own_windows,
    )(heard, zone2, area2, openness2)
    return (illuminance, new_openness.reshape(-1))


def solution(mesh):
    in_specs = (
        P("hour", None),
        P(None, "sens"),
        P(None, "sens"),
        P(None, ("sens", "hour")),
        P("hour", None),
        P("hour", None),
        P("hour", "sens"),
        P("sens", None),
        P("sens"),
        P("sens"),
    )
    out_specs = (P("hour", "sens"), P("sens"))
    return jax.shard_map(local, mesh=mesh, in_specs=in_specs, out_specs=out_specs, check_vma=False)
```

```python
import jax
import jax.numpy as jnp
from jax import lax
from jax.experimental import pallas as pl
from jax.experimental.pallas import tpu as pltpu
from jax.sharding import PartitionSpec as P

LANES = 128
CHUNK = 8
HEAD = 16
TAIL = 8
PATTERN = jnp.bfloat16
LEVELS = 65000.0
VMEM_BYTES = 40 * 1024 * 1024
ANY = pl.BlockSpec(memory_space=pl.ANY)
HBM = pl.BlockSpec(memory_space=pltpu.HBM)
SMEM = pl.BlockSpec(memory_space=pltpu.SMEM)
VMEM = pl.BlockSpec(memory_space=pltpu.VMEM)


def call(kernel, name, out_shape, flops=0, moved=0, **more):
    run = pl.pallas_call(
        kernel,
        out_shape=out_shape,
        name=name,
        compiler_params=pltpu.CompilerParams(vmem_limit_bytes=VMEM_BYTES),
        cost_estimate=pl.CostEstimate(flops=flops, bytes_accessed=moved, transcendentals=0),
        **more,
    )
    specs = more["in_specs"]
    return lambda *args: run(
        *[pltpu.with_memory_space_constraint(x, pltpu.HBM) if s is HBM else x for x, s in zip(args, specs)]
    )


def exchange(x, axis, mask):
    return lax.ppermute(x, axis, [(i, i ^ mask) for i in range(lax.axis_size(axis))])


def fetch(pairs, sems):
    copies = [pltpu.make_async_copy(source, place, sems.at[i]) for i, (source, place) in enumerate(pairs)]
    for c in copies:
        c.start()
    return copies


def pack_kernel(bins_hbm, rad_hbm, out_ref, bins_ref, rad_ref, sems):
    for c in fetch([(bins_hbm, bins_ref), (rad_hbm, rad_ref)], sems):
        c.wait()
    bins = bins_ref[:]
    kbins = bins.shape[0]
    fill = jnp.zeros((HEAD - 3 * kbins, bins.shape[1]), jnp.float32)
    parts = [rad_ref[:].astype(jnp.float32), (bins // LANES).astype(jnp.float32), (bins % LANES).astype(jnp.float32)]
    out_ref[:] = jnp.concatenate(parts + [fill], axis=0).astype(jnp.bfloat16)


def fetch_kernel(coef_hbm, zone_hbm, area_hbm, openness_hbm, coef_ref, sums_ref, zone_ref, area_ref, openness_ref, sems):
    pairs = [(zone_hbm, zone_ref), (area_hbm, area_ref), (openness_hbm, openness_ref), (coef_hbm, coef_ref)]
    copies = fetch(pairs, sems)
    for c in copies[:3]:
        c.wait()
    zone, area = zone_ref[:], area_ref[:]
    lane = lax.broadcasted_iota(jnp.int32, (1, LANES), 1)
    values = [area * openness_ref[:], area, area * area]
    for z in range(sums_ref.shape[0]):
        member = zone == z
        row = jnp.zeros((1, LANES), jnp.float32)
        for k, value in enumerate(values):
            row = jnp.where(lane == k, jnp.sum(jnp.where(member, value, 0.0), keepdims=True), row)
        sums_ref[z] = row
    copies[3].wait()


def sun_kernel(count, kbins):
    def kernel(sums_ref, coef_ref, *refs):
        heads, outs, (sums_out, acc, pattern, block) = refs[:count], refs[count : 2 * count], refs[2 * count :]
        rows = heads[0].shape[1]
        nbins = coef_ref.shape[0]
        sums_out[:] = sums_ref[:]
        lane = lax.broadcasted_iota(jnp.int32, (rows, LANES), 1)
        for g in range(count):
            small = heads[g][:].astype(jnp.float32).T
            value = jnp.zeros((rows, LANES), jnp.float32)
            where = jnp.zeros((rows, LANES), jnp.float32)
            for k in range(kbins):
                low = small[:, 2 * kbins + k : 2 * kbins + k + 1].astype(jnp.int32)
                hit = lane == low
                value = jnp.where(hit, small[:, k : k + 1], value)
                where = jnp.where(hit, small[:, kbins + k : kbins + k + 1], where)
            pattern[g * rows : (g + 1) * rows] = value.astype(pattern.dtype)
            block[g * rows : (g + 1) * rows] = where.astype(block.dtype)

        step = CHUNK * LANES
        for first in range(0, nbins, step):
            end = min(first + step, nbins)
            parts = []
            for c in range(first // LANES, pl.cdiv(end, LANES)):
                here = block[:] == jnp.asarray(c, block.dtype)
                parts.append(jnp.where(here, pattern[:], jnp.zeros_like(pattern)).astype(jnp.bfloat16))
            weights = jnp.concatenate(parts, axis=1) if len(parts) > 1 else parts[0]
            part = jnp.dot(weights[:, : end - first], coef_ref[first:end], preferred_element_type=jnp.float32)
            acc[:] = part if first == 0 else acc[:] + part

        for g in range(count):
            sun = acc[g * rows : (g + 1) * rows]
            power = jnp.ceil(jnp.log2(jnp.maximum(jnp.max(sun, axis=0, keepdims=True), 1e-30)))
            code = jnp.round(sun * (LEVELS / jnp.exp2(power)) - 0.5 * LEVELS)
            outs[g][:rows] = code.astype(jnp.int32).astype(jnp.int16)
            power = jnp.broadcast_to(power, (TAIL, power.shape[1]))
            outs[g][rows:] = power.astype(jnp.int32).astype(jnp.int16)

    return kernel


def base_kernel(
    token, sky_hbm, open_hbm, closed_hbm, target_hbm, cross_ref, closed_out, target_out, sky_ref, open_ref, closed_ref, sems
):
    pairs = [(sky_hbm, sky_ref), (open_hbm, open_ref), (closed_hbm, closed_ref), (target_hbm, target_out)]
    copies = fetch(pairs, sems)
    for c in copies[:3]:
        c.wait()
    over = (((0,), (0,)), ((), ()))
    closed = lax.dot_general(sky_ref[:], closed_ref[:], over, preferred_element_type=jnp.float32)
    opened = lax.dot_general(sky_ref[:], open_ref[:], over, preferred_element_type=jnp.float32)
    closed_out[:] = closed
    cross_ref[:] = opened - closed
    copies[3].wait()


def own_sums(sums_ref):
    sums = jnp.sum(sums_ref[:], axis=0)
    return [sums[:, k : k + 1] for k in range(3)]


def place(me_ref, mask, width):
    return pl.ds(pl.multiple_of((me_ref[0] ^ mask) * width, LANES), width)


def cross_of(codes, base):
    rows = base.shape[0]
    scale = jnp.exp2(codes[rows:].astype(jnp.int32).astype(jnp.float32)[:1]) / LEVELS
    sun = (codes[:rows].astype(jnp.int32).astype(jnp.float32) + 0.5 * LEVELS) * scale
    return base + sun


def grad_kernel(groups):
    def kernel(me_ref, sums_ref, base_ref, closed_ref, target_ref, *refs):
        codes, out_ref = refs[:groups], refs[groups]
        num, den, square = own_sums(sums_ref)
        share = num / den
        rows, width = base_ref.shape[0], codes[0].shape[1]
        total = jnp.zeros((8, width), jnp.float32)
        for mask in range(groups):
            at = place(me_ref, mask, width)
            cross = cross_of(codes[mask], base_ref[:, at])
            lit = closed_ref[:, at] + share * cross
            term = (lit - target_ref[:, at].astype(jnp.float32)) * cross
            total = total + jnp.sum(term.reshape(rows // 8, 8, width), axis=0)
        lane = lax.broadcasted_iota(jnp.int32, (1, LANES), 1)
        ratio = 2.0 * jnp.sum(total, keepdims=True) / den
        row = jnp.where(lane == 0, ratio, jnp.where(lane == 1, square, 0.0))
        out_ref[:] = jnp.broadcast_to(row[None], out_ref.shape)

    return kernel


def lit_kernel(groups):
    def kernel(me_ref, sums_ref, base_ref, closed_ref, *refs):
        codes, out_ref = refs[:groups], refs[groups]
        num, den, _ = own_sums(sums_ref)
        share = num / den
        width = codes[0].shape[1]
        for mask in range(groups):
            at = place(me_ref, mask, width)
            lit = closed_ref[:, at] + share * cross_of(codes[mask], base_ref[:, at])
            out_ref[:, at] = lit.astype(jnp.bfloat16)

    return kernel


def step_kernel(groups, windows):
    def kernel(heard_ref, zone_ref, area_ref, openness_ref, out_ref):
        ratios = []
        square = jnp.zeros((1, 1), jnp.float32)
        for z in range(heard_ref.shape[0] // groups):
            heard = heard_ref[z * groups : (z + 1) * groups]
            ratios.append(jnp.sum(heard, axis=0)[:, 0:1])
            square = square + ratios[z] * ratios[z] * heard[0, :, 1:2]
        rms = jnp.sqrt(square / windows + 1e-06)
        zone = zone_ref[:]
        chosen = jnp.zeros(zone.shape, jnp.float32)
        for z, ratio in enumerate(ratios):
            chosen = jnp.where(zone == z, ratio, chosen)
        out_ref[:] = jnp.clip(openness_ref[:] - 0.25 * (area_ref[:] * chosen) / rms, 0.0, 1.0)

    return kernel


def local(sky, sky_open, sky_closed, sun_coef, sun_bins, sun_rad, target, zone_of, area, openness):
    zones = lax.axis_size("sens")
    groups = lax.axis_size("hour")
    me = lax.axis_index("hour").astype(jnp.int32)[None]
    rows, patches = sky.shape
    kbins = sun_bins.shape[1]
    nbins, width = sun_coef.shape
    hours = rows * groups
    sensors = groups * width
    windows = area.shape[0]
    assert nbins % LANES == 0 or nbins % LANES >= 2 * kbins
    assert nbins <= 256 * LANES and width % LANES == 0 and windows % LANES == 0 and 3 * kbins <= HEAD
    assert groups & (groups - 1) == 0 and groups > 1 and rows % 16 == 0
    shape = jax.ShapeDtypeStruct
    f32, bf16 = jnp.float32, jnp.bfloat16
    dma = lambda n: pltpu.SemaphoreType.DMA((n,))

    packed = call(
        pack_kernel,
        "pack",
        shape((HEAD, rows), bf16),
        in_specs=[HBM, HBM],
        scratch_shapes=[pltpu.VMEM((kbins, rows), jnp.int32), pltpu.VMEM((kbins, rows), bf16), dma(2)],
    )(sun_bins.T, sun_rad.T)
    order = list(range(groups))[::-1]
    heads = {mask: exchange(packed, "hour", mask) if mask else packed for mask in order}

    tiles = (windows // LANES, LANES)
    coef, zone_sums, zone2, area2, openness2 = call(
        fetch_kernel,
        "coefficients",
        [shape((nbins, width), bf16), shape((zones, 1, LANES), f32)]
        + [shape(tiles, jnp.int32), shape(tiles, f32), shape(tiles, f32)],
        moved=4 * nbins * width,
        in_specs=[HBM] * 4,
        out_specs=[VMEM] * 5,
        scratch_shapes=[dma(4)],
    )(sun_coef, zone_of.reshape(tiles), area.reshape(tiles), openness.reshape(tiles))

    def sun(masks, zone_sums):
        count = len(masks)
        found = call(
            sun_kernel(count, kbins),
            "sun",
            [shape((rows + TAIL, width), jnp.int16)] * count + [shape(zone_sums.shape, f32)],
            flops=2 * count * rows * nbins * width,
            moved=2 * nbins * width,
            in_specs=[VMEM] * (2 + count),
            scratch_shapes=[
                pltpu.VMEM((count * rows, width), f32),
                pltpu.VMEM((count * rows, LANES), PATTERN),
                pltpu.VMEM((count * rows, LANES), PATTERN),
            ],
        )(zone_sums, coef, *[heads[mask] for mask in masks])
        return dict(zip(masks, found)), found[count]

    far, zone_sums = sun(order[: groups // 2], zone_sums)
    codes = {mask: exchange(x, "hour", mask) for mask, x in far.items()}
    near, _ = sun(order[groups // 2 :], zone_sums)
    codes |= {mask: exchange(x, "hour", mask) if mask else x for mask, x in near.items()}
    codes = [codes[mask] for mask in range(groups)]

    sums = lax.all_to_all(zone_sums, "sens", 0, 0)

    base, closed, wanted = call(
        base_kernel,
        "base",
        [shape((rows, sensors), f32)] * 2 + [shape((rows, sensors), bf16)],
        flops=4 * rows * patches * sensors,
        moved=8 * rows * sensors,
        in_specs=[ANY] + [HBM] * 4,
        out_specs=[VMEM] * 3,
        scratch_shapes=[
            pltpu.VMEM((patches, rows), bf16),
            pltpu.VMEM((patches, sensors), bf16),
            pltpu.VMEM((patches, sensors), bf16),
            dma(4),
        ],
    )(zone_sums, sky.T, sky_open, sky_closed, target)
    message = call(
        grad_kernel(groups),
        "grad",
        shape((zones * groups, 1, LANES), f32),
        in_specs=[SMEM] + [VMEM] * (4 + groups),
        flops=8 * hours * width,
        moved=12 * hours * width,
    )(me, sums, base, closed, wanted, *codes)
    heard = lax.all_to_all(message, ("sens", "hour"), 0, 0)
    illuminance = call(
        lit_kernel(groups),
        "lit",
        shape((rows, sensors), bf16),
        in_specs=[SMEM] + [VMEM] * (3 + groups),
        flops=4 * hours * width,
        moved=12 * hours * width,
    )(me, sums, base, closed, *codes)
    new_openness = call(
        step_kernel(groups, windows * zones),
        "step",
        shape(tiles, f32),
        in_specs=[VMEM] * 4,
    )(heard, zone2, area2, openness2)
    return (illuminance, new_openness.reshape(-1))


def solution(mesh):
    in_specs = (
        P("hour", None),
        P(None, "sens"),
        P(None, "sens"),
        P(None, ("sens", "hour")),
        P("hour", None),
        P("hour", None),
        P("hour", "sens"),
        P("sens", None),
        P("sens"),
        P("sens"),
    )
    out_specs = (P("hour", "sens"), P("sens"))
    return jax.shard_map(local, mesh=mesh, in_specs=in_specs, out_specs=out_specs, check_vma=False)
```

```python
import jax
import jax.numpy as jnp
from jax import lax
from jax.experimental import pallas as pl
from jax.experimental.pallas import tpu as pltpu
from jax.sharding import PartitionSpec as P

LANES = 128
CHUNK = 8
HEAD = 16
TAIL = 8
FRONT = 2
PATTERN = jnp.bfloat16
LEVELS = 65000.0
VMEM_BYTES = 40 * 1024 * 1024
ANY = pl.BlockSpec(memory_space=pl.ANY)
HBM = pl.BlockSpec(memory_space=pltpu.HBM)
SMEM = pl.BlockSpec(memory_space=pltpu.SMEM)
VMEM = pl.BlockSpec(memory_space=pltpu.VMEM)


def call(kernel, name, out_shape, flops=0, moved=0, **more):
    run = pl.pallas_call(
        kernel,
        out_shape=out_shape,
        name=name,
        compiler_params=pltpu.CompilerParams(vmem_limit_bytes=VMEM_BYTES),
        cost_estimate=pl.CostEstimate(flops=flops, bytes_accessed=moved, transcendentals=0),
        **more,
    )
    specs = more["in_specs"]
    return lambda *args: run(
        *[pltpu.with_memory_space_constraint(x, pltpu.HBM) if s is HBM else x for x, s in zip(args, specs)]
    )


def exchange(x, axis, mask):
    return lax.ppermute(x, axis, [(i, i ^ mask) for i in range(lax.axis_size(axis))])


def fetch(pairs, sems):
    copies = [pltpu.make_async_copy(source, place, sems.at[i]) for i, (source, place) in enumerate(pairs)]
    for c in copies:
        c.start()
    return copies


def pack_kernel(bins_hbm, rad_hbm, out_ref, bins_ref, rad_ref, sems):
    for c in fetch([(bins_hbm, bins_ref), (rad_hbm, rad_ref)], sems):
        c.wait()
    bins = bins_ref[:]
    kbins = bins.shape[0]
    fill = jnp.zeros((HEAD - 3 * kbins, bins.shape[1]), jnp.float32)
    parts = [rad_ref[:].astype(jnp.float32), (bins // LANES).astype(jnp.float32), (bins % LANES).astype(jnp.float32)]
    out_ref[:] = jnp.concatenate(parts + [fill], axis=0).astype(jnp.bfloat16)


def sums_kernel(zones):
    def kernel(zone_hbm, area_hbm, openness_hbm, sums_ref, zone_ref, area_ref, openness_ref, sems):
        for c in fetch([(zone_hbm, zone_ref), (area_hbm, area_ref), (openness_hbm, openness_ref)], sems):
            c.wait()
        zone, area = zone_ref[:], area_ref[:]
        lane = lax.broadcasted_iota(jnp.int32, sums_ref.shape, 1)
        values = [area * openness_ref[:], area, area * area]
        row = jnp.zeros(sums_ref.shape, jnp.float32)
        for z in range(zones):
            member = zone == z
            for k, value in enumerate(values):
                total = jnp.sum(jnp.where(member, value, 0.0), keepdims=True)
                row = jnp.where(lane == FRONT + 3 * z + k, total, row)
        sums_ref[:] = row

    return kernel


def sun_kernel(count, kbins, stream):
    def kernel(coef_in, *refs):
        heads, outs, rest = refs[:count], refs[count : 2 * count], refs[2 * count :]
        rows = heads[0].shape[1]
        nbins = coef_in.shape[0]
        step = CHUNK * LANES
        spans = [(first, min(first + step, nbins)) for first in range(0, nbins, step)]
        if stream:
            coef_ref, acc, pattern, block, sems = rest
            cuts = spans[:-2] + [(spans[-2][0], nbins)]
            at = [pl.ds(first, end - first) for first, end in cuts]
            copies = fetch([(coef_in.at[a], coef_ref.at[a]) for a in at], sems)
        else:
            coef_ref, (acc, pattern, block) = coef_in, rest
        lane = lax.broadcasted_iota(jnp.int32, (rows, LANES), 1)
        for g in range(count):
            small = heads[g][:].astype(jnp.float32).T
            value = jnp.zeros((rows, LANES), jnp.float32)
            where = jnp.zeros((rows, LANES), jnp.float32)
            for k in range(kbins):
                low = small[:, 2 * kbins + k : 2 * kbins + k + 1].astype(jnp.int32)
                hit = lane == low
                value = jnp.where(hit, small[:, k : k + 1], value)
                where = jnp.where(hit, small[:, kbins + k : kbins + k + 1], where)
            pattern[g * rows : (g + 1) * rows] = value.astype(pattern.dtype)
            block[g * rows : (g + 1) * rows] = where.astype(block.dtype)

        for i, (first, end) in enumerate(spans):
            parts = []
            for c in range(first // LANES, pl.cdiv(end, LANES)):
                here = block[:] == jnp.asarray(c, block.dtype)
                parts.append(jnp.where(here, pattern[:], jnp.zeros_like(pattern)).astype(jnp.bfloat16))
            weights = jnp.concatenate(parts, axis=1) if len(parts) > 1 else parts[0]
            if stream and i < len(copies):
                copies[i].wait()
            part = jnp.dot(weights[:, : end - first], coef_ref[first:end], preferred_element_type=jnp.float32)
            acc[:] = part if first == 0 else acc[:] + part

        for g in range(count):
            sun = acc[g * rows : (g + 1) * rows]
            power = jnp.ceil(jnp.log2(jnp.maximum(jnp.max(sun, axis=0, keepdims=True), 1e-30)))
            code = jnp.round(sun * (LEVELS / jnp.exp2(power)) - 0.5 * LEVELS)
            outs[g][:rows] = code.astype(jnp.int32).astype(jnp.int16)
            power = jnp.broadcast_to(power, (TAIL, power.shape[1]))
            outs[g][rows:] = power.astype(jnp.int32).astype(jnp.int16)

    return kernel


def base_kernel(
    token, sky_hbm, open_hbm, closed_hbm, target_hbm, cross_ref, closed_out, target_out, sky_ref, open_ref, closed_ref, sems
):
    pairs = [(sky_hbm, sky_ref), (open_hbm, open_ref), (closed_hbm, closed_ref), (target_hbm, target_out)]
    copies = fetch(pairs, sems)
    for c in copies[:3]:
        c.wait()
    over = (((0,), (0,)), ((), ()))
    closed = lax.dot_general(sky_ref[:], closed_ref[:], over, preferred_element_type=jnp.float32)
    opened = lax.dot_general(sky_ref[:], open_ref[:], over, preferred_element_type=jnp.float32)
    closed_out[:] = closed
    cross_ref[:] = opened - closed
    copies[3].wait()


def place(me_ref, mask, width):
    return pl.ds(pl.multiple_of((me_ref[0] ^ mask) * width, LANES), width)


def cross_of(codes, base):
    rows = base.shape[0]
    scale = jnp.exp2(codes[rows:].astype(jnp.int32).astype(jnp.float32)[:1]) / LEVELS
    sun = (codes[:rows].astype(jnp.int32).astype(jnp.float32) + 0.5 * LEVELS) * scale
    return base + sun


def grad_terms(me_ref, base_ref, closed_ref, target_ref, codes, masks, linear, square):
    rows, width = base_ref.shape[0], codes[0].shape[1]
    for mask, code in zip(masks, codes):
        at = place(me_ref, mask, width)
        cross = cross_of(code, base_ref[:, at])
        apart = closed_ref[:, at] - target_ref[:, at].astype(jnp.float32)
        linear = linear + jnp.sum((apart * cross).reshape(rows // 8, 8, width), axis=0)
        square = square + jnp.sum((cross * cross).reshape(rows // 8, 8, width), axis=0)
    return linear, square


def near_kernel(masks):
    def kernel(me_ref, base_ref, closed_ref, target_ref, *refs):
        codes, out_ref = refs[:-1], refs[-1]
        zero = jnp.zeros(out_ref.shape[1:], jnp.float32)
        out_ref[0], out_ref[1] = grad_terms(me_ref, base_ref, closed_ref, target_ref, codes, masks, zero, zero)

    return kernel


def far_kernel(masks):
    def kernel(me_ref, base_ref, closed_ref, target_ref, near_ref, sums_ref, *refs):
        codes, out_ref = refs[:-1], refs[-1]
        linear, square = grad_terms(
            me_ref, base_ref, closed_ref, target_ref, codes, masks, near_ref[0], near_ref[1]
        )
        lane = lax.broadcasted_iota(jnp.int32, sums_ref.shape, 1)
        row = jnp.where(lane == 0, 2.0 * jnp.sum(linear, keepdims=True), sums_ref[:])
        row = jnp.where(lane == 1, 2.0 * jnp.sum(square, keepdims=True), row)
        out_ref[:] = jnp.broadcast_to(row[None], out_ref.shape)

    return kernel


def last_kernel(groups, zones, windows):
    def kernel(place_ref, own_ref, heard_ref, zone_ref, area_ref, openness_ref, base_ref, closed_ref, *refs):
        codes, (lit_ref, step_ref) = refs[:groups], refs[groups:]
        sums = heard_ref[0]
        for z in range(1, zones):
            sums = sums + heard_ref[z * groups]
        zone = zone_ref[:]
        chosen = jnp.zeros(zone.shape, jnp.float32)
        square = jnp.zeros((1, 1), jnp.float32)
        own_share = jnp.zeros((1, 1), jnp.float32)
        for z in range(zones):
            at = FRONT + 3 * z
            num, den, squares = sums[:, at : at + 1], sums[:, at + 1 : at + 2], sums[:, at + 2 : at + 3]
            share = num / den
            both = jnp.sum(heard_ref[z * groups : (z + 1) * groups], axis=0)
            ratio = (both[:, 0:1] + share * both[:, 1:2]) / den
            square = square + ratio * ratio * squares
            chosen = jnp.where(zone == z, ratio, chosen)
            own_share = jnp.where(own_ref[0] == z, share, own_share)
        rms = jnp.sqrt(square / windows + 1e-06)
        step_ref[:] = jnp.clip(openness_ref[:] - 0.25 * (area_ref[:] * chosen) / rms, 0.0, 1.0)
        width = codes[0].shape[1]
        for mask in range(groups):
            at = place(place_ref, mask, width)
            lit = closed_ref[:, at] + own_share * cross_of(codes[mask], base_ref[:, at])
            lit_ref[:, at] = lit.astype(jnp.bfloat16)

    return kernel


def local(sky, sky_open, sky_closed, sun_coef, sun_bins, sun_rad, target, zone_of, area, openness):
    zones = lax.axis_size("sens")
    groups = lax.axis_size("hour")
    me = lax.axis_index("hour").astype(jnp.int32)[None]
    own_zone = lax.axis_index("sens").astype(jnp.int32)[None]
    rows, patches = sky.shape
    kbins = sun_bins.shape[1]
    nbins, width = sun_coef.shape
    hours = rows * groups
    sensors = groups * width
    windows = area.shape[0]
    assert nbins % LANES == 0 or nbins % LANES >= 2 * kbins
    assert nbins <= 256 * LANES and width % LANES == 0 and windows % LANES == 0 and 3 * kbins <= HEAD
    assert groups & (groups - 1) == 0 and groups > 1 and rows % 16 == 0
    shape = jax.ShapeDtypeStruct
    f32, bf16 = jnp.float32, jnp.bfloat16
    dma = lambda n: pltpu.SemaphoreType.DMA((n,))

    packed = call(
        pack_kernel,
        "pack",
        shape((HEAD, rows), bf16),
        in_specs=[HBM, HBM],
        scratch_shapes=[pltpu.VMEM((kbins, rows), jnp.int32), pltpu.VMEM((kbins, rows), bf16), dma(2)],
    )(sun_bins.T, sun_rad.T)
    order = list(range(groups))[::-1]
    heads = {mask: exchange(packed, "hour", mask) if mask else packed for mask in order}

    tiles = (windows // LANES, LANES)
    message = pl.cdiv(FRONT + 3 * zones, LANES) * LANES
    zone_sums, zone2, area2, openness2 = call(
        sums_kernel(zones),
        "sums",
        [shape((1, message), f32), shape(tiles, jnp.int32), shape(tiles, f32), shape(tiles, f32)],
        in_specs=[HBM] * 3,
        out_specs=[VMEM] * 4,
        scratch_shapes=[dma(3)],
    )(zone_of.reshape(tiles), area.reshape(tiles), openness.reshape(tiles))

    def sun(masks, coef, stream):
        count = len(masks)
        outs = [shape((rows + TAIL, width), jnp.int16)] * count
        scratch = [pltpu.VMEM((count * rows, width), f32)] + [pltpu.VMEM((count * rows, LANES), PATTERN)] * 2
        found = call(
            sun_kernel(count, kbins, stream),
            "sun",
            outs + [shape((nbins, width), bf16)] * stream,
            flops=2 * count * rows * nbins * width * stream,
            moved=2 * nbins * width * stream,
            in_specs=[HBM if stream else VMEM] + [VMEM] * count,
            out_specs=[VMEM] * (count + stream),
            scratch_shapes=scratch + [dma(pl.cdiv(nbins, CHUNK * LANES))] * stream,
        )(coef, *[heads[mask] for mask in masks])
        return dict(zip(masks, found)), found[-1]

    assert nbins > CHUNK * LANES
    far, near = order[: groups // 2], order[groups // 2 :]
    suns, coef = sun(far, sun_coef, 1)
    codes = {mask: exchange(x, "hour", mask) for mask, x in suns.items()}
    suns, _ = sun(near, coef, 0)
    codes |= {mask: exchange(x, "hour", mask) if mask else x for mask, x in suns.items()}

    base, closed, wanted = call(
        base_kernel,
        "base",
        [shape((rows, sensors), f32)] * 2 + [shape((rows, sensors), bf16)],
        in_specs=[ANY] + [HBM] * 4,
        out_specs=[VMEM] * 3,
        scratch_shapes=[
            pltpu.VMEM((patches, rows), bf16),
            pltpu.VMEM((patches, sensors), bf16),
            pltpu.VMEM((patches, sensors), bf16),
            dma(4),
        ],
    )(codes[0], sky.T, sky_open, sky_closed, target)
    near_sums = call(
        near_kernel(near),
        "near",
        shape((2, 8, width), f32),
        in_specs=[SMEM] + [VMEM] * (3 + len(near)),
    )(me, base, closed, wanted, *[codes[mask] for mask in near])
    sent = call(
        far_kernel(far),
        "far",
        shape((zones * groups, 1, message), f32),
        in_specs=[SMEM] + [VMEM] * (5 + len(far)),
    )(me, base, closed, wanted, near_sums, zone_sums, *[codes[mask] for mask in far])
    heard = lax.all_to_all(sent, ("sens", "hour"), 0, 0)
    illuminance, new_openness = call(
        last_kernel(groups, zones, windows * zones),
        "last",
        [shape((rows, sensors), bf16), shape(tiles, f32)],
        in_specs=[SMEM] * 2 + [VMEM] * (6 + groups),
    )(me, own_zone, heard, zone2, area2, openness2, base, closed, *[codes[mask] for mask in range(groups)])
    return (illuminance, new_openness.reshape(-1))


def solution(mesh):
    in_specs = (
        P("hour", None),
        P(None, "sens"),
        P(None, "sens"),
        P(None, ("sens", "hour")),
        P("hour", None),
        P("hour", None),
        P("hour", "sens"),
        P("sens", None),
        P("sens"),
        P("sens"),
    )
    out_specs = (P("hour", "sens"), P("sens"))
    return jax.shard_map(local, mesh=mesh, in_specs=in_specs, out_specs=out_specs, check_vma=False)
```

```python
import jax
import jax.numpy as jnp
from jax import lax
from jax.experimental import pallas as pl
from jax.experimental.pallas import tpu as pltpu
from jax.sharding import PartitionSpec as P

LANES = 128
CHUNK = 8
HEAD = 16
TAIL = 8
FRONT = 2
PATTERN = jnp.bfloat16
LEVELS = 65000.0
VMEM_BYTES = 40 * 1024 * 1024
ANY = pl.BlockSpec(memory_space=pl.ANY)
HBM = pl.BlockSpec(memory_space=pltpu.HBM)
SMEM = pl.BlockSpec(memory_space=pltpu.SMEM)
VMEM = pl.BlockSpec(memory_space=pltpu.VMEM)


def call(kernel, name, out_shape, flops=0, moved=0, **more):
    run = pl.pallas_call(
        kernel,
        out_shape=out_shape,
        name=name,
        compiler_params=pltpu.CompilerParams(vmem_limit_bytes=VMEM_BYTES),
        cost_estimate=pl.CostEstimate(flops=flops, bytes_accessed=moved, transcendentals=0),
        **more,
    )
    specs = more["in_specs"]
    return lambda *args: run(
        *[pltpu.with_memory_space_constraint(x, pltpu.HBM) if s is HBM else x for x, s in zip(args, specs)]
    )


def exchange(x, axis, mask):
    return lax.ppermute(x, axis, [(i, i ^ mask) for i in range(lax.axis_size(axis))])


def fetch(pairs, sems):
    copies = [pltpu.make_async_copy(source, place, sems.at[i]) for i, (source, place) in enumerate(pairs)]
    for c in copies:
        c.start()
    return copies


def pack_kernel(bins_hbm, rad_hbm, out_ref, bins_ref, rad_ref, sems):
    for c in fetch([(bins_hbm, bins_ref), (rad_hbm, rad_ref)], sems):
        c.wait()
    bins = bins_ref[:]
    kbins = bins.shape[0]
    fill = jnp.zeros((HEAD - 3 * kbins, bins.shape[1]), jnp.float32)
    parts = [rad_ref[:].astype(jnp.float32), (bins // LANES).astype(jnp.float32), (bins % LANES).astype(jnp.float32)]
    out_ref[:] = jnp.concatenate(parts + [fill], axis=0).astype(jnp.bfloat16)


def sums_kernel(zones):
    def kernel(zone_hbm, area_hbm, openness_hbm, sums_ref, zone_ref, area_ref, openness_ref, sems):
        for c in fetch([(zone_hbm, zone_ref), (area_hbm, area_ref), (openness_hbm, openness_ref)], sems):
            c.wait()
        zone, area = zone_ref[:], area_ref[:]
        lane = lax.broadcasted_iota(jnp.int32, sums_ref.shape, 1)
        values = [area * openness_ref[:], area, area * area]
        row = jnp.zeros(sums_ref.shape, jnp.float32)
        for z in range(zones):
            member = zone == z
            for k, value in enumerate(values):
                total = jnp.sum(jnp.where(member, value, 0.0), keepdims=True)
                row = jnp.where(lane == FRONT + 3 * z + k, total, row)
        sums_ref[:] = row

    return kernel


def sun_kernel(count, kbins, stream):
    def kernel(coef_in, *refs):
        heads, outs, rest = refs[:count], refs[count : 2 * count], refs[2 * count :]
        rows = heads[0].shape[1]
        nbins = coef_in.shape[0]
        step = CHUNK * LANES
        spans = [(first, min(first + step, nbins)) for first in range(0, nbins, step)]
        if stream:
            coef_ref, acc, pattern, block, sems = rest
            cuts = spans[:-2] + [(spans[-2][0], nbins)]
            at = [pl.ds(first, end - first) for first, end in cuts]
            copies = fetch([(coef_in.at[a], coef_ref.at[a]) for a in at], sems)
        else:
            coef_ref, (acc, pattern, block) = coef_in, rest
        lane = lax.broadcasted_iota(jnp.int32, (rows, LANES), 1)
        for g in range(count):
            small = heads[g][:].astype(jnp.float32).T
            value = jnp.zeros((rows, LANES), jnp.float32)
            where = jnp.zeros((rows, LANES), jnp.float32)
            for k in range(kbins):
                low = small[:, 2 * kbins + k : 2 * kbins + k + 1].astype(jnp.int32)
                hit = lane == low
                value = jnp.where(hit, small[:, k : k + 1], value)
                where = jnp.where(hit, small[:, kbins + k : kbins + k + 1], where)
            pattern[g * rows : (g + 1) * rows] = value.astype(pattern.dtype)
            block[g * rows : (g + 1) * rows] = where.astype(block.dtype)

        for i, (first, end) in enumerate(spans):
            parts = []
            for c in range(first // LANES, pl.cdiv(end, LANES)):
                here = block[:] == jnp.asarray(c, block.dtype)
                parts.append(jnp.where(here, pattern[:], jnp.zeros_like(pattern)).astype(jnp.bfloat16))
            weights = jnp.concatenate(parts, axis=1) if len(parts) > 1 else parts[0]
            if stream and i < len(copies):
                copies[i].wait()
            part = jnp.dot(weights[:, : end - first], coef_ref[first:end], preferred_element_type=jnp.float32)
            acc[:] = part if first == 0 else acc[:] + part

        for g in range(count):
            sun = acc[g * rows : (g + 1) * rows]
            power = jnp.ceil(jnp.log2(jnp.maximum(jnp.max(sun, axis=0, keepdims=True), 1e-30)))
            code = jnp.round(sun * (LEVELS / jnp.exp2(power)) - 0.5 * LEVELS)
            outs[g][:rows] = code.astype(jnp.int32).astype(jnp.int16)
            power = jnp.broadcast_to(power, (TAIL, power.shape[1]))
            outs[g][rows:] = power.astype(jnp.int32).astype(jnp.int16)

    return kernel


def base_kernel(
    token, sky_hbm, open_hbm, closed_hbm, target_hbm, cross_ref, closed_out, target_out, sky_ref, open_ref, closed_ref, sems
):
    pairs = [(sky_hbm, sky_ref), (open_hbm, open_ref), (closed_hbm, closed_ref), (target_hbm, target_out)]
    copies = fetch(pairs, sems)
    for c in copies[:3]:
        c.wait()
    over = (((0,), (0,)), ((), ()))
    closed = lax.dot_general(sky_ref[:], closed_ref[:], over, preferred_element_type=jnp.float32)
    opened = lax.dot_general(sky_ref[:], open_ref[:], over, preferred_element_type=jnp.float32)
    closed_out[:] = closed
    cross_ref[:] = opened - closed
    copies[3].wait()


def place(me_ref, mask, width):
    return pl.ds(pl.multiple_of((me_ref[0] ^ mask) * width, LANES), width)


def cross_of(codes, base):
    rows = base.shape[0]
    scale = jnp.exp2(codes[rows:].astype(jnp.int32).astype(jnp.float32)[:1]) / LEVELS
    sun = (codes[:rows].astype(jnp.int32).astype(jnp.float32) + 0.5 * LEVELS) * scale
    return base + sun


def grad_terms(me_ref, base_ref, closed_ref, target_ref, codes, masks, linear, square):
    rows, width = base_ref.shape[0], codes[0].shape[1]
    for mask, code in zip(masks, codes):
        at = place(me_ref, mask, width)
        cross = cross_of(code, base_ref[:, at])
        apart = closed_ref[:, at] - target_ref[:, at].astype(jnp.float32)
        linear = linear + jnp.sum((apart * cross).reshape(rows // 8, 8, width), axis=0)
        square = square + jnp.sum((cross * cross).reshape(rows // 8, 8, width), axis=0)
    return linear, square


def first_kernel(masks):
    def kernel(me_ref, base_ref, closed_ref, target_ref, *refs):
        codes, out_ref = refs[:-1], refs[-1]
        zero = jnp.zeros(out_ref.shape[1:], jnp.float32)
        out_ref[0], out_ref[1] = grad_terms(me_ref, base_ref, closed_ref, target_ref, codes, masks, zero, zero)

    return kernel


def second_kernel(masks):
    def kernel(me_ref, base_ref, closed_ref, target_ref, first_ref, sums_ref, *refs):
        codes, out_ref = refs[:-1], refs[-1]
        linear, square = grad_terms(
            me_ref, base_ref, closed_ref, target_ref, codes, masks, first_ref[0], first_ref[1]
        )
        lane = lax.broadcasted_iota(jnp.int32, sums_ref.shape, 1)
        row = jnp.where(lane == 0, 2.0 * jnp.sum(linear, keepdims=True), sums_ref[:])
        row = jnp.where(lane == 1, 2.0 * jnp.sum(square, keepdims=True), row)
        out_ref[:] = jnp.broadcast_to(row[None], out_ref.shape)

    return kernel


def last_kernel(groups, zones, windows):
    def kernel(place_ref, own_ref, heard_ref, zone_ref, area_ref, openness_ref, base_ref, closed_ref, *refs):
        codes, (lit_hbm, step_ref, lit_ref, sems) = refs[:groups], refs[groups:]
        sums = heard_ref[0]
        for z in range(1, zones):
            sums = sums + heard_ref[z * groups]
        zone = zone_ref[:]
        chosen = jnp.zeros(zone.shape, jnp.float32)
        square = jnp.zeros((1, 1), jnp.float32)
        own_share = jnp.zeros((1, 1), jnp.float32)
        for z in range(zones):
            at = FRONT + 3 * z
            num, den, squares = sums[:, at : at + 1], sums[:, at + 1 : at + 2], sums[:, at + 2 : at + 3]
            share = num / den
            both = jnp.sum(heard_ref[z * groups : (z + 1) * groups], axis=0)
            ratio = (both[:, 0:1] + share * both[:, 1:2]) / den
            square = square + ratio * ratio * squares
            chosen = jnp.where(zone == z, ratio, chosen)
            own_share = jnp.where(own_ref[0] == z, share, own_share)
        rms = jnp.sqrt(square / windows + 1e-06)
        step_ref[:] = jnp.clip(openness_ref[:] - 0.25 * (area_ref[:] * chosen) / rms, 0.0, 1.0)
        width = codes[0].shape[1]
        copies = []
        for mask in range(groups):
            at = place(place_ref, mask, width)
            lit = closed_ref[:, at] + own_share * cross_of(codes[mask], base_ref[:, at])
            lit_ref[mask] = lit.astype(jnp.bfloat16)
            copies.append(pltpu.make_async_copy(lit_ref.at[mask], lit_hbm.at[:, at], sems.at[mask]))
            copies[mask].start()
        for c in copies:
            c.wait()

    return kernel


def local(sky, sky_open, sky_closed, sun_coef, sun_bins, sun_rad, target, zone_of, area, openness):
    zones = lax.axis_size("sens")
    groups = lax.axis_size("hour")
    me = lax.axis_index("hour").astype(jnp.int32)[None]
    own_zone = lax.axis_index("sens").astype(jnp.int32)[None]
    rows, patches = sky.shape
    kbins = sun_bins.shape[1]
    nbins, width = sun_coef.shape
    hours = rows * groups
    sensors = groups * width
    windows = area.shape[0]
    assert nbins % LANES == 0 or nbins % LANES >= 2 * kbins
    assert nbins <= 256 * LANES and width % LANES == 0 and windows % LANES == 0 and 3 * kbins <= HEAD
    assert groups & (groups - 1) == 0 and groups > 1 and rows % 16 == 0
    shape = jax.ShapeDtypeStruct
    f32, bf16 = jnp.float32, jnp.bfloat16
    dma = lambda n: pltpu.SemaphoreType.DMA((n,))

    packed = call(
        pack_kernel,
        "pack",
        shape((HEAD, rows), bf16),
        in_specs=[HBM, HBM],
        scratch_shapes=[pltpu.VMEM((kbins, rows), jnp.int32), pltpu.VMEM((kbins, rows), bf16), dma(2)],
    )(sun_bins.T, sun_rad.T)
    order = list(range(groups))[::-1]
    heads = {mask: exchange(packed, "hour", mask) if mask else packed for mask in order}

    tiles = (windows // LANES, LANES)
    message = pl.cdiv(FRONT + 3 * zones, LANES) * LANES
    zone_sums, zone2, area2, openness2 = call(
        sums_kernel(zones),
        "sums",
        [shape((1, message), f32), shape(tiles, jnp.int32), shape(tiles, f32), shape(tiles, f32)],
        in_specs=[HBM] * 3,
        out_specs=[VMEM] * 4,
        scratch_shapes=[dma(3)],
    )(zone_of.reshape(tiles), area.reshape(tiles), openness.reshape(tiles))

    def sun(masks, coef, stream):
        count = len(masks)
        outs = [shape((rows + TAIL, width), jnp.int16)] * count
        scratch = [pltpu.VMEM((count * rows, width), f32)] + [pltpu.VMEM((count * rows, LANES), PATTERN)] * 2
        found = call(
            sun_kernel(count, kbins, stream),
            "sun",
            outs + [shape((nbins, width), bf16)] * stream,
            flops=2 * count * rows * nbins * width * stream,
            moved=2 * nbins * width * stream,
            in_specs=[HBM if stream else VMEM] + [VMEM] * count,
            out_specs=[VMEM] * (count + stream),
            scratch_shapes=scratch + [dma(pl.cdiv(nbins, CHUNK * LANES))] * stream,
        )(coef, *[heads[mask] for mask in masks])
        return dict(zip(masks, found)), found[-1]

    assert nbins > CHUNK * LANES
    far, near = order[: groups // 2], order[groups // 2 :]
    suns, coef = sun(far, sun_coef, 1)
    codes = {mask: exchange(x, "hour", mask) for mask, x in suns.items()}
    suns, _ = sun(near, coef, 0)
    codes |= {mask: exchange(x, "hour", mask) if mask else x for mask, x in suns.items()}

    base, closed, wanted = call(
        base_kernel,
        "base",
        [shape((rows, sensors), f32)] * 2 + [shape((rows, sensors), bf16)],
        in_specs=[ANY] + [HBM] * 4,
        out_specs=[VMEM] * 3,
        scratch_shapes=[
            pltpu.VMEM((patches, rows), bf16),
            pltpu.VMEM((patches, sensors), bf16),
            pltpu.VMEM((patches, sensors), bf16),
            dma(4),
        ],
    )(codes[0], sky.T, sky_open, sky_closed, target)
    first_sums = call(
        first_kernel(far),
        "first",
        shape((2, 8, width), f32),
        in_specs=[SMEM] + [VMEM] * (3 + len(far)),
    )(me, base, closed, wanted, *[codes[mask] for mask in far])
    sent = call(
        second_kernel(near),
        "second",
        shape((zones * groups, 1, message), f32),
        in_specs=[SMEM] + [VMEM] * (5 + len(near)),
    )(me, base, closed, wanted, first_sums, zone_sums, *[codes[mask] for mask in near])
    heard = lax.all_to_all(sent, ("sens", "hour"), 0, 0)
    illuminance, new_openness = call(
        last_kernel(groups, zones, windows * zones),
        "last",
        [shape((rows, sensors), bf16), shape(tiles, f32)],
        in_specs=[SMEM] * 2 + [VMEM] * (6 + groups),
        out_specs=[HBM, VMEM],
        scratch_shapes=[pltpu.VMEM((groups, rows, width), bf16), dma(groups)],
    )(me, own_zone, heard, zone2, area2, openness2, base, closed, *[codes[mask] for mask in range(groups)])
    return (illuminance, new_openness.reshape(-1))


def solution(mesh):
    in_specs = (
        P("hour", None),
        P(None, "sens"),
        P(None, "sens"),
        P(None, ("sens", "hour")),
        P("hour", None),
        P("hour", None),
        P("hour", "sens"),
        P("sens", None),
        P("sens"),
        P("sens"),
    )
    out_specs = (P("hour", "sens"), P("sens"))
    return jax.shard_map(local, mesh=mesh, in_specs=in_specs, out_specs=out_specs, check_vma=False)
```

```python
import jax
import jax.numpy as jnp
from jax import lax
from jax.experimental import pallas as pl
from jax.experimental.pallas import tpu as pltpu
from jax.sharding import PartitionSpec as P

LANES = 128
CHUNK = 8
HEAD = 16
TAIL = 8
PATTERN = jnp.bfloat16
LEVELS = 65000.0
VMEM_BYTES = 40 * 1024 * 1024
ANY = pl.BlockSpec(memory_space=pl.ANY)
HBM = pl.BlockSpec(memory_space=pltpu.HBM)
SMEM = pl.BlockSpec(memory_space=pltpu.SMEM)
VMEM = pl.BlockSpec(memory_space=pltpu.VMEM)


def call(kernel, name, out_shape, flops=0, moved=0, **more):
    run = pl.pallas_call(
        kernel,
        out_shape=out_shape,
        name=name,
        compiler_params=pltpu.CompilerParams(vmem_limit_bytes=VMEM_BYTES),
        cost_estimate=pl.CostEstimate(flops=flops, bytes_accessed=moved, transcendentals=0),
        **more,
    )
    specs = more["in_specs"]
    return lambda *args: run(
        *[pltpu.with_memory_space_constraint(x, pltpu.HBM) if s is HBM else x for x, s in zip(args, specs)]
    )


def exchange(x, axis, mask):
    return lax.ppermute(x, axis, [(i, i ^ mask) for i in range(lax.axis_size(axis))])


def fetch(pairs, sems):
    copies = [pltpu.make_async_copy(source, place, sems.at[i]) for i, (source, place) in enumerate(pairs)]
    for c in copies:
        c.start()
    return copies


def pack_kernel(bins_hbm, rad_hbm, out_ref, bins_ref, rad_ref, sems):
    for c in fetch([(bins_hbm, bins_ref), (rad_hbm, rad_ref)], sems):
        c.wait()
    bins = bins_ref[:]
    kbins = bins.shape[0]
    fill = jnp.zeros((HEAD - 3 * kbins, bins.shape[1]), jnp.float32)
    parts = [rad_ref[:].astype(jnp.float32), (bins // LANES).astype(jnp.float32), (bins % LANES).astype(jnp.float32)]
    out_ref[:] = jnp.concatenate(parts + [fill], axis=0).astype(jnp.bfloat16)


def fetch_kernel(zones):
    def kernel(coef_hbm, zone_hbm, area_hbm, openness_hbm, coef_ref, sums_ref, zone_ref, area_ref, openness_ref, sems):
        pairs = [(zone_hbm, zone_ref), (area_hbm, area_ref), (openness_hbm, openness_ref)]
        copies = fetch(pairs + [(coef_hbm.at[pl.ds(0, coef_ref.shape[0])], coef_ref)], sems)
        for c in copies[:3]:
            c.wait()
        zone, area = zone_ref[:], area_ref[:]
        lane = lax.broadcasted_iota(jnp.int32, sums_ref.shape, 1)
        values = [area * openness_ref[:], area, area * area]
        row = jnp.zeros(sums_ref.shape, jnp.float32)
        for z in range(zones):
            member = zone == z
            for k, value in enumerate(values):
                total = jnp.sum(jnp.where(member, value, 0.0), keepdims=True)
                row = jnp.where(lane == (2 + k) * zones + z, total, row)
        sums_ref[:] = row
        copies[3].wait()

    return kernel


def sun_kernel(sources, kbins, stream):
    count = len(sources)
    inputs = 1 + max(operand for operand, _ in sources)

    def kernel(first_ref, rest_in, *refs):
        heads, outs, rest = refs[:inputs], refs[inputs : inputs + count], refs[inputs + count :]
        rows = heads[0].shape[1]
        split = first_ref.shape[0]
        nbins = split + rest_in.shape[0] - (split if stream else 0)
        step = CHUNK * LANES
        spans = [(first, min(first + step, nbins)) for first in range(0, nbins, step)]
        if stream:
            rest_ref, both_ref, acc, pattern, block, sems = rest
            late = [span for span in spans if span[0] >= split]
            cuts = late[:-2] + [(late[-2][0], nbins)]
            copies = fetch(
                [
                    (rest_in.at[pl.ds(first, end - first)], rest_ref.at[pl.ds(first - split, end - first)])
                    for first, end in cuts
                ],
                sems,
            )
            waits = {first: c for (first, _), c in zip(cuts, copies)}
            for i, head in enumerate(heads):
                both_ref[i * HEAD : (i + 1) * HEAD] = head[:]
        else:
            rest_ref, (acc, pattern, block) = rest_in, rest
            waits = {}
        lane = lax.broadcasted_iota(jnp.int32, (rows, LANES), 1)
        for g in range(count):
            operand, offset = sources[g]
            small = heads[operand][offset : offset + HEAD].astype(jnp.float32).T
            value = jnp.zeros((rows, LANES), jnp.float32)
            where = jnp.zeros((rows, LANES), jnp.float32)
            for k in range(kbins):
                low = small[:, 2 * kbins + k : 2 * kbins + k + 1].astype(jnp.int32)
                hit = lane == low
                value = jnp.where(hit, small[:, k : k + 1], value)
                where = jnp.where(hit, small[:, kbins + k : kbins + k + 1], where)
            pattern[g * rows : (g + 1) * rows] = value.astype(pattern.dtype)
            block[g * rows : (g + 1) * rows] = where.astype(block.dtype)

        for first, end in spans:
            parts = []
            for c in range(first // LANES, pl.cdiv(end, LANES)):
                here = block[:] == jnp.asarray(c, block.dtype)
                parts.append(jnp.where(here, pattern[:], jnp.zeros_like(pattern)).astype(jnp.bfloat16))
            weights = jnp.concatenate(parts, axis=1) if len(parts) > 1 else parts[0]
            if first in waits:
                waits[first].wait()
            coef = first_ref[first:end] if first < split else rest_ref[first - split : end - split]
            part = jnp.dot(weights[:, : end - first], coef, preferred_element_type=jnp.float32)
            acc[:] = part if first == 0 else acc[:] + part

        for g in range(count):
            sun = acc[g * rows : (g + 1) * rows]
            power = jnp.ceil(jnp.log2(jnp.maximum(jnp.max(sun, axis=0, keepdims=True), 1e-30)))
            code = jnp.round(sun * (LEVELS / jnp.exp2(power)) - 0.5 * LEVELS)
            outs[g][:rows] = code.astype(jnp.int32).astype(jnp.int16)
            power = jnp.broadcast_to(power, (TAIL, power.shape[1]))
            outs[g][rows:] = power.astype(jnp.int32).astype(jnp.int16)

    return kernel


def base_kernel(
    token, sky_hbm, open_hbm, closed_hbm, target_hbm, cross_ref, closed_out, target_out, sky_ref, open_ref, closed_ref, sems
):
    pairs = [(sky_hbm, sky_ref), (open_hbm, open_ref), (closed_hbm, closed_ref), (target_hbm, target_out)]
    copies = fetch(pairs, sems)
    for c in copies[:3]:
        c.wait()
    over = (((0,), (0,)), ((), ()))
    closed = lax.dot_general(sky_ref[:], closed_ref[:], over, preferred_element_type=jnp.float32)
    opened = lax.dot_general(sky_ref[:], open_ref[:], over, preferred_element_type=jnp.float32)
    closed_out[:] = closed
    cross_ref[:] = opened - closed
    copies[3].wait()


def place(me_ref, mask, width):
    return pl.ds(pl.multiple_of((me_ref[0] ^ mask) * width, LANES), width)


def cross_of(codes, base):
    rows = base.shape[0]
    scale = jnp.exp2(codes[rows:].astype(jnp.int32).astype(jnp.float32)[:1]) / LEVELS
    sun = (codes[:rows].astype(jnp.int32).astype(jnp.float32) + 0.5 * LEVELS) * scale
    return base + sun


def grad_terms(me_ref, base_ref, closed_ref, target_ref, codes, masks, linear, square):
    rows, width = base_ref.shape[0], codes[0].shape[1]
    for mask, code in zip(masks, codes):
        at = place(me_ref, mask, width)
        cross = cross_of(code, base_ref[:, at])
        apart = closed_ref[:, at] - target_ref[:, at].astype(jnp.float32)
        linear = linear + jnp.sum((apart * cross).reshape(rows // 8, 8, width), axis=0)
        square = square + jnp.sum((cross * cross).reshape(rows // 8, 8, width), axis=0)
    return linear, square


def first_kernel(masks):
    def kernel(me_ref, base_ref, closed_ref, target_ref, *refs):
        codes, out_ref = refs[:-1], refs[-1]
        zero = jnp.zeros(out_ref.shape[1:], jnp.float32)
        out_ref[0], out_ref[1] = grad_terms(me_ref, base_ref, closed_ref, target_ref, codes, masks, zero, zero)

    return kernel


def second_kernel(masks, zones):
    def kernel(me_ref, own_ref, base_ref, closed_ref, target_ref, first_ref, sums_ref, *refs):
        codes, out_ref = refs[:-1], refs[-1]
        linear, square = grad_terms(
            me_ref, base_ref, closed_ref, target_ref, codes, masks, first_ref[0], first_ref[1]
        )
        lane = lax.broadcasted_iota(jnp.int32, sums_ref.shape, 1)
        row = jnp.where(lane == own_ref[0], 2.0 * jnp.sum(linear, keepdims=True), sums_ref[:])
        row = jnp.where(lane == own_ref[0] + zones, 2.0 * jnp.sum(square, keepdims=True), row)
        out_ref[:] = jnp.broadcast_to(row[None], out_ref.shape)

    return kernel


def last_kernel(groups, zones, windows):
    def kernel(place_ref, own_ref, heard_ref, zone_ref, area_ref, openness_ref, base_ref, closed_ref, *refs):
        codes, (lit_ref, step_ref) = refs[:groups], refs[groups:]
        total = jnp.sum(heard_ref[:], axis=0)
        linear, quadratic, num, den, squares = [total[:, i * zones : (i + 1) * zones] for i in range(5)]
        share = num / den
        lane = lax.broadcasted_iota(jnp.int32, share.shape, 1)
        own_share = jnp.sum(jnp.where(lane == own_ref[0], share, 0.0), keepdims=True)
        width = codes[0].shape[1]
        for mask in range(groups):
            at = place(place_ref, mask, width)
            lit = closed_ref[:, at] + own_share * cross_of(codes[mask], base_ref[:, at])
            lit_ref[:, at] = lit.astype(jnp.bfloat16)
        ratio = groups * (linear + share * quadratic) / den
        rms = jnp.sqrt(jnp.sum(ratio * ratio * squares, keepdims=True) / (windows * groups) + 1e-06)
        zone = zone_ref[:]
        chosen = jnp.zeros(zone.shape, jnp.float32)
        for z in range(zones):
            chosen = jnp.where(zone == z, ratio[:, z : z + 1], chosen)
        step_ref[:] = jnp.clip(openness_ref[:] - 0.25 * (area_ref[:] * chosen) / rms, 0.0, 1.0)

    return kernel


def local(sky, sky_open, sky_closed, sun_coef, sun_bins, sun_rad, target, zone_of, area, openness):
    zones = lax.axis_size("sens")
    groups = lax.axis_size("hour")
    me = lax.axis_index("hour").astype(jnp.int32)[None]
    own_zone = lax.axis_index("sens").astype(jnp.int32)[None]
    rows, patches = sky.shape
    kbins = sun_bins.shape[1]
    nbins, width = sun_coef.shape
    hours = rows * groups
    sensors = groups * width
    windows = area.shape[0]
    assert nbins % LANES == 0 or nbins % LANES >= 2 * kbins
    assert nbins <= 256 * LANES and width % LANES == 0 and windows % LANES == 0 and 3 * kbins <= HEAD
    assert groups == 4 and rows % 16 == 0
    shape = jax.ShapeDtypeStruct
    f32, bf16 = jnp.float32, jnp.bfloat16
    dma = lambda n: pltpu.SemaphoreType.DMA((n,))

    packed = call(
        pack_kernel,
        "pack",
        shape((HEAD, rows), bf16),
        in_specs=[HBM, HBM],
        scratch_shapes=[pltpu.VMEM((kbins, rows), jnp.int32), pltpu.VMEM((kbins, rows), bf16), dma(2)],
    )(sun_bins.T, sun_rad.T)
    heads = exchange(packed, "hour", 3)

    tiles = (windows // LANES, LANES)
    message = pl.cdiv(5 * zones, LANES) * LANES
    split = nbins // 2 // (CHUNK * LANES) * CHUNK * LANES + CHUNK * LANES
    assert split + 2 * CHUNK * LANES < nbins <= split + 3 * CHUNK * LANES
    coef, zone_sums, zone2, area2, openness2 = call(
        fetch_kernel(zones),
        "fetch",
        [shape((split, width), bf16), shape((1, message), f32)]
        + [shape(tiles, jnp.int32), shape(tiles, f32), shape(tiles, f32)],
        in_specs=[HBM] * 4,
        out_specs=[VMEM] * 5,
        scratch_shapes=[dma(4)],
    )(sun_coef, zone_of.reshape(tiles), area.reshape(tiles), openness.reshape(tiles))

    def sun(sources, rest, stream, *heads):
        count = len(sources)
        late = [shape((nbins - split, width), bf16), shape((2 * HEAD, rows), bf16)] if stream else []
        scratch = [pltpu.VMEM((count * rows, width), f32)] + [pltpu.VMEM((count * rows, LANES), PATTERN)] * 2
        return call(
            sun_kernel(sources, kbins, stream),
            "sun",
            [shape((rows + TAIL, width), jnp.int16)] * count + late,
            in_specs=[VMEM, HBM if stream else VMEM] + [VMEM] * len(heads),
            out_specs=[VMEM] * (count + len(late)),
            scratch_shapes=scratch + ([dma(2)] if stream else []),
        )(coef, rest, *heads)

    codes = [None] * groups
    code, late, both = sun([(1, 0)], sun_coef, True, packed, heads)
    codes[3] = exchange(code, "hour", 3)
    heads = exchange(both, "hour", 1)
    (code,) = sun([(0, HEAD)], late, False, heads)
    codes[2] = exchange(code, "hour", 2)
    code, codes[0] = sun([(0, 0), (1, 0)], late, False, heads, packed)
    codes[1] = exchange(code, "hour", 1)

    base, closed, wanted = call(
        base_kernel,
        "base",
        [shape((rows, sensors), f32)] * 2 + [shape((rows, sensors), bf16)],
        in_specs=[ANY] + [HBM] * 4,
        out_specs=[VMEM] * 3,
        scratch_shapes=[
            pltpu.VMEM((patches, rows), bf16),
            pltpu.VMEM((patches, sensors), bf16),
            pltpu.VMEM((patches, sensors), bf16),
            dma(4),
        ],
    )(codes[0], sky.T, sky_open, sky_closed, target)
    first, second = [3, 2, 0], [1]
    first_sums = call(
        first_kernel(first),
        "first",
        shape((2, 8, width), f32),
        in_specs=[SMEM] + [VMEM] * (3 + len(first)),
    )(me, base, closed, wanted, *[codes[mask] for mask in first])
    sent = call(
        second_kernel(second, zones),
        "second",
        shape((zones * groups, 1, message), f32),
        in_specs=[SMEM] * 2 + [VMEM] * (5 + len(second)),
    )(me, own_zone, base, closed, wanted, first_sums, zone_sums, *[codes[mask] for mask in second])
    heard = lax.all_to_all(sent, ("sens", "hour"), 0, 0)
    illuminance, new_openness = call(
        last_kernel(groups, zones, windows * zones),
        "last",
        [shape((rows, sensors), bf16), shape(tiles, f32)],
        in_specs=[SMEM] * 2 + [VMEM] * (6 + groups),
    )(me, own_zone, heard, zone2, area2, openness2, base, closed, *codes)
    return (illuminance, new_openness.reshape(-1))


def solution(mesh):
    in_specs = (
        P("hour", None),
        P(None, "sens"),
        P(None, "sens"),
        P(None, ("sens", "hour")),
        P("hour", None),
        P("hour", None),
        P("hour", "sens"),
        P("sens", None),
        P("sens"),
        P("sens"),
    )
    out_specs = (P("hour", "sens"), P("sens"))
    return jax.shard_map(local, mesh=mesh, in_specs=in_specs, out_specs=out_specs, check_vma=False)
```

```python
import jax
import jax.numpy as jnp
from jax import lax
from jax.experimental import pallas as pl
from jax.experimental.pallas import tpu as pltpu
from jax.sharding import PartitionSpec as P

LANES = 128
CHUNK = 8
HEAD = 16
TAIL = 8
PATTERN = jnp.bfloat16
LEVELS = 65000.0
VMEM_BYTES = 40 * 1024 * 1024
ANY = pl.BlockSpec(memory_space=pl.ANY)
HBM = pl.BlockSpec(memory_space=pltpu.HBM)
SMEM = pl.BlockSpec(memory_space=pltpu.SMEM)
VMEM = pl.BlockSpec(memory_space=pltpu.VMEM)


def call(kernel, name, out_shape, flops=0, moved=0, **more):
    run = pl.pallas_call(
        kernel,
        out_shape=out_shape,
        name=name,
        compiler_params=pltpu.CompilerParams(vmem_limit_bytes=VMEM_BYTES),
        cost_estimate=pl.CostEstimate(flops=flops, bytes_accessed=moved, transcendentals=0),
        **more,
    )
    specs = more["in_specs"]
    return lambda *args: run(
        *[pltpu.with_memory_space_constraint(x, pltpu.HBM) if s is HBM else x for x, s in zip(args, specs)]
    )


def exchange(x, axis, mask):
    return lax.ppermute(x, axis, [(i, i ^ mask) for i in range(lax.axis_size(axis))])


def fetch(pairs, sems):
    copies = [pltpu.make_async_copy(source, place, sems.at[i]) for i, (source, place) in enumerate(pairs)]
    for c in copies:
        c.start()
    return copies


def pack_kernel(me_ref, bins_hbm, rad_hbm, sky_hbm, target_hbm, out_ref, far_ref, bins_ref, rad_ref, sky_ref, sems):
    rows, width = target_hbm.shape[0], far_ref.shape[1]
    pairs = [(bins_hbm, bins_ref), (rad_hbm, rad_ref), (sky_hbm, sky_ref)]
    copies = fetch(pairs + [(target_hbm.at[:, place(me_ref, 3, width)], far_ref.at[pl.ds(0, rows)])], sems)
    copies[0].wait()
    copies[1].wait()
    bins = bins_ref[:]
    kbins = bins.shape[0]
    fill = jnp.zeros((HEAD - 3 * kbins, bins.shape[1]), jnp.float32)
    parts = [rad_ref[:].astype(jnp.float32), (bins // LANES).astype(jnp.float32), (bins % LANES).astype(jnp.float32)]
    out_ref[:] = jnp.concatenate(parts + [fill], axis=0).astype(jnp.bfloat16)
    copies[2].wait()
    part = far_ref.shape[0] - rows
    far_ref[rows:] = jnp.zeros((part, width), far_ref.dtype)
    for c in range(pl.cdiv(sky_ref.shape[0], part)):
        some = sky_ref[c * part : (c + 1) * part]
        far_ref[rows : rows + some.shape[0], c * rows : (c + 1) * rows] = some
    copies[3].wait()


def fetch_kernel(zones):
    def kernel(coef_hbm, zone_hbm, area_hbm, openness_hbm, coef_ref, sums_ref, zone_ref, area_ref, openness_ref, sems):
        pairs = [(zone_hbm, zone_ref), (area_hbm, area_ref), (openness_hbm, openness_ref)]
        copies = fetch(pairs + [(coef_hbm.at[pl.ds(0, coef_ref.shape[0])], coef_ref)], sems)
        for c in copies[:3]:
            c.wait()
        zone, area = zone_ref[:], area_ref[:]
        lane = lax.broadcasted_iota(jnp.int32, sums_ref.shape, 1)
        values = [area * openness_ref[:], area, area * area]
        row = jnp.zeros(sums_ref.shape, jnp.float32)
        for z in range(zones):
            member = zone == z
            for k, value in enumerate(values):
                total = jnp.sum(jnp.where(member, value, 0.0), keepdims=True)
                row = jnp.where(lane == (2 + k) * zones + z, total, row)
        sums_ref[:] = row
        copies[3].wait()

    return kernel


def sun_kernel(sources, kbins, stream, plain):
    count = len(sources)
    inputs = 1 + max(operand for operand, _ in sources)

    def kernel(first_ref, rest_in, *refs):
        heads, outs, rest = refs[:inputs], refs[inputs : inputs + count], refs[inputs + count :]
        rows = heads[0].shape[1]
        split = first_ref.shape[0]
        nbins = split + rest_in.shape[0] - (split if stream else 0)
        step = CHUNK * LANES
        spans = [(first, min(first + step, nbins)) for first in range(0, nbins, step)]
        if stream:
            rest_ref, both_ref, acc, pattern, block, sems = rest
            late = [span for span in spans if span[0] >= split]
            cuts = late[:-2] + [(late[-2][0], nbins)]
            copies = fetch(
                [
                    (rest_in.at[pl.ds(first, end - first)], rest_ref.at[pl.ds(first - split, end - first)])
                    for first, end in cuts
                ],
                sems,
            )
            waits = {first: c for (first, _), c in zip(cuts, copies)}
            for i, head in enumerate(heads):
                both_ref[i * HEAD : (i + 1) * HEAD] = head[:]
        else:
            rest_ref, (plain_ref, acc, pattern, block) = rest_in, rest
            waits = {}
        lane = lax.broadcasted_iota(jnp.int32, (rows, LANES), 1)
        for g in range(count):
            operand, offset = sources[g]
            small = heads[operand][offset : offset + HEAD].astype(jnp.float32).T
            value = jnp.zeros((rows, LANES), jnp.float32)
            where = jnp.zeros((rows, LANES), jnp.float32)
            for k in range(kbins):
                low = small[:, 2 * kbins + k : 2 * kbins + k + 1].astype(jnp.int32)
                hit = lane == low
                value = jnp.where(hit, small[:, k : k + 1], value)
                where = jnp.where(hit, small[:, kbins + k : kbins + k + 1], where)
            pattern[g * rows : (g + 1) * rows] = value.astype(pattern.dtype)
            block[g * rows : (g + 1) * rows] = where.astype(block.dtype)

        for first, end in spans:
            parts = []
            for c in range(first // LANES, pl.cdiv(end, LANES)):
                here = block[:] == jnp.asarray(c, block.dtype)
                parts.append(jnp.where(here, pattern[:], jnp.zeros_like(pattern)).astype(jnp.bfloat16))
            weights = jnp.concatenate(parts, axis=1) if len(parts) > 1 else parts[0]
            if first in waits:
                waits[first].wait()
            coef = first_ref[first:end] if first < split else rest_ref[first - split : end - split]
            part = jnp.dot(weights[:, : end - first], coef, preferred_element_type=jnp.float32)
            acc[:] = part if first == 0 else acc[:] + part

        for g in range(count):
            sun = acc[g * rows : (g + 1) * rows]
            if plain == g:
                plain_ref[:] = sun
            power = jnp.ceil(jnp.log2(jnp.maximum(jnp.max(sun, axis=0, keepdims=True), 1e-30)))
            code = jnp.round(sun * (LEVELS / jnp.exp2(power)) - 0.5 * LEVELS)
            outs[g][:rows] = code.astype(jnp.int32).astype(jnp.int16)
            power = jnp.broadcast_to(power, (TAIL, power.shape[1]))
            outs[g][rows:] = power.astype(jnp.int32).astype(jnp.int16)

    return kernel


def base_kernel(patches):
    def kernel(
        me_ref, far_ref, sun_ref, code_ref, sky_hbm, open_hbm, closed_hbm, target_hbm,
        cross_ref, closed_out, target_out, sums_ref, code_out, sky_ref, open_ref, closed_ref, sems,
    ):
        pairs = [(sky_hbm, sky_ref), (open_hbm, open_ref), (closed_hbm, closed_ref), (target_hbm, target_out)]
        copies = fetch(pairs, sems)
        code_out[:] = code_ref[:]
        rows, width = sun_ref.shape
        part = far_ref.shape[0] - rows
        blocks = [far_ref[rows:, c * rows : (c + 1) * rows] for c in range(pl.cdiv(patches, part))]
        far_sky = jnp.concatenate(blocks, axis=0)[:patches]
        for c in copies[:3]:
            c.wait()
        over = (((0,), (0,)), ((), ()))
        dot = lambda x, y: lax.dot_general(x, y, over, preferred_element_type=jnp.float32)
        own = place(me_ref, 0, width)
        closed = dot(far_sky, closed_ref[:, own])
        cross = dot(far_sky, open_ref[:, own]) - closed + sun_ref[:]
        apart = closed - far_ref[:rows].astype(jnp.float32)
        sums_ref[0] = jnp.sum((apart * cross).reshape(rows // 8, 8, width), axis=0)
        sums_ref[1] = jnp.sum((cross * cross).reshape(rows // 8, 8, width), axis=0)
        closed = dot(sky_ref[:], closed_ref[:])
        closed_out[:] = closed
        cross_ref[:] = dot(sky_ref[:], open_ref[:]) - closed
        copies[3].wait()

    return kernel


def place(me_ref, mask, width):
    return pl.ds(pl.multiple_of((me_ref[0] ^ mask) * width, LANES), width)


def cross_of(codes, base):
    rows = base.shape[0]
    scale = jnp.exp2(codes[rows:].astype(jnp.int32).astype(jnp.float32)[:1]) / LEVELS
    sun = (codes[:rows].astype(jnp.int32).astype(jnp.float32) + 0.5 * LEVELS) * scale
    return base + sun


def grad_terms(me_ref, base_ref, closed_ref, target_ref, codes, masks, linear, square):
    rows, width = base_ref.shape[0], codes[0].shape[1]
    for mask, code in zip(masks, codes):
        at = place(me_ref, mask, width)
        cross = cross_of(code, base_ref[:, at])
        apart = closed_ref[:, at] - target_ref[:, at].astype(jnp.float32)
        linear = linear + jnp.sum((apart * cross).reshape(rows // 8, 8, width), axis=0)
        square = square + jnp.sum((cross * cross).reshape(rows // 8, 8, width), axis=0)
    return linear, square


def first_kernel(masks):
    def kernel(me_ref, base_ref, closed_ref, target_ref, sums_ref, *refs):
        codes, out_ref = refs[:-1], refs[-1]
        out_ref[0], out_ref[1] = grad_terms(
            me_ref, base_ref, closed_ref, target_ref, codes, masks, sums_ref[0], sums_ref[1]
        )

    return kernel


def second_kernel(masks, zones):
    def kernel(me_ref, own_ref, base_ref, closed_ref, target_ref, first_ref, sums_ref, *refs):
        codes, out_ref = refs[:-1], refs[-1]
        linear, square = grad_terms(
            me_ref, base_ref, closed_ref, target_ref, codes, masks, first_ref[0], first_ref[1]
        )
        lane = lax.broadcasted_iota(jnp.int32, sums_ref.shape, 1)
        row = jnp.where(lane == own_ref[0], 2.0 * jnp.sum(linear, keepdims=True), sums_ref[:])
        row = jnp.where(lane == own_ref[0] + zones, 2.0 * jnp.sum(square, keepdims=True), row)
        out_ref[:] = jnp.broadcast_to(row[None], out_ref.shape)

    return kernel


def last_kernel(groups, zones, windows):
    def kernel(place_ref, own_ref, heard_ref, zone_ref, area_ref, openness_ref, base_ref, closed_ref, *refs):
        codes, (lit_ref, step_ref) = refs[:groups], refs[groups:]
        total = jnp.sum(heard_ref[:], axis=0)
        linear, quadratic, num, den, squares = [total[:, i * zones : (i + 1) * zones] for i in range(5)]
        share = num / den
        lane = lax.broadcasted_iota(jnp.int32, share.shape, 1)
        own_share = jnp.sum(jnp.where(lane == own_ref[0], share, 0.0), keepdims=True)
        width = codes[0].shape[1]
        for mask in range(groups):
            at = place(place_ref, mask, width)
            lit = closed_ref[:, at] + own_share * cross_of(codes[mask], base_ref[:, at])
            lit_ref[:, at] = lit.astype(jnp.bfloat16)
        ratio = groups * (linear + share * quadratic) / den
        rms = jnp.sqrt(jnp.sum(ratio * ratio * squares, keepdims=True) / (windows * groups) + 1e-06)
        zone = zone_ref[:]
        chosen = jnp.zeros(zone.shape, jnp.float32)
        for z in range(zones):
            chosen = jnp.where(zone == z, ratio[:, z : z + 1], chosen)
        step_ref[:] = jnp.clip(openness_ref[:] - 0.25 * (area_ref[:] * chosen) / rms, 0.0, 1.0)

    return kernel


def local(sky, sky_open, sky_closed, sun_coef, sun_bins, sun_rad, target, zone_of, area, openness):
    zones = lax.axis_size("sens")
    groups = lax.axis_size("hour")
    me = lax.axis_index("hour").astype(jnp.int32)[None]
    own_zone = lax.axis_index("sens").astype(jnp.int32)[None]
    rows, patches = sky.shape
    kbins = sun_bins.shape[1]
    nbins, width = sun_coef.shape
    hours = rows * groups
    sensors = groups * width
    windows = area.shape[0]
    assert nbins % LANES == 0 or nbins % LANES >= 2 * kbins
    assert nbins <= 256 * LANES and width % LANES == 0 and windows % LANES == 0 and 3 * kbins <= HEAD
    assert groups == 4 and rows % 16 == 0
    shape = jax.ShapeDtypeStruct
    f32, bf16 = jnp.float32, jnp.bfloat16
    dma = lambda n: pltpu.SemaphoreType.DMA((n,))

    part = -(-pl.cdiv(patches, width // rows) // 8) * 8
    assert rows == LANES and patches <= part * (width // rows)
    packed, far = call(
        pack_kernel,
        "pack",
        [shape((HEAD, rows), bf16), shape((rows + part, width), bf16)],
        in_specs=[SMEM] + [HBM] * 4,
        out_specs=[VMEM] * 2,
        scratch_shapes=[
            pltpu.VMEM((kbins, rows), jnp.int32),
            pltpu.VMEM((kbins, rows), bf16),
            pltpu.VMEM((patches, rows), bf16),
            dma(4),
        ],
    )(me, sun_bins.T, sun_rad.T, sky.T, target)
    heads = exchange(packed, "hour", 2)
    far = exchange(far, "hour", 3)

    tiles = (windows // LANES, LANES)
    message = pl.cdiv(5 * zones, LANES) * LANES
    split = nbins // 2 // (CHUNK * LANES) * CHUNK * LANES + CHUNK * LANES
    assert split + 2 * CHUNK * LANES < nbins <= split + 3 * CHUNK * LANES
    coef, zone_sums, zone2, area2, openness2 = call(
        fetch_kernel(zones),
        "fetch",
        [shape((split, width), bf16), shape((1, message), f32)]
        + [shape(tiles, jnp.int32), shape(tiles, f32), shape(tiles, f32)],
        in_specs=[HBM] * 4,
        out_specs=[VMEM] * 5,
        scratch_shapes=[dma(4)],
    )(sun_coef, zone_of.reshape(tiles), area.reshape(tiles), openness.reshape(tiles))

    def sun(sources, rest, stream, *heads):
        count = len(sources)
        late = [shape((nbins - split, width), bf16), shape((2 * HEAD, rows), bf16)]
        late = late if stream else [shape((rows, width), f32)]
        scratch = [pltpu.VMEM((count * rows, width), f32)] + [pltpu.VMEM((count * rows, LANES), PATTERN)] * 2
        return call(
            sun_kernel(sources, kbins, stream, None if stream else 0),
            "sun",
            [shape((rows + TAIL, width), jnp.int16)] * count + late,
            in_specs=[VMEM, HBM if stream else VMEM] + [VMEM] * len(heads),
            out_specs=[VMEM] * (count + len(late)),
            scratch_shapes=scratch + ([dma(2)] if stream else []),
        )(coef, rest, *heads)

    codes = [None] * groups
    code, late, both = sun([(1, 0)], sun_coef, True, packed, heads)
    codes[2] = exchange(code, "hour", 2)
    heads = exchange(both, "hour", 1)
    far_code, code, codes[0], far_sun = sun([(0, HEAD), (0, 0), (1, 0)], late, False, heads, packed)
    codes[1] = exchange(code, "hour", 1)

    base, closed, wanted, far_sums, far_code = call(
        base_kernel(patches),
        "base",
        [shape((rows, sensors), f32)] * 2
        + [shape((rows, sensors), bf16), shape((2, 8, width), f32), shape(far_code.shape, jnp.int16)],
        in_specs=[SMEM] + [VMEM] * 3 + [HBM] * 4,
        out_specs=[VMEM] * 5,
        scratch_shapes=[
            pltpu.VMEM((patches, rows), bf16),
            pltpu.VMEM((patches, sensors), bf16),
            pltpu.VMEM((patches, sensors), bf16),
            dma(4),
        ],
    )(me, far, far_sun, far_code, sky.T, sky_open, sky_closed, target)
    codes[3] = exchange(far_code, "hour", 3)
    first, second = [2, 0], [1]
    first_sums = call(
        first_kernel(first),
        "first",
        shape((2, 8, width), f32),
        in_specs=[SMEM] + [VMEM] * (4 + len(first)),
    )(me, base, closed, wanted, far_sums, *[codes[mask] for mask in first])
    sent = call(
        second_kernel(second, zones),
        "second",
        shape((zones * groups, 1, message), f32),
        in_specs=[SMEM] * 2 + [VMEM] * (5 + len(second)),
    )(me, own_zone, base, closed, wanted, first_sums, zone_sums, *[codes[mask] for mask in second])
    heard = lax.all_to_all(sent, ("sens", "hour"), 0, 0)
    illuminance, new_openness = call(
        last_kernel(groups, zones, windows * zones),
        "last",
        [shape((rows, sensors), bf16), shape(tiles, f32)],
        in_specs=[SMEM] * 2 + [VMEM] * (6 + groups),
    )(me, own_zone, heard, zone2, area2, openness2, base, closed, *codes)
    return (illuminance, new_openness.reshape(-1))


def solution(mesh):
    in_specs = (
        P("hour", None),
        P(None, "sens"),
        P(None, "sens"),
        P(None, ("sens", "hour")),
        P("hour", None),
        P("hour", None),
        P("hour", "sens"),
        P("sens", None),
        P("sens"),
        P("sens"),
    )
    out_specs = (P("hour", "sens"), P("sens"))
    return jax.shard_map(local, mesh=mesh, in_specs=in_specs, out_specs=out_specs, check_vma=False)
```

```python
import jax
import jax.numpy as jnp
from jax import lax
from jax.experimental import pallas as pl
from jax.experimental.pallas import tpu as pltpu
from jax.sharding import PartitionSpec as P

LANES = 128
CHUNK = 8
HEAD = 16
TAIL = 8
PATTERN = jnp.bfloat16
LEVELS = 65000.0
VMEM_BYTES = 40 * 1024 * 1024
ANY = pl.BlockSpec(memory_space=pl.ANY)
HBM = pl.BlockSpec(memory_space=pltpu.HBM)
SMEM = pl.BlockSpec(memory_space=pltpu.SMEM)
VMEM = pl.BlockSpec(memory_space=pltpu.VMEM)


def call(kernel, name, out_shape, flops=0, moved=0, **more):
    run = pl.pallas_call(
        kernel,
        out_shape=out_shape,
        name=name,
        compiler_params=pltpu.CompilerParams(vmem_limit_bytes=VMEM_BYTES),
        cost_estimate=pl.CostEstimate(flops=flops, bytes_accessed=moved, transcendentals=0),
        **more,
    )
    specs = more["in_specs"]
    return lambda *args: run(
        *[pltpu.with_memory_space_constraint(x, pltpu.HBM) if s is HBM else x for x, s in zip(args, specs)]
    )


def exchange(x, axis, mask):
    return lax.ppermute(x, axis, [(i, i ^ mask) for i in range(lax.axis_size(axis))])


def fetch(pairs, sems):
    copies = [pltpu.make_async_copy(source, place, sems.at[i]) for i, (source, place) in enumerate(pairs)]
    for c in copies:
        c.start()
    return copies


def pack_kernel(bins_hbm, rad_hbm, out_ref, bins_ref, rad_ref, sems):
    for c in fetch([(bins_hbm, bins_ref), (rad_hbm, rad_ref)], sems):
        c.wait()
    bins = bins_ref[:]
    kbins = bins.shape[0]
    fill = jnp.zeros((HEAD - 3 * kbins, bins.shape[1]), jnp.float32)
    parts = [rad_ref[:].astype(jnp.float32), (bins // LANES).astype(jnp.float32), (bins % LANES).astype(jnp.float32)]
    out_ref[:] = jnp.concatenate(parts + [fill], axis=0).astype(jnp.bfloat16)


def fetch_kernel(zones):
    def kernel(coef_hbm, zone_hbm, area_hbm, openness_hbm, coef_ref, sums_ref, zone_ref, area_ref, openness_ref, sems):
        pairs = [(zone_hbm, zone_ref), (area_hbm, area_ref), (openness_hbm, openness_ref)]
        copies = fetch(pairs + [(coef_hbm.at[pl.ds(0, coef_ref.shape[0])], coef_ref)], sems)
        for c in copies[:3]:
            c.wait()
        zone, area = zone_ref[:], area_ref[:]
        lane = lax.broadcasted_iota(jnp.int32, sums_ref.shape, 1)
        values = [area * openness_ref[:], area, area * area]
        row = jnp.zeros(sums_ref.shape, jnp.float32)
        for z in range(zones):
            member = zone == z
            for k, value in enumerate(values):
                total = jnp.sum(jnp.where(member, value, 0.0), keepdims=True)
                row = jnp.where(lane == (2 + k) * zones + z, total, row)
        sums_ref[:] = row
        copies[3].wait()

    return kernel


def sun_kernel(sources, kbins, stream):
    count = len(sources)
    inputs = 1 + max(operand for operand, _ in sources)

    def kernel(first_ref, rest_in, *refs):
        heads, outs, rest = refs[:inputs], refs[inputs : inputs + count], refs[inputs + count :]
        rows = heads[0].shape[1]
        split = first_ref.shape[0]
        nbins = split + rest_in.shape[0] - (split if stream else 0)
        step = CHUNK * LANES
        spans = [(first, min(first + step, nbins)) for first in range(0, nbins, step)]
        if stream:
            rest_ref, both_ref, acc, pattern, block, sems = rest
            late = [span for span in spans if span[0] >= split]
            cuts = late[:-2] + [(late[-2][0], nbins)]
            copies = fetch(
                [
                    (rest_in.at[pl.ds(first, end - first)], rest_ref.at[pl.ds(first - split, end - first)])
                    for first, end in cuts
                ],
                sems,
            )
            waits = {first: c for (first, _), c in zip(cuts, copies)}
            for i, head in enumerate(heads):
                both_ref[i * HEAD : (i + 1) * HEAD] = head[:]
        else:
            rest_ref, (acc, pattern, block) = rest_in, rest
            waits = {}
        lane = lax.broadcasted_iota(jnp.int32, (rows, LANES), 1)
        for g in range(count):
            operand, offset = sources[g]
            small = heads[operand][offset : offset + HEAD].astype(jnp.float32).T
            value = jnp.zeros((rows, LANES), jnp.float32)
            where = jnp.zeros((rows, LANES), jnp.float32)
            for k in range(kbins):
                low = small[:, 2 * kbins + k : 2 * kbins + k + 1].astype(jnp.int32)
                hit = lane == low
                value = jnp.where(hit, small[:, k : k + 1], value)
                where = jnp.where(hit, small[:, kbins + k : kbins + k + 1], where)
            pattern[g * rows : (g + 1) * rows] = value.astype(pattern.dtype)
            block[g * rows : (g + 1) * rows] = where.astype(block.dtype)

        for first, end in spans:
            parts = []
            for c in range(first // LANES, pl.cdiv(end, LANES)):
                here = block[:] == jnp.asarray(c, block.dtype)
                parts.append(jnp.where(here, pattern[:], jnp.zeros_like(pattern)).astype(jnp.bfloat16))
            weights = jnp.concatenate(parts, axis=1) if len(parts) > 1 else parts[0]
            if first in waits:
                waits[first].wait()
            coef = first_ref[first:end] if first < split else rest_ref[first - split : end - split]
            part = jnp.dot(weights[:, : end - first], coef, preferred_element_type=jnp.float32)
            acc[:] = part if first == 0 else acc[:] + part

        for g in range(count):
            sun = acc[g * rows : (g + 1) * rows]
            power = jnp.ceil(jnp.log2(jnp.maximum(jnp.max(sun, axis=0, keepdims=True), 1e-30)))
            code = jnp.round(sun * (LEVELS / jnp.exp2(power)) - 0.5 * LEVELS)
            outs[g][:rows] = code.astype(jnp.int32).astype(jnp.int16)
            power = jnp.broadcast_to(power, (TAIL, power.shape[1]))
            outs[g][rows:] = power.astype(jnp.int32).astype(jnp.int16)

    return kernel


def base_kernel(
    token, sky_hbm, open_hbm, closed_hbm, target_hbm, cross_ref, closed_out, target_out, sky_ref, open_ref, closed_ref, sems
):
    pairs = [(sky_hbm, sky_ref), (open_hbm, open_ref), (closed_hbm, closed_ref), (target_hbm, target_out)]
    copies = fetch(pairs, sems)
    for c in copies[:3]:
        c.wait()
    over = (((0,), (0,)), ((), ()))
    closed = lax.dot_general(sky_ref[:], closed_ref[:], over, preferred_element_type=jnp.float32)
    opened = lax.dot_general(sky_ref[:], open_ref[:], over, preferred_element_type=jnp.float32)
    closed_out[:] = closed
    cross_ref[:] = opened - closed
    copies[3].wait()


def place(me_ref, mask, width):
    return pl.ds(pl.multiple_of((me_ref[0] ^ mask) * width, LANES), width)


def cross_of(codes, base):
    rows = base.shape[0]
    scale = jnp.exp2(codes[rows:].astype(jnp.int32).astype(jnp.float32)[:1]) / LEVELS
    sun = (codes[:rows].astype(jnp.int32).astype(jnp.float32) + 0.5 * LEVELS) * scale
    return base + sun


def grad_terms(me_ref, base_ref, closed_ref, target_ref, codes, masks, linear, square):
    rows, width = base_ref.shape[0], codes[0].shape[1]
    for mask, code in zip(masks, codes):
        at = place(me_ref, mask, width)
        cross = cross_of(code, base_ref[:, at])
        apart = closed_ref[:, at] - target_ref[:, at].astype(jnp.float32)
        linear = linear + jnp.sum((apart * cross).reshape(rows // 8, 8, width), axis=0)
        square = square + jnp.sum((cross * cross).reshape(rows // 8, 8, width), axis=0)
    return linear, square


def first_kernel(masks):
    def kernel(me_ref, base_ref, closed_ref, target_ref, *refs):
        codes, out_ref = refs[:-1], refs[-1]
        zero = jnp.zeros(out_ref.shape[1:], jnp.float32)
        out_ref[0], out_ref[1] = grad_terms(me_ref, base_ref, closed_ref, target_ref, codes, masks, zero, zero)

    return kernel


def second_kernel(masks, zones):
    def kernel(me_ref, own_ref, base_ref, closed_ref, target_ref, first_ref, sums_ref, *refs):
        codes, out_ref = refs[:-1], refs[-1]
        linear, square = grad_terms(
            me_ref, base_ref, closed_ref, target_ref, codes, masks, first_ref[0], first_ref[1]
        )
        lane = lax.broadcasted_iota(jnp.int32, sums_ref.shape, 1)
        row = jnp.where(lane == own_ref[0], 2.0 * jnp.sum(linear, keepdims=True), sums_ref[:])
        row = jnp.where(lane == own_ref[0] + zones, 2.0 * jnp.sum(square, keepdims=True), row)
        out_ref[:] = jnp.broadcast_to(row[None], out_ref.shape)

    return kernel


def last_kernel(groups, zones, windows):
    def kernel(place_ref, own_ref, heard_ref, zone_ref, area_ref, openness_ref, base_ref, closed_ref, *refs):
        codes, (lit_ref, step_ref) = refs[:groups], refs[groups:]
        total = jnp.sum(heard_ref[:], axis=0)
        linear, quadratic, num, den, squares = [total[:, i * zones : (i + 1) * zones] for i in range(5)]
        share = num / den
        lane = lax.broadcasted_iota(jnp.int32, share.shape, 1)
        own_share = jnp.sum(jnp.where(lane == own_ref[0], share, 0.0), keepdims=True)
        width = codes[0].shape[1]
        for mask in range(groups):
            at = place(place_ref, mask, width)
            lit = closed_ref[:, at] + own_share * cross_of(codes[mask], base_ref[:, at])
            lit_ref[:, at] = lit.astype(jnp.bfloat16)
        ratio = groups * (linear + share * quadratic) / den
        rms = jnp.sqrt(jnp.sum(ratio * ratio * squares, keepdims=True) / (windows * groups) + 1e-06)
        zone = zone_ref[:]
        chosen = jnp.zeros(zone.shape, jnp.float32)
        for z in range(zones):
            chosen = jnp.where(zone == z, ratio[:, z : z + 1], chosen)
        step_ref[:] = jnp.clip(openness_ref[:] - 0.25 * (area_ref[:] * chosen) / rms, 0.0, 1.0)

    return kernel


def local(sky, sky_open, sky_closed, sun_coef, sun_bins, sun_rad, target, zone_of, area, openness):
    zones = lax.axis_size("sens")
    groups = lax.axis_size("hour")
    me = lax.axis_index("hour").astype(jnp.int32)[None]
    own_zone = lax.axis_index("sens").astype(jnp.int32)[None]
    rows, patches = sky.shape
    kbins = sun_bins.shape[1]
    nbins, width = sun_coef.shape
    hours = rows * groups
    sensors = groups * width
    windows = area.shape[0]
    assert nbins % LANES == 0 or nbins % LANES >= 2 * kbins
    assert nbins <= 256 * LANES and width % LANES == 0 and windows % LANES == 0 and 3 * kbins <= HEAD
    assert groups == 4 and rows % 16 == 0
    shape = jax.ShapeDtypeStruct
    f32, bf16 = jnp.float32, jnp.bfloat16
    dma = lambda n: pltpu.SemaphoreType.DMA((n,))

    packed = call(
        pack_kernel,
        "pack",
        shape((HEAD, rows), bf16),
        in_specs=[HBM, HBM],
        scratch_shapes=[pltpu.VMEM((kbins, rows), jnp.int32), pltpu.VMEM((kbins, rows), bf16), dma(2)],
    )(sun_bins.T, sun_rad.T)
    heads = exchange(packed, "hour", 2)

    tiles = (windows // LANES, LANES)
    message = pl.cdiv(5 * zones, LANES) * LANES
    split = nbins // 2 // (CHUNK * LANES) * CHUNK * LANES + CHUNK * LANES
    assert split + 2 * CHUNK * LANES < nbins <= split + 3 * CHUNK * LANES
    coef, zone_sums, zone2, area2, openness2 = call(
        fetch_kernel(zones),
        "fetch",
        [shape((split, width), bf16), shape((1, message), f32)]
        + [shape(tiles, jnp.int32), shape(tiles, f32), shape(tiles, f32)],
        in_specs=[HBM] * 4,
        out_specs=[VMEM] * 5,
        scratch_shapes=[dma(4)],
    )(sun_coef, zone_of.reshape(tiles), area.reshape(tiles), openness.reshape(tiles))

    def sun(sources, rest, stream, *heads):
        count = len(sources)
        late = [shape((nbins - split, width), bf16), shape((2 * HEAD, rows), bf16)] if stream else []
        scratch = [pltpu.VMEM((count * rows, width), f32)] + [pltpu.VMEM((count * rows, LANES), PATTERN)] * 2
        return call(
            sun_kernel(sources, kbins, stream),
            "sun",
            [shape((rows + TAIL, width), jnp.int16)] * count + late,
            in_specs=[VMEM, HBM if stream else VMEM] + [VMEM] * len(heads),
            out_specs=[VMEM] * (count + len(late)),
            scratch_shapes=scratch + ([dma(2)] if stream else []),
        )(coef, rest, *heads)

    codes = [None] * groups
    code, late, both = sun([(1, 0)], sun_coef, True, packed, heads)
    codes[2] = exchange(code, "hour", 2)
    heads = exchange(both, "hour", 1)
    (code,) = sun([(0, HEAD)], late, False, heads)
    codes[3] = exchange(code, "hour", 3)
    code, codes[0] = sun([(0, 0), (1, 0)], late, False, heads, packed)
    codes[1] = exchange(code, "hour", 1)

    base, closed, wanted = call(
        base_kernel,
        "base",
        [shape((rows, sensors), f32)] * 2 + [shape((rows, sensors), bf16)],
        in_specs=[ANY] + [HBM] * 4,
        out_specs=[VMEM] * 3,
        scratch_shapes=[
            pltpu.VMEM((patches, rows), bf16),
            pltpu.VMEM((patches, sensors), bf16),
            pltpu.VMEM((patches, sensors), bf16),
            dma(4),
        ],
    )(codes[0], sky.T, sky_open, sky_closed, target)
    first, second = [2, 3, 0], [1]
    first_sums = call(
        first_kernel(first),
        "first",
        shape((2, 8, width), f32),
        in_specs=[SMEM] + [VMEM] * (3 + len(first)),
    )(me, base, closed, wanted, *[codes[mask] for mask in first])
    sent = call(
        second_kernel(second, zones),
        "second",
        shape((zones * groups, 1, message), f32),
        in_specs=[SMEM] * 2 + [VMEM] * (5 + len(second)),
    )(me, own_zone, base, closed, wanted, first_sums, zone_sums, *[codes[mask] for mask in second])
    heard = lax.all_to_all(sent, ("sens", "hour"), 0, 0)
    illuminance, new_openness = call(
        last_kernel(groups, zones, windows * zones),
        "last",
        [shape((rows, sensors), bf16), shape(tiles, f32)],
        in_specs=[SMEM] * 2 + [VMEM] * (6 + groups),
    )(me, own_zone, heard, zone2, area2, openness2, base, closed, *codes)
    return (illuminance, new_openness.reshape(-1))


def solution(mesh):
    in_specs = (
        P("hour", None),
        P(None, "sens"),
        P(None, "sens"),
        P(None, ("sens", "hour")),
        P("hour", None),
        P("hour", None),
        P("hour", "sens"),
        P("sens", None),
        P("sens"),
        P("sens"),
    )
    out_specs = (P("hour", "sens"), P("sens"))
    return jax.shard_map(local, mesh=mesh, in_specs=in_specs, out_specs=out_specs, check_vma=False)
```

```python
import jax
import jax.numpy as jnp
from jax import lax
from jax.experimental import pallas as pl
from jax.experimental.pallas import tpu as pltpu
from jax.sharding import PartitionSpec as P

LANES = 128
CHUNK = 8
HEAD = 16
TAIL = 8
PATTERN = jnp.bfloat16
LEVELS = 65000.0
VMEM_BYTES = 40 * 1024 * 1024
ANY = pl.BlockSpec(memory_space=pl.ANY)
HBM = pl.BlockSpec(memory_space=pltpu.HBM)
SMEM = pl.BlockSpec(memory_space=pltpu.SMEM)
VMEM = pl.BlockSpec(memory_space=pltpu.VMEM)


def call(kernel, name, out_shape, flops=0, moved=0, **more):
    run = pl.pallas_call(
        kernel,
        out_shape=out_shape,
        name=name,
        compiler_params=pltpu.CompilerParams(vmem_limit_bytes=VMEM_BYTES),
        cost_estimate=pl.CostEstimate(flops=flops, bytes_accessed=moved, transcendentals=0),
        **more,
    )
    specs = more["in_specs"]
    return lambda *args: run(
        *[pltpu.with_memory_space_constraint(x, pltpu.HBM) if s is HBM else x for x, s in zip(args, specs)]
    )


def exchange(x, axis, mask):
    return lax.ppermute(x, axis, [(i, i ^ mask) for i in range(lax.axis_size(axis))])


def fetch(pairs, sems):
    copies = [pltpu.make_async_copy(source, place, sems.at[i]) for i, (source, place) in enumerate(pairs)]
    for c in copies:
        c.start()
    return copies


def pack_kernel(bins_hbm, rad_hbm, out_ref, bins_ref, rad_ref, sems):
    for c in fetch([(bins_hbm, bins_ref), (rad_hbm, rad_ref)], sems):
        c.wait()
    bins = bins_ref[:]
    kbins = bins.shape[0]
    fill = jnp.zeros((HEAD - 3 * kbins, bins.shape[1]), jnp.float32)
    parts = [rad_ref[:].astype(jnp.float32), (bins // LANES).astype(jnp.float32), (bins % LANES).astype(jnp.float32)]
    out_ref[:] = jnp.concatenate(parts + [fill], axis=0).astype(jnp.bfloat16)


def fetch_kernel(zones):
    def kernel(coef_hbm, zone_hbm, area_hbm, openness_hbm, coef_ref, sums_ref, zone_ref, area_ref, openness_ref, sems):
        pairs = [(zone_hbm, zone_ref), (area_hbm, area_ref), (openness_hbm, openness_ref)]
        copies = fetch(pairs + [(coef_hbm.at[pl.ds(0, coef_ref.shape[0])], coef_ref)], sems)
        for c in copies[:3]:
            c.wait()
        zone, area = zone_ref[:], area_ref[:]
        lane = lax.broadcasted_iota(jnp.int32, sums_ref.shape, 1)
        values = [area * openness_ref[:], area, area * area]
        row = jnp.zeros(sums_ref.shape, jnp.float32)
        for z in range(zones):
            member = zone == z
            for k, value in enumerate(values):
                total = jnp.sum(jnp.where(member, value, 0.0), keepdims=True)
                row = jnp.where(lane == (2 + k) * zones + z, total, row)
        sums_ref[:] = row
        copies[3].wait()

    return kernel


def sun_kernel(count, kbins, stream):
    def kernel(first_ref, rest_in, *refs):
        heads, outs, rest = refs[:count], refs[count : 2 * count], refs[2 * count :]
        rows = heads[0].shape[1]
        split = first_ref.shape[0]
        nbins = split + rest_in.shape[0] - (split if stream else 0)
        step = CHUNK * LANES
        spans = [(first, min(first + step, nbins)) for first in range(0, nbins, step)]
        if stream:
            rest_ref, acc, pattern, block, sems = rest
            late = [span for span in spans if span[0] >= split]
            cuts = late[:-2] + [(late[-2][0], nbins)]
            copies = fetch(
                [
                    (rest_in.at[pl.ds(first, end - first)], rest_ref.at[pl.ds(first - split, end - first)])
                    for first, end in cuts
                ],
                sems,
            )
            waits = {first: c for (first, _), c in zip(cuts, copies)}
        else:
            rest_ref, (acc, pattern, block) = rest_in, rest
            waits = {}
        lane = lax.broadcasted_iota(jnp.int32, (rows, LANES), 1)
        for g in range(count):
            small = heads[g][:].astype(jnp.float32).T
            value = jnp.zeros((rows, LANES), jnp.float32)
            where = jnp.zeros((rows, LANES), jnp.float32)
            for k in range(kbins):
                low = small[:, 2 * kbins + k : 2 * kbins + k + 1].astype(jnp.int32)
                hit = lane == low
                value = jnp.where(hit, small[:, k : k + 1], value)
                where = jnp.where(hit, small[:, kbins + k : kbins + k + 1], where)
            pattern[g * rows : (g + 1) * rows] = value.astype(pattern.dtype)
            block[g * rows : (g + 1) * rows] = where.astype(block.dtype)

        for first, end in spans:
            parts = []
            for c in range(first // LANES, pl.cdiv(end, LANES)):
                here = block[:] == jnp.asarray(c, block.dtype)
                parts.append(jnp.where(here, pattern[:], jnp.zeros_like(pattern)).astype(jnp.bfloat16))
            weights = jnp.concatenate(parts, axis=1) if len(parts) > 1 else parts[0]
            if first in waits:
                waits[first].wait()
            coef = first_ref[first:end] if first < split else rest_ref[first - split : end - split]
            part = jnp.dot(weights[:, : end - first], coef, preferred_element_type=jnp.float32)
            acc[:] = part if first == 0 else acc[:] + part

        for g in range(count):
            sun = acc[g * rows : (g + 1) * rows]
            power = jnp.ceil(jnp.log2(jnp.maximum(jnp.max(sun, axis=0, keepdims=True), 1e-30)))
            code = jnp.round(sun * (LEVELS / jnp.exp2(power)) - 0.5 * LEVELS)
            code = code.astype(jnp.int32).astype(jnp.int16)
            cuts = [slice(c, c + LANES) for c in range(0, code.shape[1], LANES)]
            for c, cut in enumerate(cuts):
                outs[g][c * rows : (c + 1) * rows] = code[:, cut]
            tail = [power[:, cut] for cut in cuts] + [jnp.zeros((TAIL - len(cuts), LANES), jnp.float32)]
            outs[g][len(cuts) * rows :] = jnp.concatenate(tail, axis=0).astype(jnp.int32).astype(jnp.int16)

    return kernel


def base_kernel(
    token, sky_hbm, open_hbm, closed_hbm, target_hbm, cross_ref, closed_out, target_out, sky_ref, open_ref, closed_ref, sems
):
    pairs = [(sky_hbm, sky_ref), (open_hbm, open_ref), (closed_hbm, closed_ref), (target_hbm, target_out)]
    copies = fetch(pairs, sems)
    for c in copies[:3]:
        c.wait()
    over = (((0,), (0,)), ((), ()))
    closed = lax.dot_general(sky_ref[:], closed_ref[:], over, preferred_element_type=jnp.float32)
    opened = lax.dot_general(sky_ref[:], open_ref[:], over, preferred_element_type=jnp.float32)
    closed_out[:] = closed
    cross_ref[:] = opened - closed
    copies[3].wait()


def place(me_ref, mask, width):
    return pl.ds(pl.multiple_of((me_ref[0] ^ mask) * width, LANES), width)


def cross_of(codes, base):
    rows, width = base.shape
    columns = width // LANES
    scales = jnp.exp2(codes[columns * rows :].astype(jnp.int32).astype(jnp.float32)) / LEVELS
    suns = []
    for c in range(columns):
        code = codes[c * rows : (c + 1) * rows].astype(jnp.int32).astype(jnp.float32)
        suns.append((code + 0.5 * LEVELS) * scales[c : c + 1])
    return base + jnp.concatenate(suns, axis=1)


def grad_terms(me_ref, base_ref, closed_ref, target_ref, codes, masks, linear, square):
    rows, width = base_ref.shape[0], linear.shape[1]
    for mask, code in zip(masks, codes):
        at = place(me_ref, mask, width)
        cross = cross_of(code, base_ref[:, at])
        apart = closed_ref[:, at] - target_ref[:, at].astype(jnp.float32)
        linear = linear + jnp.sum((apart * cross).reshape(rows // 8, 8, width), axis=0)
        square = square + jnp.sum((cross * cross).reshape(rows // 8, 8, width), axis=0)
    return linear, square


def first_kernel(masks):
    def kernel(me_ref, base_ref, closed_ref, target_ref, *refs):
        codes, out_ref = refs[:-1], refs[-1]
        zero = jnp.zeros(out_ref.shape[1:], jnp.float32)
        out_ref[0], out_ref[1] = grad_terms(me_ref, base_ref, closed_ref, target_ref, codes, masks, zero, zero)

    return kernel


def second_kernel(masks, zones):
    def kernel(me_ref, own_ref, base_ref, closed_ref, target_ref, first_ref, sums_ref, *refs):
        codes, out_ref = refs[:-1], refs[-1]
        linear, square = grad_terms(
            me_ref, base_ref, closed_ref, target_ref, codes, masks, first_ref[0], first_ref[1]
        )
        lane = lax.broadcasted_iota(jnp.int32, sums_ref.shape, 1)
        row = jnp.where(lane == own_ref[0], 2.0 * jnp.sum(linear, keepdims=True), sums_ref[:])
        row = jnp.where(lane == own_ref[0] + zones, 2.0 * jnp.sum(square, keepdims=True), row)
        out_ref[:] = jnp.broadcast_to(row[None], out_ref.shape)

    return kernel


def last_kernel(groups, zones, windows):
    def kernel(place_ref, own_ref, heard_ref, zone_ref, area_ref, openness_ref, base_ref, closed_ref, *refs):
        codes, (lit_ref, step_ref) = refs[:groups], refs[groups:]
        total = jnp.sum(heard_ref[:], axis=0)
        linear, quadratic, num, den, squares = [total[:, i * zones : (i + 1) * zones] for i in range(5)]
        share = num / den
        lane = lax.broadcasted_iota(jnp.int32, share.shape, 1)
        own_share = jnp.sum(jnp.where(lane == own_ref[0], share, 0.0), keepdims=True)
        width = closed_ref.shape[1] // groups
        for mask in range(groups):
            at = place(place_ref, mask, width)
            lit = closed_ref[:, at] + own_share * cross_of(codes[mask], base_ref[:, at])
            lit_ref[:, at] = lit.astype(jnp.bfloat16)
        ratio = groups * (linear + share * quadratic) / den
        rms = jnp.sqrt(jnp.sum(ratio * ratio * squares, keepdims=True) / (windows * groups) + 1e-06)
        zone = zone_ref[:]
        chosen = jnp.zeros(zone.shape, jnp.float32)
        for z in range(zones):
            chosen = jnp.where(zone == z, ratio[:, z : z + 1], chosen)
        step_ref[:] = jnp.clip(openness_ref[:] - 0.25 * (area_ref[:] * chosen) / rms, 0.0, 1.0)

    return kernel


def local(sky, sky_open, sky_closed, sun_coef, sun_bins, sun_rad, target, zone_of, area, openness):
    zones = lax.axis_size("sens")
    groups = lax.axis_size("hour")
    me = lax.axis_index("hour").astype(jnp.int32)[None]
    own_zone = lax.axis_index("sens").astype(jnp.int32)[None]
    rows, patches = sky.shape
    kbins = sun_bins.shape[1]
    nbins, width = sun_coef.shape
    hours = rows * groups
    sensors = groups * width
    windows = area.shape[0]
    assert nbins % LANES == 0 or nbins % LANES >= 2 * kbins
    assert nbins <= 256 * LANES and width % LANES == 0 and windows % LANES == 0 and 3 * kbins <= HEAD
    assert groups == 4 and rows % 16 == 0
    shape = jax.ShapeDtypeStruct
    f32, bf16 = jnp.float32, jnp.bfloat16
    dma = lambda n: pltpu.SemaphoreType.DMA((n,))

    packed = call(
        pack_kernel,
        "pack",
        shape((HEAD, rows), bf16),
        in_specs=[HBM, HBM],
        scratch_shapes=[pltpu.VMEM((kbins, rows), jnp.int32), pltpu.VMEM((kbins, rows), bf16), dma(2)],
    )(sun_bins.T, sun_rad.T)
    heads = {mask: exchange(packed, "hour", mask) for mask in (2, 1, 3)} | {0: packed}

    tiles = (windows // LANES, LANES)
    message = pl.cdiv(5 * zones, LANES) * LANES
    split = nbins // 2 // (CHUNK * LANES) * CHUNK * LANES + CHUNK * LANES
    assert split + 2 * CHUNK * LANES < nbins <= split + 3 * CHUNK * LANES
    coef, zone_sums, zone2, area2, openness2 = call(
        fetch_kernel(zones),
        "fetch",
        [shape((split, width), bf16), shape((1, message), f32)]
        + [shape(tiles, jnp.int32), shape(tiles, f32), shape(tiles, f32)],
        in_specs=[HBM] * 4,
        out_specs=[VMEM] * 5,
        scratch_shapes=[dma(4)],
    )(sun_coef, zone_of.reshape(tiles), area.reshape(tiles), openness.reshape(tiles))

    assert width // LANES <= TAIL

    def sun(masks, rest, stream):
        count = len(masks)
        late = [shape((nbins - split, width), bf16)] if stream else []
        scratch = [pltpu.VMEM((count * rows, width), f32)] + [pltpu.VMEM((count * rows, LANES), PATTERN)] * 2
        return call(
            sun_kernel(count, kbins, stream),
            "sun",
            [shape((width // LANES * rows + TAIL, LANES), jnp.int16)] * count + late,
            in_specs=[VMEM, HBM if stream else VMEM] + [VMEM] * count,
            out_specs=[VMEM] * (count + len(late)),
            scratch_shapes=scratch + ([dma(2)] if stream else []),
        )(coef, rest, *[heads[mask] for mask in masks])

    codes = [None] * groups
    codes[2], late = sun([2], sun_coef, True)
    codes[1], codes[3] = sun([1, 3], late, False)
    (codes[0],) = sun([0], late, False)
    codes = [exchange(code, "hour", mask) if mask else code for mask, code in enumerate(codes)]

    base, closed, wanted = call(
        base_kernel,
        "base",
        [shape((rows, sensors), f32)] * 2 + [shape((rows, sensors), bf16)],
        in_specs=[ANY] + [HBM] * 4,
        out_specs=[VMEM] * 3,
        scratch_shapes=[
            pltpu.VMEM((patches, rows), bf16),
            pltpu.VMEM((patches, sensors), bf16),
            pltpu.VMEM((patches, sensors), bf16),
            dma(4),
        ],
    )(codes[0], sky.T, sky_open, sky_closed, target)
    first, second = [2, 0], [1, 3]
    first_sums = call(
        first_kernel(first),
        "first",
        shape((2, 8, width), f32),
        in_specs=[SMEM] + [VMEM] * (3 + len(first)),
    )(me, base, closed, wanted, *[codes[mask] for mask in first])
    sent = call(
        second_kernel(second, zones),
        "second",
        shape((zones * groups, 1, message), f32),
        in_specs=[SMEM] * 2 + [VMEM] * (5 + len(second)),
    )(me, own_zone, base, closed, wanted, first_sums, zone_sums, *[codes[mask] for mask in second])
    heard = lax.all_to_all(sent, ("sens", "hour"), 0, 0)
    illuminance, new_openness = call(
        last_kernel(groups, zones, windows * zones),
        "last",
        [shape((rows, sensors), bf16), shape(tiles, f32)],
        in_specs=[SMEM] * 2 + [VMEM] * (6 + groups),
    )(me, own_zone, heard, zone2, area2, openness2, base, closed, *codes)
    return (illuminance, new_openness.reshape(-1))


def solution(mesh):
    in_specs = (
        P("hour", None),
        P(None, "sens"),
        P(None, "sens"),
        P(None, ("sens", "hour")),
        P("hour", None),
        P("hour", None),
        P("hour", "sens"),
        P("sens", None),
        P("sens"),
        P("sens"),
    )
    out_specs = (P("hour", "sens"), P("sens"))
    return jax.shard_map(local, mesh=mesh, in_specs=in_specs, out_specs=out_specs, check_vma=False)
```

```python
import jax
import jax.numpy as jnp
from jax import lax
from jax.experimental import pallas as pl
from jax.experimental.pallas import tpu as pltpu
from jax.sharding import PartitionSpec as P

LANES = 128
CHUNK = 8
HEAD = 16
TAIL = 8
PATTERN = jnp.bfloat16
LEVELS = 65000.0
VMEM_BYTES = 12 * 1024 * 1024
ANY = pl.BlockSpec(memory_space=pl.ANY)
HBM = pl.BlockSpec(memory_space=pltpu.HBM)
SMEM = pl.BlockSpec(memory_space=pltpu.SMEM)
VMEM = pl.BlockSpec(memory_space=pltpu.VMEM)


def call(kernel, name, out_shape, flops=0, moved=0, **more):
    run = pl.pallas_call(
        kernel,
        out_shape=out_shape,
        name=name,
        compiler_params=pltpu.CompilerParams(vmem_limit_bytes=VMEM_BYTES),
        cost_estimate=pl.CostEstimate(flops=flops, bytes_accessed=moved, transcendentals=0),
        **more,
    )
    specs = more["in_specs"]
    return lambda *args: run(
        *[pltpu.with_memory_space_constraint(x, pltpu.HBM) if s is HBM else x for x, s in zip(args, specs)]
    )


def exchange(x, axis, mask):
    return lax.ppermute(x, axis, [(i, i ^ mask) for i in range(lax.axis_size(axis))])


def fetch(pairs, sems):
    copies = [pltpu.make_async_copy(source, place, sems.at[i]) for i, (source, place) in enumerate(pairs)]
    for c in copies:
        c.start()
    return copies


def pack_kernel(bins_hbm, rad_hbm, out_ref, bins_ref, rad_ref, sems):
    for c in fetch([(bins_hbm, bins_ref), (rad_hbm, rad_ref)], sems):
        c.wait()
    bins = bins_ref[:]
    kbins = bins.shape[0]
    fill = jnp.zeros((HEAD - 3 * kbins, bins.shape[1]), jnp.float32)
    parts = [rad_ref[:].astype(jnp.float32), (bins // LANES).astype(jnp.float32), (bins % LANES).astype(jnp.float32)]
    out_ref[:] = jnp.concatenate(parts + [fill], axis=0).astype(jnp.bfloat16)


def fetch_kernel(zones):
    def kernel(coef_hbm, zone_hbm, area_hbm, openness_hbm, coef_ref, sums_ref, zone_ref, area_ref, openness_ref, sems):
        pairs = [(zone_hbm, zone_ref), (area_hbm, area_ref), (openness_hbm, openness_ref)]
        copies = fetch(pairs + [(coef_hbm.at[pl.ds(0, coef_ref.shape[0])], coef_ref)], sems)
        for c in copies[:3]:
            c.wait()
        zone, area = zone_ref[:], area_ref[:]
        lane = lax.broadcasted_iota(jnp.int32, sums_ref.shape, 1)
        values = [area * openness_ref[:], area, area * area]
        row = jnp.zeros(sums_ref.shape, jnp.float32)
        for z in range(zones):
            member = zone == z
            for k, value in enumerate(values):
                total = jnp.sum(jnp.where(member, value, 0.0), keepdims=True)
                row = jnp.where(lane == (2 + k) * zones + z, total, row)
        sums_ref[:] = row
        copies[3].wait()

    return kernel


def sun_kernel(count, kbins, stream):
    def kernel(first_ref, rest_in, *refs):
        heads, outs, rest = refs[:count], refs[count : 2 * count], refs[2 * count :]
        rows = heads[0].shape[1]
        split = first_ref.shape[0]
        nbins = split + rest_in.shape[0] - (split if stream else 0)
        step = CHUNK * LANES
        spans = [(first, min(first + step, nbins)) for first in range(0, nbins, step)]
        if stream:
            rest_ref, acc, pattern, block, sems = rest
            late = [span for span in spans if span[0] >= split]
            cuts = late[:-2] + [(late[-2][0], nbins)]
            copies = fetch(
                [
                    (rest_in.at[pl.ds(first, end - first)], rest_ref.at[pl.ds(first - split, end - first)])
                    for first, end in cuts
                ],
                sems,
            )
            waits = {first: c for (first, _), c in zip(cuts, copies)}
        else:
            rest_ref, (acc, pattern, block) = rest_in, rest
            waits = {}
        lane = lax.broadcasted_iota(jnp.int32, (rows, LANES), 1)
        for g in range(count):
            small = heads[g][:].astype(jnp.float32).T
            value = jnp.zeros((rows, LANES), jnp.float32)
            where = jnp.zeros((rows, LANES), jnp.float32)
            for k in range(kbins):
                low = small[:, 2 * kbins + k : 2 * kbins + k + 1].astype(jnp.int32)
                hit = lane == low
                value = jnp.where(hit, small[:, k : k + 1], value)
                where = jnp.where(hit, small[:, kbins + k : kbins + k + 1], where)
            pattern[g * rows : (g + 1) * rows] = value.astype(pattern.dtype)
            block[g * rows : (g + 1) * rows] = where.astype(block.dtype)

        for first, end in spans:
            parts = []
            for c in range(first // LANES, pl.cdiv(end, LANES)):
                here = block[:] == jnp.asarray(c, block.dtype)
                parts.append(jnp.where(here, pattern[:], jnp.zeros_like(pattern)).astype(jnp.bfloat16))
            weights = jnp.concatenate(parts, axis=1) if len(parts) > 1 else parts[0]
            if first in waits:
                waits[first].wait()
            coef = first_ref[first:end] if first < split else rest_ref[first - split : end - split]
            part = jnp.dot(weights[:, : end - first], coef, preferred_element_type=jnp.float32)
            acc[:] = part if first == 0 else acc[:] + part

        for g in range(count):
            sun = acc[g * rows : (g + 1) * rows]
            power = jnp.ceil(jnp.log2(jnp.maximum(jnp.max(sun, axis=0, keepdims=True), 1e-30)))
            code = jnp.round(sun * (LEVELS / jnp.exp2(power)) - 0.5 * LEVELS)
            code = code.astype(jnp.int32).astype(jnp.int16)
            cuts = [slice(c, c + LANES) for c in range(0, code.shape[1], LANES)]
            for c, cut in enumerate(cuts):
                outs[g][c * rows : (c + 1) * rows] = code[:, cut]
            tail = [power[:, cut] for cut in cuts] + [jnp.zeros((TAIL - len(cuts), LANES), jnp.float32)]
            outs[g][len(cuts) * rows :] = jnp.concatenate(tail, axis=0).astype(jnp.int32).astype(jnp.int16)

    return kernel


def base_kernel(
    token, sky_hbm, open_hbm, closed_hbm, target_hbm, cross_ref, closed_out, target_out, sky_ref, open_ref, closed_ref, sems
):
    pairs = [(sky_hbm, sky_ref), (open_hbm, open_ref), (closed_hbm, closed_ref), (target_hbm, target_out)]
    copies = fetch(pairs, sems)
    for c in copies[:3]:
        c.wait()
    over = (((0,), (0,)), ((), ()))
    closed = lax.dot_general(sky_ref[:], closed_ref[:], over, preferred_element_type=jnp.float32)
    opened = lax.dot_general(sky_ref[:], open_ref[:], over, preferred_element_type=jnp.float32)
    closed_out[:] = closed
    cross_ref[:] = opened - closed
    copies[3].wait()


def place(me_ref, mask, width):
    return pl.ds(pl.multiple_of((me_ref[0] ^ mask) * width, LANES), width)


def cross_of(codes, base):
    rows, width = base.shape
    columns = width // LANES
    scales = jnp.exp2(codes[columns * rows :].astype(jnp.int32).astype(jnp.float32)) / LEVELS
    suns = []
    for c in range(columns):
        code = codes[c * rows : (c + 1) * rows].astype(jnp.int32).astype(jnp.float32)
        suns.append((code + 0.5 * LEVELS) * scales[c : c + 1])
    return base + jnp.concatenate(suns, axis=1)


def grad_terms(me_ref, base_ref, closed_ref, target_ref, codes, masks, linear, square):
    rows, width = base_ref.shape[0], linear.shape[1]
    for mask, code in zip(masks, codes):
        at = place(me_ref, mask, width)
        cross = cross_of(code, base_ref[:, at])
        apart = closed_ref[:, at] - target_ref[:, at].astype(jnp.float32)
        linear = linear + jnp.sum((apart * cross).reshape(rows // 8, 8, width), axis=0)
        square = square + jnp.sum((cross * cross).reshape(rows // 8, 8, width), axis=0)
    return linear, square


def first_kernel(masks):
    def kernel(me_ref, base_ref, closed_ref, target_ref, *refs):
        codes, out_ref = refs[:-1], refs[-1]
        zero = jnp.zeros(out_ref.shape[1:], jnp.float32)
        out_ref[0], out_ref[1] = grad_terms(me_ref, base_ref, closed_ref, target_ref, codes, masks, zero, zero)

    return kernel


def second_kernel(masks, zones):
    def kernel(me_ref, own_ref, base_ref, closed_ref, target_ref, first_ref, sums_ref, *refs):
        codes, out_ref = refs[:-1], refs[-1]
        linear, square = grad_terms(
            me_ref, base_ref, closed_ref, target_ref, codes, masks, first_ref[0], first_ref[1]
        )
        lane = lax.broadcasted_iota(jnp.int32, sums_ref.shape, 1)
        row = jnp.where(lane == own_ref[0], 2.0 * jnp.sum(linear, keepdims=True), sums_ref[:])
        row = jnp.where(lane == own_ref[0] + zones, 2.0 * jnp.sum(square, keepdims=True), row)
        out_ref[:] = jnp.broadcast_to(row[None], out_ref.shape)

    return kernel


def last_kernel(groups, zones, windows):
    def kernel(place_ref, own_ref, heard_ref, zone_ref, area_ref, openness_ref, base_ref, closed_ref, *refs):
        codes, (lit_ref, step_ref) = refs[:groups], refs[groups:]
        total = jnp.sum(heard_ref[:], axis=0)
        linear, quadratic, num, den, squares = [total[:, i * zones : (i + 1) * zones] for i in range(5)]
        share = num / den
        lane = lax.broadcasted_iota(jnp.int32, share.shape, 1)
        own_share = jnp.sum(jnp.where(lane == own_ref[0], share, 0.0), keepdims=True)
        width = closed_ref.shape[1] // groups
        for mask in range(groups):
            at = place(place_ref, mask, width)
            lit = closed_ref[:, at] + own_share * cross_of(codes[mask], base_ref[:, at])
            lit_ref[:, at] = lit.astype(jnp.bfloat16)
        ratio = groups * (linear + share * quadratic) / den
        rms = jnp.sqrt(jnp.sum(ratio * ratio * squares, keepdims=True) / (windows * groups) + 1e-06)
        zone = zone_ref[:]
        chosen = jnp.zeros(zone.shape, jnp.float32)
        for z in range(zones):
            chosen = jnp.where(zone == z, ratio[:, z : z + 1], chosen)
        step_ref[:] = jnp.clip(openness_ref[:] - 0.25 * (area_ref[:] * chosen) / rms, 0.0, 1.0)

    return kernel


def local(sky, sky_open, sky_closed, sun_coef, sun_bins, sun_rad, target, zone_of, area, openness):
    zones = lax.axis_size("sens")
    groups = lax.axis_size("hour")
    me = lax.axis_index("hour").astype(jnp.int32)[None]
    own_zone = lax.axis_index("sens").astype(jnp.int32)[None]
    rows, patches = sky.shape
    kbins = sun_bins.shape[1]
    nbins, width = sun_coef.shape
    hours = rows * groups
    sensors = groups * width
    windows = area.shape[0]
    assert nbins % LANES == 0 or nbins % LANES >= 2 * kbins
    assert nbins <= 256 * LANES and width % LANES == 0 and windows % LANES == 0 and 3 * kbins <= HEAD
    assert groups == 4 and rows % 16 == 0
    shape = jax.ShapeDtypeStruct
    f32, bf16 = jnp.float32, jnp.bfloat16
    dma = lambda n: pltpu.SemaphoreType.DMA((n,))

    packed = call(
        pack_kernel,
        "pack",
        shape((HEAD, rows), bf16),
        in_specs=[HBM, HBM],
        scratch_shapes=[pltpu.VMEM((kbins, rows), jnp.int32), pltpu.VMEM((kbins, rows), bf16), dma(2)],
    )(sun_bins.T, sun_rad.T)
    heads = {mask: exchange(packed, "hour", mask) for mask in (2, 1, 3)} | {0: packed}

    tiles = (windows // LANES, LANES)
    message = pl.cdiv(5 * zones, LANES) * LANES
    split = nbins // 2 // (CHUNK * LANES) * CHUNK * LANES + CHUNK * LANES
    assert split + 2 * CHUNK * LANES < nbins <= split + 3 * CHUNK * LANES
    coef, zone_sums, zone2, area2, openness2 = call(
        fetch_kernel(zones),
        "fetch",
        [shape((split, width), bf16), shape((1, message), f32)]
        + [shape(tiles, jnp.int32), shape(tiles, f32), shape(tiles, f32)],
        in_specs=[HBM] * 4,
        out_specs=[VMEM] * 5,
        scratch_shapes=[dma(4)],
    )(sun_coef, zone_of.reshape(tiles), area.reshape(tiles), openness.reshape(tiles))

    assert width // LANES <= TAIL

    def sun(masks, rest, stream):
        count = len(masks)
        late = [shape((nbins - split, width), bf16)] if stream else []
        scratch = [pltpu.VMEM((count * rows, width), f32)] + [pltpu.VMEM((count * rows, LANES), PATTERN)] * 2
        return call(
            sun_kernel(count, kbins, stream),
            "sun",
            [shape((width // LANES * rows + TAIL, LANES), jnp.int16)] * count + late,
            in_specs=[VMEM, HBM if stream else VMEM] + [VMEM] * count,
            out_specs=[VMEM] * (count + len(late)),
            scratch_shapes=scratch + ([dma(2)] if stream else []),
        )(coef, rest, *[heads[mask] for mask in masks])

    codes = [None] * groups
    codes[2], late = sun([2], sun_coef, True)
    codes[1], codes[3] = sun([1, 3], late, False)
    (codes[0],) = sun([0], late, False)
    codes = [exchange(code, "hour", mask) if mask else code for mask, code in enumerate(codes)]

    base, closed, wanted = call(
        base_kernel,
        "base",
        [shape((rows, sensors), f32)] * 2 + [shape((rows, sensors), bf16)],
        in_specs=[ANY] + [HBM] * 4,
        out_specs=[VMEM] * 3,
        scratch_shapes=[
            pltpu.VMEM((patches, rows), bf16),
            pltpu.VMEM((patches, sensors), bf16),
            pltpu.VMEM((patches, sensors), bf16),
            dma(4),
        ],
    )(codes[0], sky.T, sky_open, sky_closed, target)
    first, second = [2, 0], [1, 3]
    first_sums = call(
        first_kernel(first),
        "first",
        shape((2, 8, width), f32),
        in_specs=[SMEM] + [VMEM] * (3 + len(first)),
    )(me, base, closed, wanted, *[codes[mask] for mask in first])
    sent = call(
        second_kernel(second, zones),
        "second",
        shape((zones * groups, 1, message), f32),
        in_specs=[SMEM] * 2 + [VMEM] * (5 + len(second)),
    )(me, own_zone, base, closed, wanted, first_sums, zone_sums, *[codes[mask] for mask in second])
    heard = lax.all_to_all(sent, ("sens", "hour"), 0, 0)
    illuminance, new_openness = call(
        last_kernel(groups, zones, windows * zones),
        "last",
        [shape((rows, sensors), bf16), shape(tiles, f32)],
        in_specs=[SMEM] * 2 + [VMEM] * (6 + groups),
    )(me, own_zone, heard, zone2, area2, openness2, base, closed, *codes)
    return (illuminance, new_openness.reshape(-1))


def solution(mesh):
    in_specs = (
        P("hour", None),
        P(None, "sens"),
        P(None, "sens"),
        P(None, ("sens", "hour")),
        P("hour", None),
        P("hour", None),
        P("hour", "sens"),
        P("sens", None),
        P("sens"),
        P("sens"),
    )
    out_specs = (P("hour", "sens"), P("sens"))
    return jax.shard_map(local, mesh=mesh, in_specs=in_specs, out_specs=out_specs, check_vma=False)
```

```python
import jax
import jax.numpy as jnp
from jax import lax
from jax.experimental import pallas as pl
from jax.experimental.pallas import tpu as pltpu
from jax.sharding import PartitionSpec as P

LANES = 128
CHUNK = 8
HEAD = 16
TAIL = 8
PATTERN = jnp.bfloat16
LEVELS = 65000.0
VMEM_BYTES = 12 * 1024 * 1024
ANY = pl.BlockSpec(memory_space=pl.ANY)
HBM = pl.BlockSpec(memory_space=pltpu.HBM)
SMEM = pl.BlockSpec(memory_space=pltpu.SMEM)
VMEM = pl.BlockSpec(memory_space=pltpu.VMEM)


def call(kernel, name, out_shape, flops=0, moved=0, **more):
    run = pl.pallas_call(
        kernel,
        out_shape=out_shape,
        name=name,
        compiler_params=pltpu.CompilerParams(vmem_limit_bytes=VMEM_BYTES),
        cost_estimate=pl.CostEstimate(flops=flops, bytes_accessed=moved, transcendentals=0),
        **more,
    )
    specs = more["in_specs"]
    return lambda *args: run(
        *[pltpu.with_memory_space_constraint(x, pltpu.HBM) if s is HBM else x for x, s in zip(args, specs)]
    )


def exchange(x, axis, mask):
    return lax.ppermute(x, axis, [(i, i ^ mask) for i in range(lax.axis_size(axis))])


def fetch(pairs, sems):
    copies = [pltpu.make_async_copy(source, place, sems.at[i]) for i, (source, place) in enumerate(pairs)]
    for c in copies:
        c.start()
    return copies


def pack_kernel(me_ref, own_ref, bins_hbm, rad_hbm, out_ref, bins_ref, rad_ref, sems):
    for c in fetch([(bins_hbm, bins_ref), (rad_hbm, rad_ref)], sems):
        c.wait()
    bins = bins_ref[:]
    kbins = bins.shape[0]
    fill = jnp.zeros((HEAD - 3 * kbins, bins.shape[1]), jnp.float32)
    parts = [rad_ref[:].astype(jnp.float32), (bins // LANES).astype(jnp.float32), (bins % LANES).astype(jnp.float32)]
    out_ref[:] = jnp.concatenate(parts + [fill], axis=0).astype(jnp.bfloat16)


def fetch_kernel(zones):
    def kernel(coef_hbm, zone_hbm, area_hbm, openness_hbm, coef_ref, sums_ref, zone_ref, area_ref, openness_ref, sems):
        pairs = [(zone_hbm, zone_ref), (area_hbm, area_ref), (openness_hbm, openness_ref)]
        copies = fetch(pairs + [(coef_hbm.at[pl.ds(0, coef_ref.shape[0])], coef_ref)], sems)
        for c in copies[:3]:
            c.wait()
        zone, area = zone_ref[:], area_ref[:]
        lane = lax.broadcasted_iota(jnp.int32, sums_ref.shape, 1)
        values = [area * openness_ref[:], area, area * area]
        row = jnp.zeros(sums_ref.shape, jnp.float32)
        for z in range(zones):
            member = zone == z
            for k, value in enumerate(values):
                total = jnp.sum(jnp.where(member, value, 0.0), keepdims=True)
                row = jnp.where(lane == (2 + k) * zones + z, total, row)
        sums_ref[:] = row
        copies[3].wait()

    return kernel


def sun_kernel(count, kbins, stream):
    def kernel(first_ref, rest_in, *refs):
        heads, outs, rest = refs[:count], refs[count : 2 * count], refs[2 * count :]
        rows = heads[0].shape[1]
        split = first_ref.shape[0]
        nbins = split + rest_in.shape[0] - (split if stream else 0)
        step = CHUNK * LANES
        spans = [(first, min(first + step, nbins)) for first in range(0, nbins, step)]
        if stream:
            rest_ref, acc, pattern, block, sems = rest
            late = [span for span in spans if span[0] >= split]
            cuts = late[:-2] + [(late[-2][0], nbins)]
            copies = fetch(
                [
                    (rest_in.at[pl.ds(first, end - first)], rest_ref.at[pl.ds(first - split, end - first)])
                    for first, end in cuts
                ],
                sems,
            )
            waits = {first: c for (first, _), c in zip(cuts, copies)}
        else:
            rest_ref, (acc, pattern, block) = rest_in, rest
            waits = {}
        lane = lax.broadcasted_iota(jnp.int32, (rows, LANES), 1)
        for g in range(count):
            small = heads[g][:].astype(jnp.float32).T
            value = jnp.zeros((rows, LANES), jnp.float32)
            where = jnp.zeros((rows, LANES), jnp.float32)
            for k in range(kbins):
                low = small[:, 2 * kbins + k : 2 * kbins + k + 1].astype(jnp.int32)
                hit = lane == low
                value = jnp.where(hit, small[:, k : k + 1], value)
                where = jnp.where(hit, small[:, kbins + k : kbins + k + 1], where)
            pattern[g * rows : (g + 1) * rows] = value.astype(pattern.dtype)
            block[g * rows : (g + 1) * rows] = where.astype(block.dtype)

        for first, end in spans:
            parts = []
            for c in range(first // LANES, pl.cdiv(end, LANES)):
                here = block[:] == jnp.asarray(c, block.dtype)
                parts.append(jnp.where(here, pattern[:], jnp.zeros_like(pattern)).astype(jnp.bfloat16))
            weights = jnp.concatenate(parts, axis=1) if len(parts) > 1 else parts[0]
            if first in waits:
                waits[first].wait()
            coef = first_ref[first:end] if first < split else rest_ref[first - split : end - split]
            part = jnp.dot(weights[:, : end - first], coef, preferred_element_type=jnp.float32)
            acc[:] = part if first == 0 else acc[:] + part

        for g in range(count):
            sun = acc[g * rows : (g + 1) * rows]
            power = jnp.ceil(jnp.log2(jnp.maximum(jnp.max(sun, axis=0, keepdims=True), 1e-30)))
            code = jnp.round(sun * (LEVELS / jnp.exp2(power)) - 0.5 * LEVELS)
            code = code.astype(jnp.int32).astype(jnp.int16)
            cuts = [slice(c, c + LANES) for c in range(0, code.shape[1], LANES)]
            for c, cut in enumerate(cuts):
                outs[g][c * rows : (c + 1) * rows] = code[:, cut]
            tail = [power[:, cut] for cut in cuts] + [jnp.zeros((TAIL - len(cuts), LANES), jnp.float32)]
            outs[g][len(cuts) * rows :] = jnp.concatenate(tail, axis=0).astype(jnp.int32).astype(jnp.int16)

    return kernel


def base_kernel(
    token, sky_hbm, open_hbm, closed_hbm, target_hbm, cross_ref, closed_out, target_out, sky_ref, open_ref, closed_ref, sems
):
    pairs = [(sky_hbm, sky_ref), (open_hbm, open_ref), (closed_hbm, closed_ref), (target_hbm, target_out)]
    copies = fetch(pairs, sems)
    for c in copies[:3]:
        c.wait()
    over = (((0,), (0,)), ((), ()))
    closed = lax.dot_general(sky_ref[:], closed_ref[:], over, preferred_element_type=jnp.float32)
    opened = lax.dot_general(sky_ref[:], open_ref[:], over, preferred_element_type=jnp.float32)
    closed_out[:] = closed
    cross_ref[:] = opened - closed
    copies[3].wait()


def place(me_ref, mask, width):
    return pl.ds(pl.multiple_of((me_ref[0] ^ mask) * width, LANES), width)


def cross_of(codes, base):
    rows, width = base.shape
    columns = width // LANES
    scales = jnp.exp2(codes[columns * rows :].astype(jnp.int32).astype(jnp.float32)) / LEVELS
    suns = []
    for c in range(columns):
        code = codes[c * rows : (c + 1) * rows].astype(jnp.int32).astype(jnp.float32)
        suns.append((code + 0.5 * LEVELS) * scales[c : c + 1])
    return base + jnp.concatenate(suns, axis=1)


def grad_terms(me_ref, base_ref, closed_ref, target_ref, codes, masks, linear, square):
    rows, width = base_ref.shape[0], linear.shape[1]
    for mask, code in zip(masks, codes):
        at = place(me_ref, mask, width)
        cross = cross_of(code, base_ref[:, at])
        apart = closed_ref[:, at] - target_ref[:, at].astype(jnp.float32)
        linear = linear + jnp.sum((apart * cross).reshape(rows // 8, 8, width), axis=0)
        square = square + jnp.sum((cross * cross).reshape(rows // 8, 8, width), axis=0)
    return linear, square


def first_kernel(masks):
    def kernel(me_ref, base_ref, closed_ref, target_ref, *refs):
        codes, out_ref = refs[:-1], refs[-1]
        zero = jnp.zeros(out_ref.shape[1:], jnp.float32)
        out_ref[0], out_ref[1] = grad_terms(me_ref, base_ref, closed_ref, target_ref, codes, masks, zero, zero)

    return kernel


def second_kernel(masks, zones):
    def kernel(me_ref, own_ref, base_ref, closed_ref, target_ref, first_ref, sums_ref, *refs):
        codes, out_ref = refs[:-1], refs[-1]
        linear, square = grad_terms(
            me_ref, base_ref, closed_ref, target_ref, codes, masks, first_ref[0], first_ref[1]
        )
        lane = lax.broadcasted_iota(jnp.int32, sums_ref.shape, 1)
        row = jnp.where(lane == own_ref[0], 2.0 * jnp.sum(linear, keepdims=True), sums_ref[:])
        row = jnp.where(lane == own_ref[0] + zones, 2.0 * jnp.sum(square, keepdims=True), row)
        out_ref[:] = jnp.broadcast_to(row[None], out_ref.shape)

    return kernel


def last_kernel(groups, zones, windows):
    def kernel(place_ref, own_ref, heard_ref, zone_ref, area_ref, openness_ref, base_ref, closed_ref, *refs):
        codes, (lit_ref, step_ref) = refs[:groups], refs[groups:]
        total = jnp.sum(heard_ref[:], axis=0)
        linear, quadratic, num, den, squares = [total[:, i * zones : (i + 1) * zones] for i in range(5)]
        share = num / den
        lane = lax.broadcasted_iota(jnp.int32, share.shape, 1)
        own_share = jnp.sum(jnp.where(lane == own_ref[0], share, 0.0), keepdims=True)
        width = closed_ref.shape[1] // groups
        for mask in range(groups):
            at = place(place_ref, mask, width)
            lit = closed_ref[:, at] + own_share * cross_of(codes[mask], base_ref[:, at])
            lit_ref[:, at] = lit.astype(jnp.bfloat16)
        ratio = groups * (linear + share * quadratic) / den
        rms = jnp.sqrt(jnp.sum(ratio * ratio * squares, keepdims=True) / (windows * groups) + 1e-06)
        zone = zone_ref[:]
        chosen = jnp.zeros(zone.shape, jnp.float32)
        for z in range(zones):
            chosen = jnp.where(zone == z, ratio[:, z : z + 1], chosen)
        step_ref[:] = jnp.clip(openness_ref[:] - 0.25 * (area_ref[:] * chosen) / rms, 0.0, 1.0)

    return kernel


def local(sky, sky_open, sky_closed, sun_coef, sun_bins, sun_rad, target, zone_of, area, openness):
    zones = lax.axis_size("sens")
    groups = lax.axis_size("hour")
    me = lax.axis_index("hour").astype(jnp.int32)[None]
    own_zone = lax.axis_index("sens").astype(jnp.int32)[None]
    rows, patches = sky.shape
    kbins = sun_bins.shape[1]
    nbins, width = sun_coef.shape
    hours = rows * groups
    sensors = groups * width
    windows = area.shape[0]
    assert nbins % LANES == 0 or nbins % LANES >= 2 * kbins
    assert nbins <= 256 * LANES and width % LANES == 0 and windows % LANES == 0 and 3 * kbins <= HEAD
    assert groups == 4 and rows % 16 == 0
    shape = jax.ShapeDtypeStruct
    f32, bf16 = jnp.float32, jnp.bfloat16
    dma = lambda n: pltpu.SemaphoreType.DMA((n,))

    packed = call(
        pack_kernel,
        "pack",
        shape((HEAD, rows), bf16),
        in_specs=[SMEM, SMEM, HBM, HBM],
        scratch_shapes=[pltpu.VMEM((kbins, rows), jnp.int32), pltpu.VMEM((kbins, rows), bf16), dma(2)],
    )(me, own_zone, sun_bins.T, sun_rad.T)
    heads = {mask: exchange(packed, "hour", mask) for mask in (2, 1, 3)} | {0: packed}

    tiles = (windows // LANES, LANES)
    message = pl.cdiv(5 * zones, LANES) * LANES
    split = nbins // 2 // (CHUNK * LANES) * CHUNK * LANES + CHUNK * LANES
    assert split + 2 * CHUNK * LANES < nbins <= split + 3 * CHUNK * LANES
    coef, zone_sums, zone2, area2, openness2 = call(
        fetch_kernel(zones),
        "fetch",
        [shape((split, width), bf16), shape((1, message), f32)]
        + [shape(tiles, jnp.int32), shape(tiles, f32), shape(tiles, f32)],
        in_specs=[HBM] * 4,
        out_specs=[VMEM] * 5,
        scratch_shapes=[dma(4)],
    )(sun_coef, zone_of.reshape(tiles), area.reshape(tiles), openness.reshape(tiles))

    assert width // LANES <= TAIL

    def sun(masks, rest, stream):
        count = len(masks)
        late = [shape((nbins - split, width), bf16)] if stream else []
        scratch = [pltpu.VMEM((count * rows, width), f32)] + [pltpu.VMEM((count * rows, LANES), PATTERN)] * 2
        return call(
            sun_kernel(count, kbins, stream),
            "sun",
            [shape((width // LANES * rows + TAIL, LANES), jnp.int16)] * count + late,
            in_specs=[VMEM, HBM if stream else VMEM] + [VMEM] * count,
            out_specs=[VMEM] * (count + len(late)),
            scratch_shapes=scratch + ([dma(2)] if stream else []),
        )(coef, rest, *[heads[mask] for mask in masks])

    codes = [None] * groups
    codes[2], late = sun([2], sun_coef, True)
    codes[1], codes[3] = sun([1, 3], late, False)
    (codes[0],) = sun([0], late, False)
    codes = [exchange(code, "hour", mask) if mask else code for mask, code in enumerate(codes)]

    base, closed, wanted = call(
        base_kernel,
        "base",
        [shape((rows, sensors), f32)] * 2 + [shape((rows, sensors), bf16)],
        in_specs=[ANY] + [HBM] * 4,
        out_specs=[VMEM] * 3,
        scratch_shapes=[
            pltpu.VMEM((patches, rows), bf16),
            pltpu.VMEM((patches, sensors), bf16),
            pltpu.VMEM((patches, sensors), bf16),
            dma(4),
        ],
    )(codes[0], sky.T, sky_open, sky_closed, target)
    first, second = [2, 0], [1, 3]
    first_sums = call(
        first_kernel(first),
        "first",
        shape((2, 8, width), f32),
        in_specs=[SMEM] + [VMEM] * (3 + len(first)),
    )(me, base, closed, wanted, *[codes[mask] for mask in first])
    sent = call(
        second_kernel(second, zones),
        "second",
        shape((zones * groups, 1, message), f32),
        in_specs=[SMEM] * 2 + [VMEM] * (5 + len(second)),
    )(me, own_zone, base, closed, wanted, first_sums, zone_sums, *[codes[mask] for mask in second])
    heard = lax.all_to_all(sent, ("sens", "hour"), 0, 0)
    illuminance, new_openness = call(
        last_kernel(groups, zones, windows * zones),
        "last",
        [shape((rows, sensors), bf16), shape(tiles, f32)],
        in_specs=[SMEM] * 2 + [VMEM] * (6 + groups),
    )(me, own_zone, heard, zone2, area2, openness2, base, closed, *codes)
    return (illuminance, new_openness.reshape(-1))


def solution(mesh):
    in_specs = (
        P("hour", None),
        P(None, "sens"),
        P(None, "sens"),
        P(None, ("sens", "hour")),
        P("hour", None),
        P("hour", None),
        P("hour", "sens"),
        P("sens", None),
        P("sens"),
        P("sens"),
    )
    out_specs = (P("hour", "sens"), P("sens"))
    return jax.shard_map(local, mesh=mesh, in_specs=in_specs, out_specs=out_specs, check_vma=False)
```

```python
import jax
import jax.numpy as jnp
from jax import lax
from jax.experimental import pallas as pl
from jax.experimental.pallas import tpu as pltpu
from jax.sharding import PartitionSpec as P

LANES = 128
CHUNK = 8
HEAD = 16
TAIL = 8
PATTERN = jnp.bfloat16
LEVELS = 65000.0
VMEM_BYTES = 12 * 1024 * 1024
ANY = pl.BlockSpec(memory_space=pl.ANY)
HBM = pl.BlockSpec(memory_space=pltpu.HBM)
SMEM = pl.BlockSpec(memory_space=pltpu.SMEM)
VMEM = pl.BlockSpec(memory_space=pltpu.VMEM)


def call(kernel, name, out_shape, flops=0, moved=0, **more):
    run = pl.pallas_call(
        kernel,
        out_shape=out_shape,
        name=name,
        compiler_params=pltpu.CompilerParams(vmem_limit_bytes=VMEM_BYTES),
        cost_estimate=pl.CostEstimate(flops=flops, bytes_accessed=moved, transcendentals=0),
        **more,
    )
    specs = more["in_specs"]
    return lambda *args: run(
        *[pltpu.with_memory_space_constraint(x, pltpu.HBM) if s is HBM else x for x, s in zip(args, specs)]
    )


def exchange(x, axis, mask):
    return lax.ppermute(x, axis, [(i, i ^ mask) for i in range(lax.axis_size(axis))])


def fetch(pairs, sems):
    copies = [pltpu.make_async_copy(source, place, sems.at[i]) for i, (source, place) in enumerate(pairs)]
    for c in copies:
        c.start()
    return copies


def pack_kernel(me_ref, own_ref, bins_hbm, rad_hbm, out_ref, bins_ref, rad_ref, sems):
    for c in fetch([(bins_hbm, bins_ref), (rad_hbm, rad_ref)], sems):
        c.wait()
    bins = bins_ref[:]
    kbins = bins.shape[0]
    fill = jnp.zeros((HEAD - 3 * kbins, bins.shape[1]), jnp.float32)
    parts = [rad_ref[:].astype(jnp.float32), (bins // LANES).astype(jnp.float32), (bins % LANES).astype(jnp.float32)]
    out_ref[:] = jnp.concatenate(parts + [fill], axis=0).astype(jnp.bfloat16)


def fetch_kernel(zones):
    def kernel(coef_hbm, zone_hbm, area_hbm, openness_hbm, coef_ref, sums_ref, zone_ref, area_ref, openness_ref, sems):
        pairs = [(zone_hbm, zone_ref), (area_hbm, area_ref), (openness_hbm, openness_ref)]
        copies = fetch(pairs + [(coef_hbm.at[pl.ds(0, coef_ref.shape[0])], coef_ref)], sems)
        for c in copies[:3]:
            c.wait()
        zone, area = zone_ref[:], area_ref[:]
        lane = lax.broadcasted_iota(jnp.int32, sums_ref.shape, 1)
        values = [area * openness_ref[:], area, area * area]
        row = jnp.zeros(sums_ref.shape, jnp.float32)
        for z in range(zones):
            member = zone == z
            for k, value in enumerate(values):
                total = jnp.sum(jnp.where(member, value, 0.0), keepdims=True)
                row = jnp.where(lane == (2 + k) * zones + z, total, row)
        sums_ref[:] = row
        copies[3].wait()

    return kernel


def join_kernel(token, one_ref, two_ref, out_ref):
    out_ref[:HEAD] = one_ref[:]
    out_ref[HEAD:] = two_ref[:]


def sun_kernel(sources, kbins, stream):
    count = len(sources)
    inputs = 1 + max(operand for operand, _ in sources)

    def kernel(first_ref, rest_in, *refs):
        heads, outs, rest = refs[:inputs], refs[inputs : inputs + count], refs[inputs + count :]
        rows = heads[0].shape[1]
        split = first_ref.shape[0]
        nbins = split + rest_in.shape[0] - (split if stream else 0)
        step = CHUNK * LANES
        spans = [(first, min(first + step, nbins)) for first in range(0, nbins, step)]
        if stream:
            rest_ref, acc, pattern, block, sems = rest
            late = [span for span in spans if span[0] >= split]
            cuts = late[:-2] + [(late[-2][0], nbins)]
            copies = fetch(
                [
                    (rest_in.at[pl.ds(first, end - first)], rest_ref.at[pl.ds(first - split, end - first)])
                    for first, end in cuts
                ],
                sems,
            )
            waits = {first: c for (first, _), c in zip(cuts, copies)}
        else:
            rest_ref, (acc, pattern, block) = rest_in, rest
            waits = {}
        lane = lax.broadcasted_iota(jnp.int32, (rows, LANES), 1)
        for g in range(count):
            operand, offset = sources[g]
            small = heads[operand][offset : offset + HEAD].astype(jnp.float32).T
            value = jnp.zeros((rows, LANES), jnp.float32)
            where = jnp.zeros((rows, LANES), jnp.float32)
            for k in range(kbins):
                low = small[:, 2 * kbins + k : 2 * kbins + k + 1].astype(jnp.int32)
                hit = lane == low
                value = jnp.where(hit, small[:, k : k + 1], value)
                where = jnp.where(hit, small[:, kbins + k : kbins + k + 1], where)
            pattern[g * rows : (g + 1) * rows] = value.astype(pattern.dtype)
            block[g * rows : (g + 1) * rows] = where.astype(block.dtype)

        for first, end in spans:
            parts = []
            for c in range(first // LANES, pl.cdiv(end, LANES)):
                here = block[:] == jnp.asarray(c, block.dtype)
                parts.append(jnp.where(here, pattern[:], jnp.zeros_like(pattern)).astype(jnp.bfloat16))
            weights = jnp.concatenate(parts, axis=1) if len(parts) > 1 else parts[0]
            if first in waits:
                waits[first].wait()
            coef = first_ref[first:end] if first < split else rest_ref[first - split : end - split]
            part = jnp.dot(weights[:, : end - first], coef, preferred_element_type=jnp.float32)
            acc[:] = part if first == 0 else acc[:] + part

        for g in range(count):
            sun = acc[g * rows : (g + 1) * rows]
            power = jnp.ceil(jnp.log2(jnp.maximum(jnp.max(sun, axis=0, keepdims=True), 1e-30)))
            code = jnp.round(sun * (LEVELS / jnp.exp2(power)) - 0.5 * LEVELS)
            code = code.astype(jnp.int32).astype(jnp.int16)
            cuts = [slice(c, c + LANES) for c in range(0, code.shape[1], LANES)]
            for c, cut in enumerate(cuts):
                outs[g][c * rows : (c + 1) * rows] = code[:, cut]
            tail = [power[:, cut] for cut in cuts] + [jnp.zeros((TAIL - len(cuts), LANES), jnp.float32)]
            outs[g][len(cuts) * rows :] = jnp.concatenate(tail, axis=0).astype(jnp.int32).astype(jnp.int16)

    return kernel


def base_kernel(
    token, sky_hbm, open_hbm, closed_hbm, target_hbm, cross_ref, closed_out, target_out, sky_ref, open_ref, closed_ref, sems
):
    pairs = [(sky_hbm, sky_ref), (open_hbm, open_ref), (closed_hbm, closed_ref), (target_hbm, target_out)]
    copies = fetch(pairs, sems)
    for c in copies[:3]:
        c.wait()
    over = (((0,), (0,)), ((), ()))
    closed = lax.dot_general(sky_ref[:], closed_ref[:], over, preferred_element_type=jnp.float32)
    opened = lax.dot_general(sky_ref[:], open_ref[:], over, preferred_element_type=jnp.float32)
    closed_out[:] = closed
    cross_ref[:] = opened - closed
    copies[3].wait()


def place(me_ref, mask, width):
    return pl.ds(pl.multiple_of((me_ref[0] ^ mask) * width, LANES), width)


def cross_of(codes, base):
    rows, width = base.shape
    columns = width // LANES
    scales = jnp.exp2(codes[columns * rows :].astype(jnp.int32).astype(jnp.float32)) / LEVELS
    suns = []
    for c in range(columns):
        code = codes[c * rows : (c + 1) * rows].astype(jnp.int32).astype(jnp.float32)
        suns.append((code + 0.5 * LEVELS) * scales[c : c + 1])
    return base + jnp.concatenate(suns, axis=1)


def grad_terms(me_ref, base_ref, closed_ref, target_ref, codes, masks, linear, square):
    rows, width = base_ref.shape[0], linear.shape[1]
    for mask, code in zip(masks, codes):
        at = place(me_ref, mask, width)
        cross = cross_of(code, base_ref[:, at])
        apart = closed_ref[:, at] - target_ref[:, at].astype(jnp.float32)
        linear = linear + jnp.sum((apart * cross).reshape(rows // 8, 8, width), axis=0)
        square = square + jnp.sum((cross * cross).reshape(rows // 8, 8, width), axis=0)
    return linear, square


def first_kernel(masks):
    def kernel(me_ref, base_ref, closed_ref, target_ref, *refs):
        codes, out_ref = refs[:-1], refs[-1]
        zero = jnp.zeros(out_ref.shape[1:], jnp.float32)
        out_ref[0], out_ref[1] = grad_terms(me_ref, base_ref, closed_ref, target_ref, codes, masks, zero, zero)

    return kernel


def second_kernel(masks, zones):
    def kernel(me_ref, own_ref, base_ref, closed_ref, target_ref, first_ref, sums_ref, *refs):
        codes, out_ref = refs[:-1], refs[-1]
        linear, square = grad_terms(
            me_ref, base_ref, closed_ref, target_ref, codes, masks, first_ref[0], first_ref[1]
        )
        lane = lax.broadcasted_iota(jnp.int32, sums_ref.shape, 1)
        row = jnp.where(lane == own_ref[0], 2.0 * jnp.sum(linear, keepdims=True), sums_ref[:])
        row = jnp.where(lane == own_ref[0] + zones, 2.0 * jnp.sum(square, keepdims=True), row)
        out_ref[:] = jnp.broadcast_to(row[None], out_ref.shape)

    return kernel


def last_kernel(groups, zones, windows):
    def kernel(place_ref, own_ref, heard_ref, zone_ref, area_ref, openness_ref, base_ref, closed_ref, *refs):
        codes, (lit_ref, step_ref) = refs[:groups], refs[groups:]
        total = jnp.sum(heard_ref[:], axis=0)
        linear, quadratic, num, den, squares = [total[:, i * zones : (i + 1) * zones] for i in range(5)]
        share = num / den
        lane = lax.broadcasted_iota(jnp.int32, share.shape, 1)
        own_share = jnp.sum(jnp.where(lane == own_ref[0], share, 0.0), keepdims=True)
        width = closed_ref.shape[1] // groups
        for mask in range(groups):
            at = place(place_ref, mask, width)
            lit = closed_ref[:, at] + own_share * cross_of(codes[mask], base_ref[:, at])
            lit_ref[:, at] = lit.astype(jnp.bfloat16)
        ratio = groups * (linear + share * quadratic) / den
        rms = jnp.sqrt(jnp.sum(ratio * ratio * squares, keepdims=True) / (windows * groups) + 1e-06)
        zone = zone_ref[:]
        chosen = jnp.zeros(zone.shape, jnp.float32)
        for z in range(zones):
            chosen = jnp.where(zone == z, ratio[:, z : z + 1], chosen)
        step_ref[:] = jnp.clip(openness_ref[:] - 0.25 * (area_ref[:] * chosen) / rms, 0.0, 1.0)

    return kernel


def local(sky, sky_open, sky_closed, sun_coef, sun_bins, sun_rad, target, zone_of, area, openness):
    zones = lax.axis_size("sens")
    groups = lax.axis_size("hour")
    me = lax.axis_index("hour").astype(jnp.int32)[None]
    own_zone = lax.axis_index("sens").astype(jnp.int32)[None]
    rows, patches = sky.shape
    kbins = sun_bins.shape[1]
    nbins, width = sun_coef.shape
    hours = rows * groups
    sensors = groups * width
    windows = area.shape[0]
    assert nbins % LANES == 0 or nbins % LANES >= 2 * kbins
    assert nbins <= 256 * LANES and width % LANES == 0 and windows % LANES == 0 and 3 * kbins <= HEAD
    assert groups == 4 and rows % 16 == 0
    shape = jax.ShapeDtypeStruct
    f32, bf16 = jnp.float32, jnp.bfloat16
    dma = lambda n: pltpu.SemaphoreType.DMA((n,))

    packed = call(
        pack_kernel,
        "pack",
        shape((HEAD, rows), bf16),
        in_specs=[SMEM, SMEM, HBM, HBM],
        scratch_shapes=[pltpu.VMEM((kbins, rows), jnp.int32), pltpu.VMEM((kbins, rows), bf16), dma(2)],
    )(me, own_zone, sun_bins.T, sun_rad.T)
    far = exchange(packed, "hour", 2)

    tiles = (windows // LANES, LANES)
    message = pl.cdiv(5 * zones, LANES) * LANES
    split = (nbins // (CHUNK * LANES) - 1) * CHUNK * LANES
    assert 0 < split and split + CHUNK * LANES < nbins
    coef, zone_sums, zone2, area2, openness2 = call(
        fetch_kernel(zones),
        "fetch",
        [shape((split, width), bf16), shape((1, message), f32)]
        + [shape(tiles, jnp.int32), shape(tiles, f32), shape(tiles, f32)],
        in_specs=[HBM] * 4,
        out_specs=[VMEM] * 5,
        scratch_shapes=[dma(4)],
    )(sun_coef, zone_of.reshape(tiles), area.reshape(tiles), openness.reshape(tiles))

    both = call(join_kernel, "join", shape((2 * HEAD, rows), bf16), in_specs=[ANY] + [VMEM] * 2)(zone_sums, packed, far)
    near = exchange(both, "hour", 1)

    assert width // LANES <= TAIL

    def sun(sources, rest, stream, *heads):
        count = len(sources)
        late = [shape((nbins - split, width), bf16)] if stream else []
        scratch = [pltpu.VMEM((count * rows, width), f32)] + [pltpu.VMEM((count * rows, LANES), PATTERN)] * 2
        return call(
            sun_kernel(sources, kbins, stream),
            "sun",
            [shape((width // LANES * rows + TAIL, LANES), jnp.int16)] * count + late,
            in_specs=[VMEM, HBM if stream else VMEM] + [VMEM] * len(heads),
            out_specs=[VMEM] * (count + len(late)),
            scratch_shapes=scratch + ([dma(1)] if stream else []),
        )(coef, rest, *heads)

    codes = [None] * groups
    codes[2], late = sun([(0, 0)], sun_coef, True, far)
    codes[1], codes[3] = sun([(0, 0), (0, HEAD)], late, False, near)
    (codes[0],) = sun([(0, 0)], late, False, packed)
    codes = [exchange(code, "hour", mask) if mask else code for mask, code in enumerate(codes)]

    base, closed, wanted = call(
        base_kernel,
        "base",
        [shape((rows, sensors), f32)] * 2 + [shape((rows, sensors), bf16)],
        in_specs=[ANY] + [HBM] * 4,
        out_specs=[VMEM] * 3,
        scratch_shapes=[
            pltpu.VMEM((patches, rows), bf16),
            pltpu.VMEM((patches, sensors), bf16),
            pltpu.VMEM((patches, sensors), bf16),
            dma(4),
        ],
    )(codes[0], sky.T, sky_open, sky_closed, target)
    first, second = [2, 0], [1, 3]
    first_sums = call(
        first_kernel(first),
        "first",
        shape((2, 8, width), f32),
        in_specs=[SMEM] + [VMEM] * (3 + len(first)),
    )(me, base, closed, wanted, *[codes[mask] for mask in first])
    sent = call(
        second_kernel(second, zones),
        "second",
        shape((zones * groups, 1, message), f32),
        in_specs=[SMEM] * 2 + [VMEM] * (5 + len(second)),
    )(me, own_zone, base, closed, wanted, first_sums, zone_sums, *[codes[mask] for mask in second])
    heard = lax.all_to_all(sent, ("sens", "hour"), 0, 0)
    illuminance, new_openness = call(
        last_kernel(groups, zones, windows * zones),
        "last",
        [shape((rows, sensors), bf16), shape(tiles, f32)],
        in_specs=[SMEM] * 2 + [VMEM] * (6 + groups),
    )(me, own_zone, heard, zone2, area2, openness2, base, closed, *codes)
    return (illuminance, new_openness.reshape(-1))


def solution(mesh):
    in_specs = (
        P("hour", None),
        P(None, "sens"),
        P(None, "sens"),
        P(None, ("sens", "hour")),
        P("hour", None),
        P("hour", None),
        P("hour", "sens"),
        P("sens", None),
        P("sens"),
        P("sens"),
    )
    out_specs = (P("hour", "sens"), P("sens"))
    return jax.shard_map(local, mesh=mesh, in_specs=in_specs, out_specs=out_specs, check_vma=False)
```

```python
import jax
import jax.numpy as jnp
from jax import lax
from jax.experimental import pallas as pl
from jax.experimental.pallas import tpu as pltpu
from jax.sharding import PartitionSpec as P

LANES = 128
CHUNK = 8
HEAD = 16
TAIL = 8
PATTERN = jnp.bfloat16
LEVELS = 65000.0
VMEM_BYTES = 12 * 1024 * 1024
ANY = pl.BlockSpec(memory_space=pl.ANY)
HBM = pl.BlockSpec(memory_space=pltpu.HBM)
SMEM = pl.BlockSpec(memory_space=pltpu.SMEM)
VMEM = pl.BlockSpec(memory_space=pltpu.VMEM)


def call(kernel, name, out_shape, flops=0, moved=0, **more):
    run = pl.pallas_call(
        kernel,
        out_shape=out_shape,
        name=name,
        compiler_params=pltpu.CompilerParams(vmem_limit_bytes=VMEM_BYTES),
        cost_estimate=pl.CostEstimate(flops=flops, bytes_accessed=moved, transcendentals=0),
        **more,
    )
    specs = more["in_specs"]
    return lambda *args: run(
        *[pltpu.with_memory_space_constraint(x, pltpu.HBM) if s is HBM else x for x, s in zip(args, specs)]
    )


def exchange(x, axis, mask):
    return lax.ppermute(x, axis, [(i, i ^ mask) for i in range(lax.axis_size(axis))])


def fetch(pairs, sems):
    copies = [pltpu.make_async_copy(source, place, sems.at[i]) for i, (source, place) in enumerate(pairs)]
    for c in copies:
        c.start()
    return copies


def pack_kernel(me_ref, own_ref, bins_hbm, rad_hbm, out_ref, bins_ref, rad_ref, sems):
    for c in fetch([(bins_hbm, bins_ref), (rad_hbm, rad_ref)], sems):
        c.wait()
    bins = bins_ref[:]
    kbins = bins.shape[0]
    fill = jnp.zeros((HEAD - 3 * kbins, bins.shape[1]), jnp.float32)
    parts = [rad_ref[:].astype(jnp.float32), (bins // LANES).astype(jnp.float32), (bins % LANES).astype(jnp.float32)]
    out_ref[:] = jnp.concatenate(parts + [fill], axis=0).astype(jnp.bfloat16)


def fetch_kernel(zones):
    def kernel(coef_hbm, zone_hbm, area_hbm, openness_hbm, coef_ref, sums_ref, zone_ref, area_ref, openness_ref, sems):
        pairs = [(zone_hbm, zone_ref), (area_hbm, area_ref), (openness_hbm, openness_ref)]
        copies = fetch(pairs + [(coef_hbm.at[pl.ds(0, coef_ref.shape[0])], coef_ref)], sems)
        for c in copies[:3]:
            c.wait()
        zone, area = zone_ref[:], area_ref[:]
        lane = lax.broadcasted_iota(jnp.int32, sums_ref.shape, 1)
        values = [area * openness_ref[:], area, area * area]
        row = jnp.zeros(sums_ref.shape, jnp.float32)
        for z in range(zones):
            member = zone == z
            for k, value in enumerate(values):
                total = jnp.sum(jnp.where(member, value, 0.0), keepdims=True)
                row = jnp.where(lane == (2 + k) * zones + z, total, row)
        sums_ref[:] = row
        copies[3].wait()

    return kernel


def join_kernel(token, one_ref, two_ref, out_ref):
    out_ref[:HEAD] = one_ref[:]
    out_ref[HEAD:] = two_ref[:]


def sun_kernel(sources, kbins, stream):
    count = len(sources)
    inputs = 1 + max(operand for operand, _ in sources)

    def kernel(first_ref, rest_in, *refs):
        heads, outs, rest = refs[:inputs], refs[inputs : inputs + count], refs[inputs + count :]
        rows = heads[0].shape[1]
        split = first_ref.shape[0]
        nbins = split + rest_in.shape[0] - (split if stream else 0)
        step = CHUNK * LANES
        spans = [(first, min(first + step, nbins)) for first in range(0, nbins, step)]
        if stream:
            rest_ref, acc, pattern, block, sems = rest
            late = [span for span in spans if span[0] >= split]
            cuts = late[:-2] + [(late[-2][0], nbins)]
            copies = fetch(
                [
                    (rest_in.at[pl.ds(first, end - first)], rest_ref.at[pl.ds(first - split, end - first)])
                    for first, end in cuts
                ],
                sems,
            )
            waits = {first: c for (first, _), c in zip(cuts, copies)}
        else:
            rest_ref, (acc, pattern, block) = rest_in, rest
            waits = {}
        lane = lax.broadcasted_iota(jnp.int32, (rows, LANES), 1)
        for g in range(count):
            operand, offset = sources[g]
            small = heads[operand][offset : offset + HEAD].astype(jnp.float32).T
            value = jnp.zeros((rows, LANES), jnp.float32)
            where = jnp.zeros((rows, LANES), jnp.float32)
            for k in range(kbins):
                low = small[:, 2 * kbins + k : 2 * kbins + k + 1].astype(jnp.int32)
                hit = lane == low
                value = jnp.where(hit, small[:, k : k + 1], value)
                where = jnp.where(hit, small[:, kbins + k : kbins + k + 1], where)
            pattern[g * rows : (g + 1) * rows] = value.astype(pattern.dtype)
            block[g * rows : (g + 1) * rows] = where.astype(block.dtype)

        for first, end in spans:
            parts = []
            for c in range(first // LANES, pl.cdiv(end, LANES)):
                here = block[:] == jnp.asarray(c, block.dtype)
                parts.append(jnp.where(here, pattern[:], jnp.zeros_like(pattern)).astype(jnp.bfloat16))
            weights = jnp.concatenate(parts, axis=1) if len(parts) > 1 else parts[0]
            if first in waits:
                waits[first].wait()
            coef = first_ref[first:end] if first < split else rest_ref[first - split : end - split]
            part = jnp.dot(weights[:, : end - first], coef, preferred_element_type=jnp.float32)
            acc[:] = part if first == 0 else acc[:] + part

        for g in range(count):
            sun = acc[g * rows : (g + 1) * rows]
            power = jnp.ceil(jnp.log2(jnp.maximum(jnp.max(sun, axis=0, keepdims=True), 1e-30)))
            code = jnp.round(sun * (LEVELS / jnp.exp2(power)) - 0.5 * LEVELS)
            code = code.astype(jnp.int32).astype(jnp.int16)
            cuts = [slice(c, c + LANES) for c in range(0, code.shape[1], LANES)]
            for c, cut in enumerate(cuts):
                outs[g][c * rows : (c + 1) * rows] = code[:, cut]
            tail = [power[:, cut] for cut in cuts] + [jnp.zeros((TAIL - len(cuts), LANES), jnp.float32)]
            outs[g][len(cuts) * rows :] = jnp.concatenate(tail, axis=0).astype(jnp.int32).astype(jnp.int16)

    return kernel


def base_kernel(
    token, sky_hbm, open_hbm, closed_hbm, target_hbm, cross_ref, closed_out, target_out, sky_ref, open_ref, closed_ref, sems
):
    pairs = [(sky_hbm, sky_ref), (open_hbm, open_ref), (closed_hbm, closed_ref), (target_hbm, target_out)]
    copies = fetch(pairs, sems)
    for c in copies[:3]:
        c.wait()
    over = (((0,), (0,)), ((), ()))
    closed = lax.dot_general(sky_ref[:], closed_ref[:], over, preferred_element_type=jnp.float32)
    opened = lax.dot_general(sky_ref[:], open_ref[:], over, preferred_element_type=jnp.float32)
    closed_out[:] = closed
    cross_ref[:] = opened - closed
    copies[3].wait()


def place(me_ref, mask, width):
    return pl.ds(pl.multiple_of((me_ref[0] ^ mask) * width, LANES), width)


def cross_of(codes, base):
    rows, width = base.shape
    columns = width // LANES
    scales = jnp.exp2(codes[columns * rows :].astype(jnp.int32).astype(jnp.float32)) / LEVELS
    suns = []
    for c in range(columns):
        code = codes[c * rows : (c + 1) * rows].astype(jnp.int32).astype(jnp.float32)
        suns.append((code + 0.5 * LEVELS) * scales[c : c + 1])
    return base + jnp.concatenate(suns, axis=1)


def grad_terms(me_ref, base_ref, closed_ref, target_ref, codes, masks, linear, square):
    rows, width = base_ref.shape[0], linear.shape[1]
    for mask, code in zip(masks, codes):
        at = place(me_ref, mask, width)
        cross = cross_of(code, base_ref[:, at])
        apart = closed_ref[:, at] - target_ref[:, at].astype(jnp.float32)
        linear = linear + jnp.sum((apart * cross).reshape(rows // 8, 8, width), axis=0)
        square = square + jnp.sum((cross * cross).reshape(rows // 8, 8, width), axis=0)
    return linear, square


def first_kernel(masks):
    def kernel(me_ref, base_ref, closed_ref, target_ref, *refs):
        codes, out_ref = refs[:-1], refs[-1]
        zero = jnp.zeros(out_ref.shape[1:], jnp.float32)
        out_ref[0], out_ref[1] = grad_terms(me_ref, base_ref, closed_ref, target_ref, codes, masks, zero, zero)

    return kernel


def second_kernel(masks, zones):
    def kernel(me_ref, own_ref, base_ref, closed_ref, target_ref, first_ref, sums_ref, *refs):
        codes, out_ref = refs[:-1], refs[-1]
        linear, square = grad_terms(
            me_ref, base_ref, closed_ref, target_ref, codes, masks, first_ref[0], first_ref[1]
        )
        lane = lax.broadcasted_iota(jnp.int32, sums_ref.shape, 1)
        row = jnp.where(lane == own_ref[0], 2.0 * jnp.sum(linear, keepdims=True), sums_ref[:])
        row = jnp.where(lane == own_ref[0] + zones, 2.0 * jnp.sum(square, keepdims=True), row)
        out_ref[:] = row

    return kernel


def last_kernel(groups, zones, windows):
    def kernel(place_ref, own_ref, heard_ref, zone_ref, area_ref, openness_ref, base_ref, closed_ref, *refs):
        codes, (lit_ref, step_ref) = refs[:groups], refs[groups:]
        total = jnp.sum(heard_ref[:], axis=0, keepdims=True)
        linear, quadratic, num, den, squares = [total[:, i * zones : (i + 1) * zones] for i in range(5)]
        share = num / den
        lane = lax.broadcasted_iota(jnp.int32, share.shape, 1)
        own_share = jnp.sum(jnp.where(lane == own_ref[0], share, 0.0), keepdims=True)
        width = closed_ref.shape[1] // groups
        for mask in range(groups):
            at = place(place_ref, mask, width)
            lit = closed_ref[:, at] + own_share * cross_of(codes[mask], base_ref[:, at])
            lit_ref[:, at] = lit.astype(jnp.bfloat16)
        ratio = groups * (linear + share * quadratic) / den
        rms = jnp.sqrt(jnp.sum(ratio * ratio * squares, keepdims=True) / (windows * groups) + 1e-06)
        zone = zone_ref[:]
        chosen = jnp.zeros(zone.shape, jnp.float32)
        for z in range(zones):
            chosen = jnp.where(zone == z, ratio[:, z : z + 1], chosen)
        step_ref[:] = jnp.clip(openness_ref[:] - 0.25 * (area_ref[:] * chosen) / rms, 0.0, 1.0)

    return kernel


def local(sky, sky_open, sky_closed, sun_coef, sun_bins, sun_rad, target, zone_of, area, openness):
    zones = lax.axis_size("sens")
    groups = lax.axis_size("hour")
    me = lax.axis_index("hour").astype(jnp.int32)[None]
    own_zone = lax.axis_index("sens").astype(jnp.int32)[None]
    rows, patches = sky.shape
    kbins = sun_bins.shape[1]
    nbins, width = sun_coef.shape
    hours = rows * groups
    sensors = groups * width
    windows = area.shape[0]
    assert nbins % LANES == 0 or nbins % LANES >= 2 * kbins
    assert nbins <= 256 * LANES and width % LANES == 0 and windows % LANES == 0 and 3 * kbins <= HEAD
    assert groups == 4 and rows % 16 == 0
    shape = jax.ShapeDtypeStruct
    f32, bf16 = jnp.float32, jnp.bfloat16
    dma = lambda n: pltpu.SemaphoreType.DMA((n,))

    packed = call(
        pack_kernel,
        "pack",
        shape((HEAD, rows), bf16),
        in_specs=[SMEM, SMEM, HBM, HBM],
        scratch_shapes=[pltpu.VMEM((kbins, rows), jnp.int32), pltpu.VMEM((kbins, rows), bf16), dma(2)],
    )(me, own_zone, sun_bins.T, sun_rad.T)
    far = exchange(packed, "hour", 2)

    tiles = (windows // LANES, LANES)
    message = pl.cdiv(5 * zones, LANES) * LANES
    split = (nbins // (CHUNK * LANES) - 1) * CHUNK * LANES
    assert 0 < split and split + CHUNK * LANES < nbins
    coef, zone_sums, zone2, area2, openness2 = call(
        fetch_kernel(zones),
        "fetch",
        [shape((split, width), bf16), shape((1, message), f32)]
        + [shape(tiles, jnp.int32), shape(tiles, f32), shape(tiles, f32)],
        in_specs=[HBM] * 4,
        out_specs=[VMEM] * 5,
        scratch_shapes=[dma(4)],
    )(sun_coef, zone_of.reshape(tiles), area.reshape(tiles), openness.reshape(tiles))

    both = call(join_kernel, "join", shape((2 * HEAD, rows), bf16), in_specs=[ANY] + [VMEM] * 2)(zone_sums, packed, far)
    near = exchange(both, "hour", 1)

    assert width // LANES <= TAIL

    def sun(sources, rest, stream, *heads):
        count = len(sources)
        late = [shape((nbins - split, width), bf16)] if stream else []
        scratch = [pltpu.VMEM((count * rows, width), f32)] + [pltpu.VMEM((count * rows, LANES), PATTERN)] * 2
        return call(
            sun_kernel(sources, kbins, stream),
            "sun",
            [shape((width // LANES * rows + TAIL, LANES), jnp.int16)] * count + late,
            in_specs=[VMEM, HBM if stream else VMEM] + [VMEM] * len(heads),
            out_specs=[VMEM] * (count + len(late)),
            scratch_shapes=scratch + ([dma(1)] if stream else []),
        )(coef, rest, *heads)

    codes = [None] * groups
    codes[2], late = sun([(0, 0)], sun_coef, True, far)
    codes[1], codes[3] = sun([(0, 0), (0, HEAD)], late, False, near)
    (codes[0],) = sun([(0, 0)], late, False, packed)
    codes = [exchange(code, "hour", mask) if mask else code for mask, code in enumerate(codes)]

    base, closed, wanted = call(
        base_kernel,
        "base",
        [shape((rows, sensors), f32)] * 2 + [shape((rows, sensors), bf16)],
        in_specs=[ANY] + [HBM] * 4,
        out_specs=[VMEM] * 3,
        scratch_shapes=[
            pltpu.VMEM((patches, rows), bf16),
            pltpu.VMEM((patches, sensors), bf16),
            pltpu.VMEM((patches, sensors), bf16),
            dma(4),
        ],
    )(codes[0], sky.T, sky_open, sky_closed, target)
    first, second = [2, 0], [1, 3]
    first_sums = call(
        first_kernel(first),
        "first",
        shape((2, 8, width), f32),
        in_specs=[SMEM] + [VMEM] * (3 + len(first)),
    )(me, base, closed, wanted, *[codes[mask] for mask in first])
    sent = call(
        second_kernel(second, zones),
        "second",
        shape((1, message), f32),
        in_specs=[SMEM] * 2 + [VMEM] * (5 + len(second)),
    )(me, own_zone, base, closed, wanted, first_sums, zone_sums, *[codes[mask] for mask in second])
    heard = lax.all_gather(sent, ("sens", "hour"), axis=0, tiled=True)
    illuminance, new_openness = call(
        last_kernel(groups, zones, windows * zones),
        "last",
        [shape((rows, sensors), bf16), shape(tiles, f32)],
        in_specs=[SMEM] * 2 + [VMEM] * (6 + groups),
    )(me, own_zone, heard, zone2, area2, openness2, base, closed, *codes)
    return (illuminance, new_openness.reshape(-1))


def solution(mesh):
    in_specs = (
        P("hour", None),
        P(None, "sens"),
        P(None, "sens"),
        P(None, ("sens", "hour")),
        P("hour", None),
        P("hour", None),
        P("hour", "sens"),
        P("sens", None),
        P("sens"),
        P("sens"),
    )
    out_specs = (P("hour", "sens"), P("sens"))
    return jax.shard_map(local, mesh=mesh, in_specs=in_specs, out_specs=out_specs, check_vma=False)
```

```python
import jax
import jax.numpy as jnp
from jax import lax
from jax.experimental import pallas as pl
from jax.experimental.pallas import tpu as pltpu
from jax.sharding import PartitionSpec as P

LANES = 128
CHUNK = 8
HEAD = 16
TAIL = 8
PATTERN = jnp.bfloat16
LEVELS = 65000.0
VMEM_BYTES = 12 * 1024 * 1024
ANY = pl.BlockSpec(memory_space=pl.ANY)
HBM = pl.BlockSpec(memory_space=pltpu.HBM)
SMEM = pl.BlockSpec(memory_space=pltpu.SMEM)
VMEM = pl.BlockSpec(memory_space=pltpu.VMEM)


def call(kernel, name, out_shape, flops=0, moved=0, **more):
    run = pl.pallas_call(
        kernel,
        out_shape=out_shape,
        name=name,
        compiler_params=pltpu.CompilerParams(vmem_limit_bytes=VMEM_BYTES),
        cost_estimate=pl.CostEstimate(flops=flops, bytes_accessed=moved, transcendentals=0),
        **more,
    )
    specs = more["in_specs"]
    return lambda *args: run(
        *[pltpu.with_memory_space_constraint(x, pltpu.HBM) if s is HBM else x for x, s in zip(args, specs)]
    )


def exchange(x, axis, mask):
    return lax.ppermute(x, axis, [(i, i ^ mask) for i in range(lax.axis_size(axis))])


def fetch(pairs, sems):
    copies = [pltpu.make_async_copy(source, place, sems.at[i]) for i, (source, place) in enumerate(pairs)]
    for c in copies:
        c.start()
    return copies


def pack_kernel(me_ref, own_ref, bins_hbm, rad_hbm, out_ref, bins_ref, rad_ref, sems):
    for c in fetch([(bins_hbm, bins_ref), (rad_hbm, rad_ref)], sems):
        c.wait()
    bins = bins_ref[:]
    kbins = bins.shape[0]
    fill = jnp.zeros((HEAD - 3 * kbins, bins.shape[1]), jnp.float32)
    parts = [rad_ref[:].astype(jnp.float32), (bins // LANES).astype(jnp.float32), (bins % LANES).astype(jnp.float32)]
    out_ref[:] = jnp.concatenate(parts + [fill], axis=0).astype(jnp.bfloat16)


def fetch_kernel(zones):
    def kernel(coef_hbm, zone_hbm, area_hbm, openness_hbm, coef_ref, sums_ref, zone_ref, area_ref, openness_ref, sems):
        pairs = [(zone_hbm, zone_ref), (area_hbm, area_ref), (openness_hbm, openness_ref)]
        copies = fetch(pairs + [(coef_hbm.at[pl.ds(0, coef_ref.shape[0])], coef_ref)], sems)
        for c in copies[:3]:
            c.wait()
        zone, area = zone_ref[:], area_ref[:]
        lane = lax.broadcasted_iota(jnp.int32, sums_ref.shape, 1)
        values = [area * openness_ref[:], area, area * area]
        row = jnp.zeros(sums_ref.shape, jnp.float32)
        for z in range(zones):
            member = zone == z
            for k, value in enumerate(values):
                total = jnp.sum(jnp.where(member, value, 0.0), keepdims=True)
                row = jnp.where(lane == (2 + k) * zones + z, total, row)
        sums_ref[:] = row
        copies[3].wait()

    return kernel


def join_kernel(token, one_ref, two_ref, out_ref):
    out_ref[:HEAD] = one_ref[:]
    out_ref[HEAD:] = two_ref[:]


def sun_kernel(sources, kbins, stream):
    count = len(sources)
    inputs = 1 + max(operand for operand, _ in sources)

    def kernel(first_ref, rest_in, *refs):
        heads, outs, rest = refs[:inputs], refs[inputs : inputs + count], refs[inputs + count :]
        rows = heads[0].shape[1]
        split = first_ref.shape[0]
        nbins = split + rest_in.shape[0] - (split if stream else 0)
        step = CHUNK * LANES
        spans = [(first, min(first + step, nbins)) for first in range(0, nbins, step)]
        if stream:
            rest_ref, acc, pattern, block, sems = rest
            late = [span for span in spans if span[0] >= split]
            cuts = late[:-2] + [(late[-2][0], nbins)]
            copies = fetch(
                [
                    (rest_in.at[pl.ds(first, end - first)], rest_ref.at[pl.ds(first - split, end - first)])
                    for first, end in cuts
                ],
                sems,
            )
            waits = {first: c for (first, _), c in zip(cuts, copies)}
        else:
            rest_ref, (acc, pattern, block) = rest_in, rest
            waits = {}
        lane = lax.broadcasted_iota(jnp.int32, (rows, LANES), 1)
        for g in range(count):
            operand, offset = sources[g]
            small = heads[operand][offset : offset + HEAD].astype(jnp.float32).T
            value = jnp.zeros((rows, LANES), jnp.float32)
            where = jnp.zeros((rows, LANES), jnp.float32)
            for k in range(kbins):
                low = small[:, 2 * kbins + k : 2 * kbins + k + 1].astype(jnp.int32)
                hit = lane == low
                value = jnp.where(hit, small[:, k : k + 1], value)
                where = jnp.where(hit, small[:, kbins + k : kbins + k + 1], where)
            pattern[g * rows : (g + 1) * rows] = value.astype(pattern.dtype)
            block[g * rows : (g + 1) * rows] = where.astype(block.dtype)

        for first, end in spans:
            parts = []
            for c in range(first // LANES, pl.cdiv(end, LANES)):
                here = block[:] == jnp.asarray(c, block.dtype)
                parts.append(jnp.where(here, pattern[:], jnp.zeros_like(pattern)).astype(jnp.bfloat16))
            weights = jnp.concatenate(parts, axis=1) if len(parts) > 1 else parts[0]
            if first in waits:
                waits[first].wait()
            coef = first_ref[first:end] if first < split else rest_ref[first - split : end - split]
            part = jnp.dot(weights[:, : end - first], coef, preferred_element_type=jnp.float32)
            acc[:] = part if first == 0 else acc[:] + part

        for g in range(count):
            sun = acc[g * rows : (g + 1) * rows]
            power = jnp.ceil(jnp.log2(jnp.maximum(jnp.max(sun, axis=0, keepdims=True), 1e-30)))
            code = jnp.round(sun * (LEVELS / jnp.exp2(power)) - 0.5 * LEVELS)
            code = code.astype(jnp.int32).astype(jnp.int16)
            cuts = [slice(c, c + LANES) for c in range(0, code.shape[1], LANES)]
            for c, cut in enumerate(cuts):
                outs[g][c * rows : (c + 1) * rows] = code[:, cut]
            tail = [power[:, cut] for cut in cuts] + [jnp.zeros((TAIL - len(cuts), LANES), jnp.float32)]
            outs[g][len(cuts) * rows :] = jnp.concatenate(tail, axis=0).astype(jnp.int32).astype(jnp.int16)

    return kernel


def base_kernel(
    token, sky_hbm, open_hbm, closed_hbm, target_hbm, cross_ref, closed_out, target_out, sky_ref, open_ref, closed_ref, sems
):
    pairs = [(sky_hbm, sky_ref), (open_hbm, open_ref), (closed_hbm, closed_ref), (target_hbm, target_out)]
    copies = fetch(pairs, sems)
    for c in copies[:3]:
        c.wait()
    over = (((0,), (0,)), ((), ()))
    closed = lax.dot_general(sky_ref[:], closed_ref[:], over, preferred_element_type=jnp.float32)
    opened = lax.dot_general(sky_ref[:], open_ref[:], over, preferred_element_type=jnp.float32)
    closed_out[:] = closed
    cross_ref[:] = opened - closed
    copies[3].wait()


def place(me_ref, mask, width):
    return pl.ds(pl.multiple_of((me_ref[0] ^ mask) * width, LANES), width)


def cross_of(codes, base):
    rows, width = base.shape
    columns = width // LANES
    scales = jnp.exp2(codes[columns * rows :].astype(jnp.int32).astype(jnp.float32)) / LEVELS
    suns = []
    for c in range(columns):
        code = codes[c * rows : (c + 1) * rows].astype(jnp.int32).astype(jnp.float32)
        suns.append((code + 0.5 * LEVELS) * scales[c : c + 1])
    return base + jnp.concatenate(suns, axis=1)


def grad_terms(me_ref, base_ref, closed_ref, target_ref, codes, crosses, masks, linear, square):
    rows, width = base_ref.shape[0], linear.shape[1]
    for mask, code, cross_ref in zip(masks, codes, crosses):
        at = place(me_ref, mask, width)
        cross = cross_of(code, base_ref[:, at])
        cross_ref[:] = cross
        apart = closed_ref[:, at] - target_ref[:, at].astype(jnp.float32)
        linear = linear + jnp.sum((apart * cross).reshape(rows // 8, 8, width), axis=0)
        square = square + jnp.sum((cross * cross).reshape(rows // 8, 8, width), axis=0)
    return linear, square


def first_kernel(masks):
    count = len(masks)

    def kernel(me_ref, base_ref, closed_ref, target_ref, *refs):
        codes, crosses, out_ref = refs[:count], refs[count : 2 * count], refs[-1]
        zero = jnp.zeros(out_ref.shape[1:], jnp.float32)
        out_ref[0], out_ref[1] = grad_terms(
            me_ref, base_ref, closed_ref, target_ref, codes, crosses, masks, zero, zero
        )

    return kernel


def second_kernel(masks, zones):
    count = len(masks)

    def kernel(me_ref, own_ref, base_ref, closed_ref, target_ref, first_ref, sums_ref, *refs):
        codes, crosses, out_ref = refs[:count], refs[count : 2 * count], refs[-1]
        linear, square = grad_terms(
            me_ref, base_ref, closed_ref, target_ref, codes, crosses, masks, first_ref[0], first_ref[1]
        )
        lane = lax.broadcasted_iota(jnp.int32, sums_ref.shape, 1)
        row = jnp.where(lane == own_ref[0], 2.0 * jnp.sum(linear, keepdims=True), sums_ref[:])
        row = jnp.where(lane == own_ref[0] + zones, 2.0 * jnp.sum(square, keepdims=True), row)
        out_ref[:] = jnp.broadcast_to(row[None], out_ref.shape)

    return kernel


def last_kernel(groups, zones, windows):
    def kernel(place_ref, own_ref, heard_ref, zone_ref, area_ref, openness_ref, closed_ref, *refs):
        crosses, (lit_ref, step_ref) = refs[:groups], refs[groups:]
        total = jnp.sum(heard_ref[:], axis=0)
        linear, quadratic, num, den, squares = [total[:, i * zones : (i + 1) * zones] for i in range(5)]
        share = num / den
        lane = lax.broadcasted_iota(jnp.int32, share.shape, 1)
        own_share = jnp.sum(jnp.where(lane == own_ref[0], share, 0.0), keepdims=True)
        width = closed_ref.shape[1] // groups
        for mask in range(groups):
            at = place(place_ref, mask, width)
            lit = closed_ref[:, at] + own_share * crosses[mask][:]
            lit_ref[:, at] = lit.astype(jnp.bfloat16)
        ratio = groups * (linear + share * quadratic) / den
        rms = jnp.sqrt(jnp.sum(ratio * ratio * squares, keepdims=True) / (windows * groups) + 1e-06)
        zone = zone_ref[:]
        chosen = jnp.zeros(zone.shape, jnp.float32)
        for z in range(zones):
            chosen = jnp.where(zone == z, ratio[:, z : z + 1], chosen)
        step_ref[:] = jnp.clip(openness_ref[:] - 0.25 * (area_ref[:] * chosen) / rms, 0.0, 1.0)

    return kernel


def local(sky, sky_open, sky_closed, sun_coef, sun_bins, sun_rad, target, zone_of, area, openness):
    zones = lax.axis_size("sens")
    groups = lax.axis_size("hour")
    me = lax.axis_index("hour").astype(jnp.int32)[None]
    own_zone = lax.axis_index("sens").astype(jnp.int32)[None]
    rows, patches = sky.shape
    kbins = sun_bins.shape[1]
    nbins, width = sun_coef.shape
    hours = rows * groups
    sensors = groups * width
    windows = area.shape[0]
    assert nbins % LANES == 0 or nbins % LANES >= 2 * kbins
    assert nbins <= 256 * LANES and width % LANES == 0 and windows % LANES == 0 and 3 * kbins <= HEAD
    assert groups == 4 and rows % 16 == 0
    shape = jax.ShapeDtypeStruct
    f32, bf16 = jnp.float32, jnp.bfloat16
    dma = lambda n: pltpu.SemaphoreType.DMA((n,))

    packed = call(
        pack_kernel,
        "pack",
        shape((HEAD, rows), bf16),
        in_specs=[SMEM, SMEM, HBM, HBM],
        scratch_shapes=[pltpu.VMEM((kbins, rows), jnp.int32), pltpu.VMEM((kbins, rows), bf16), dma(2)],
    )(me, own_zone, sun_bins.T, sun_rad.T)
    far = exchange(packed, "hour", 2)

    tiles = (windows // LANES, LANES)
    message = pl.cdiv(5 * zones, LANES) * LANES
    split = (nbins // (CHUNK * LANES) - 1) * CHUNK * LANES
    assert 0 < split and split + CHUNK * LANES < nbins
    coef, zone_sums, zone2, area2, openness2 = call(
        fetch_kernel(zones),
        "fetch",
        [shape((split, width), bf16), shape((1, message), f32)]
        + [shape(tiles, jnp.int32), shape(tiles, f32), shape(tiles, f32)],
        in_specs=[HBM] * 4,
        out_specs=[VMEM] * 5,
        scratch_shapes=[dma(4)],
    )(sun_coef, zone_of.reshape(tiles), area.reshape(tiles), openness.reshape(tiles))

    both = call(join_kernel, "join", shape((2 * HEAD, rows), bf16), in_specs=[ANY] + [VMEM] * 2)(zone_sums, packed, far)
    near = exchange(both, "hour", 1)

    assert width // LANES <= TAIL

    def sun(sources, rest, stream, *heads):
        count = len(sources)
        late = [shape((nbins - split, width), bf16)] if stream else []
        scratch = [pltpu.VMEM((count * rows, width), f32)] + [pltpu.VMEM((count * rows, LANES), PATTERN)] * 2
        return call(
            sun_kernel(sources, kbins, stream),
            "sun",
            [shape((width // LANES * rows + TAIL, LANES), jnp.int16)] * count + late,
            in_specs=[VMEM, HBM if stream else VMEM] + [VMEM] * len(heads),
            out_specs=[VMEM] * (count + len(late)),
            scratch_shapes=scratch + ([dma(1)] if stream else []),
        )(coef, rest, *heads)

    codes = [None] * groups
    codes[2], late = sun([(0, 0)], sun_coef, True, far)
    codes[1], codes[3] = sun([(0, 0), (0, HEAD)], late, False, near)
    (codes[0],) = sun([(0, 0)], late, False, packed)
    codes = [exchange(code, "hour", mask) if mask else code for mask, code in enumerate(codes)]

    base, closed, wanted = call(
        base_kernel,
        "base",
        [shape((rows, sensors), f32)] * 2 + [shape((rows, sensors), bf16)],
        in_specs=[ANY] + [HBM] * 4,
        out_specs=[VMEM] * 3,
        scratch_shapes=[
            pltpu.VMEM((patches, rows), bf16),
            pltpu.VMEM((patches, sensors), bf16),
            pltpu.VMEM((patches, sensors), bf16),
            dma(4),
        ],
    )(codes[0], sky.T, sky_open, sky_closed, target)
    first, second = [2, 0], [1, 3]
    block = shape((rows, width), f32)
    *first_crosses, first_sums = call(
        first_kernel(first),
        "first",
        [block] * len(first) + [shape((2, 8, width), f32)],
        in_specs=[SMEM] + [VMEM] * (3 + len(first)),
        out_specs=[VMEM] * (1 + len(first)),
    )(me, base, closed, wanted, *[codes[mask] for mask in first])
    *second_crosses, sent = call(
        second_kernel(second, zones),
        "second",
        [block] * len(second) + [shape((zones * groups, 1, message), f32)],
        in_specs=[SMEM] * 2 + [VMEM] * (5 + len(second)),
        out_specs=[VMEM] * (1 + len(second)),
    )(me, own_zone, base, closed, wanted, first_sums, zone_sums, *[codes[mask] for mask in second])
    crosses = dict(zip(first + second, first_crosses + second_crosses))
    heard = lax.all_to_all(sent, ("hour", "sens"), 0, 0)
    illuminance, new_openness = call(
        last_kernel(groups, zones, windows * zones),
        "last",
        [shape((rows, sensors), bf16), shape(tiles, f32)],
        in_specs=[SMEM] * 2 + [VMEM] * (5 + groups),
    )(me, own_zone, heard, zone2, area2, openness2, closed, *[crosses[mask] for mask in range(groups)])
    return (illuminance, new_openness.reshape(-1))


def solution(mesh):
    in_specs = (
        P("hour", None),
        P(None, "sens"),
        P(None, "sens"),
        P(None, ("sens", "hour")),
        P("hour", None),
        P("hour", None),
        P("hour", "sens"),
        P("sens", None),
        P("sens"),
        P("sens"),
    )
    out_specs = (P("hour", "sens"), P("sens"))
    return jax.shard_map(local, mesh=mesh, in_specs=in_specs, out_specs=out_specs, check_vma=False)
```

```python
import jax
import jax.numpy as jnp
from jax import lax
from jax.experimental import pallas as pl
from jax.experimental.pallas import tpu as pltpu
from jax.sharding import PartitionSpec as P

LANES = 128
CHUNK = 8
HEAD = 16
TAIL = 8
PATTERN = jnp.bfloat16
LEVELS = 65000.0
VMEM_BYTES = 12 * 1024 * 1024
ANY = pl.BlockSpec(memory_space=pl.ANY)
HBM = pl.BlockSpec(memory_space=pltpu.HBM)
SMEM = pl.BlockSpec(memory_space=pltpu.SMEM)
VMEM = pl.BlockSpec(memory_space=pltpu.VMEM)


def call(kernel, name, out_shape, flops=0, moved=0, **more):
    run = pl.pallas_call(
        kernel,
        out_shape=out_shape,
        name=name,
        compiler_params=pltpu.CompilerParams(vmem_limit_bytes=VMEM_BYTES),
        cost_estimate=pl.CostEstimate(flops=flops, bytes_accessed=moved, transcendentals=0),
        **more,
    )
    specs = more["in_specs"]
    return lambda *args: run(
        *[pltpu.with_memory_space_constraint(x, pltpu.HBM) if s is HBM else x for x, s in zip(args, specs)]
    )


def exchange(x, axis, mask):
    return lax.ppermute(x, axis, [(i, i ^ mask) for i in range(lax.axis_size(axis))])


def fetch(pairs, sems):
    copies = [pltpu.make_async_copy(source, place, sems.at[i]) for i, (source, place) in enumerate(pairs)]
    for c in copies:
        c.start()
    return copies


def pack_kernel(me_ref, own_ref, bins_hbm, rad_hbm, out_ref, bins_ref, rad_ref, sems):
    for c in fetch([(bins_hbm, bins_ref), (rad_hbm, rad_ref)], sems):
        c.wait()
    bins = bins_ref[:]
    kbins = bins.shape[0]
    fill = jnp.zeros((HEAD - 3 * kbins, bins.shape[1]), jnp.float32)
    parts = [rad_ref[:].astype(jnp.float32), (bins // LANES).astype(jnp.float32), (bins % LANES).astype(jnp.float32)]
    out_ref[:] = jnp.concatenate(parts + [fill], axis=0).astype(jnp.bfloat16)


def fetch_kernel(zones):
    def kernel(coef_hbm, zone_hbm, area_hbm, openness_hbm, coef_ref, sums_ref, zone_ref, area_ref, openness_ref, sems):
        pairs = [(zone_hbm, zone_ref), (area_hbm, area_ref), (openness_hbm, openness_ref)]
        copies = fetch(pairs + [(coef_hbm, coef_ref)], sems)
        for c in copies[:3]:
            c.wait()
        zone, area = zone_ref[:], area_ref[:]
        lane = lax.broadcasted_iota(jnp.int32, sums_ref.shape, 1)
        values = [area * openness_ref[:], area, area * area]
        row = jnp.zeros(sums_ref.shape, jnp.float32)
        for z in range(zones):
            member = zone == z
            for k, value in enumerate(values):
                total = jnp.sum(jnp.where(member, value, 0.0), keepdims=True)
                row = jnp.where(lane == (2 + k) * zones + z, total, row)
        sums_ref[:] = row
        copies[3].wait()

    return kernel


def join_kernel(token, one_ref, two_ref, out_ref):
    out_ref[:HEAD] = one_ref[:]
    out_ref[HEAD:] = two_ref[:]


def sun_kernel(sources, kbins):
    count = len(sources)
    inputs = 1 + max(operand for operand, _ in sources)

    def kernel(coef_ref, *refs):
        heads, outs, (acc, pattern, block) = refs[:inputs], refs[inputs : inputs + count], refs[inputs + count :]
        rows = heads[0].shape[1]
        nbins = coef_ref.shape[0]
        step = CHUNK * LANES
        spans = [(first, min(first + step, nbins)) for first in range(0, nbins, step)]
        lane = lax.broadcasted_iota(jnp.int32, (rows, LANES), 1)
        for g in range(count):
            operand, offset = sources[g]
            small = heads[operand][offset : offset + HEAD].astype(jnp.float32).T
            value = jnp.zeros((rows, LANES), jnp.float32)
            where = jnp.zeros((rows, LANES), jnp.float32)
            for k in range(kbins):
                low = small[:, 2 * kbins + k : 2 * kbins + k + 1].astype(jnp.int32)
                hit = lane == low
                value = jnp.where(hit, small[:, k : k + 1], value)
                where = jnp.where(hit, small[:, kbins + k : kbins + k + 1], where)
            pattern[g * rows : (g + 1) * rows] = value.astype(pattern.dtype)
            block[g * rows : (g + 1) * rows] = where.astype(block.dtype)

        for first, end in spans:
            parts = []
            for c in range(first // LANES, pl.cdiv(end, LANES)):
                here = block[:] == jnp.asarray(c, block.dtype)
                parts.append(jnp.where(here, pattern[:], jnp.zeros_like(pattern)).astype(jnp.bfloat16))
            weights = jnp.concatenate(parts, axis=1) if len(parts) > 1 else parts[0]
            part = jnp.dot(weights[:, : end - first], coef_ref[first:end], preferred_element_type=jnp.float32)
            acc[:] = part if first == 0 else acc[:] + part

        for g in range(count):
            sun = acc[g * rows : (g + 1) * rows]
            power = jnp.ceil(jnp.log2(jnp.maximum(jnp.max(sun, axis=0, keepdims=True), 1e-30)))
            code = jnp.round(sun * (LEVELS / jnp.exp2(power)) - 0.5 * LEVELS)
            code = code.astype(jnp.int32).astype(jnp.int16)
            cuts = [slice(c, c + LANES) for c in range(0, code.shape[1], LANES)]
            for c, cut in enumerate(cuts):
                outs[g][c * rows : (c + 1) * rows] = code[:, cut]
            tail = [power[:, cut] for cut in cuts] + [jnp.zeros((TAIL - len(cuts), LANES), jnp.float32)]
            outs[g][len(cuts) * rows :] = jnp.concatenate(tail, axis=0).astype(jnp.int32).astype(jnp.int16)

    return kernel


def base_kernel(
    token, sky_hbm, open_hbm, closed_hbm, target_hbm, cross_ref, closed_out, target_out, sky_ref, open_ref, closed_ref, sems
):
    pairs = [(sky_hbm, sky_ref), (open_hbm, open_ref), (closed_hbm, closed_ref), (target_hbm, target_out)]
    copies = fetch(pairs, sems)
    for c in copies[:3]:
        c.wait()
    over = (((0,), (0,)), ((), ()))
    closed = lax.dot_general(sky_ref[:], closed_ref[:], over, preferred_element_type=jnp.float32)
    opened = lax.dot_general(sky_ref[:], open_ref[:], over, preferred_element_type=jnp.float32)
    closed_out[:] = closed
    cross_ref[:] = opened - closed
    copies[3].wait()


def place(me_ref, mask, width):
    return pl.ds(pl.multiple_of((me_ref[0] ^ mask) * width, LANES), width)


def cross_of(codes, base):
    rows, width = base.shape
    columns = width // LANES
    scales = jnp.exp2(codes[columns * rows :].astype(jnp.int32).astype(jnp.float32)) / LEVELS
    suns = []
    for c in range(columns):
        code = codes[c * rows : (c + 1) * rows].astype(jnp.int32).astype(jnp.float32)
        suns.append((code + 0.5 * LEVELS) * scales[c : c + 1])
    return base + jnp.concatenate(suns, axis=1)


def grad_terms(me_ref, base_ref, closed_ref, target_ref, codes, crosses, masks, linear, square):
    rows, width = base_ref.shape[0], linear.shape[1]
    for mask, code, cross_ref in zip(masks, codes, crosses):
        at = place(me_ref, mask, width)
        cross = cross_of(code, base_ref[:, at])
        cross_ref[:] = cross
        apart = closed_ref[:, at] - target_ref[:, at].astype(jnp.float32)
        linear = linear + jnp.sum((apart * cross).reshape(rows // 8, 8, width), axis=0)
        square = square + jnp.sum((cross * cross).reshape(rows // 8, 8, width), axis=0)
    return linear, square


def first_kernel(masks):
    count = len(masks)

    def kernel(me_ref, base_ref, closed_ref, target_ref, *refs):
        codes, crosses, out_ref = refs[:count], refs[count : 2 * count], refs[-1]
        zero = jnp.zeros(out_ref.shape[1:], jnp.float32)
        out_ref[0], out_ref[1] = grad_terms(
            me_ref, base_ref, closed_ref, target_ref, codes, crosses, masks, zero, zero
        )

    return kernel


def second_kernel(masks, zones):
    count = len(masks)

    def kernel(me_ref, own_ref, base_ref, closed_ref, target_ref, first_ref, sums_ref, *refs):
        codes, crosses, out_ref = refs[:count], refs[count : 2 * count], refs[-1]
        linear, square = grad_terms(
            me_ref, base_ref, closed_ref, target_ref, codes, crosses, masks, first_ref[0], first_ref[1]
        )
        lane = lax.broadcasted_iota(jnp.int32, sums_ref.shape, 1)
        row = jnp.where(lane == own_ref[0], 2.0 * jnp.sum(linear, keepdims=True), sums_ref[:])
        row = jnp.where(lane == own_ref[0] + zones, 2.0 * jnp.sum(square, keepdims=True), row)
        out_ref[:] = jnp.broadcast_to(row[None], out_ref.shape)

    return kernel


def last_kernel(groups, zones, windows):
    def kernel(place_ref, own_ref, heard_ref, zone_ref, area_ref, openness_ref, closed_ref, *refs):
        crosses, (lit_ref, step_ref) = refs[:groups], refs[groups:]
        total = jnp.sum(heard_ref[:], axis=0)
        linear, quadratic, num, den, squares = [total[:, i * zones : (i + 1) * zones] for i in range(5)]
        share = num / den
        lane = lax.broadcasted_iota(jnp.int32, share.shape, 1)
        own_share = jnp.sum(jnp.where(lane == own_ref[0], share, 0.0), keepdims=True)
        width = closed_ref.shape[1] // groups
        for mask in range(groups):
            at = place(place_ref, mask, width)
            lit = closed_ref[:, at] + own_share * crosses[mask][:]
            lit_ref[:, at] = lit.astype(jnp.bfloat16)
        ratio = groups * (linear + share * quadratic) / den
        rms = jnp.sqrt(jnp.sum(ratio * ratio * squares, keepdims=True) / (windows * groups) + 1e-06)
        zone = zone_ref[:]
        chosen = jnp.zeros(zone.shape, jnp.float32)
        for z in range(zones):
            chosen = jnp.where(zone == z, ratio[:, z : z + 1], chosen)
        step_ref[:] = jnp.clip(openness_ref[:] - 0.25 * (area_ref[:] * chosen) / rms, 0.0, 1.0)

    return kernel


def local(sky, sky_open, sky_closed, sun_coef, sun_bins, sun_rad, target, zone_of, area, openness):
    zones = lax.axis_size("sens")
    groups = lax.axis_size("hour")
    me = lax.axis_index("hour").astype(jnp.int32)[None]
    own_zone = lax.axis_index("sens").astype(jnp.int32)[None]
    rows, patches = sky.shape
    kbins = sun_bins.shape[1]
    nbins, width = sun_coef.shape
    hours = rows * groups
    sensors = groups * width
    windows = area.shape[0]
    assert nbins % LANES == 0 or nbins % LANES >= 2 * kbins
    assert nbins <= 256 * LANES and width % LANES == 0 and windows % LANES == 0 and 3 * kbins <= HEAD
    assert groups == 4 and rows % 16 == 0
    shape = jax.ShapeDtypeStruct
    f32, bf16 = jnp.float32, jnp.bfloat16
    dma = lambda n: pltpu.SemaphoreType.DMA((n,))

    packed = call(
        pack_kernel,
        "pack",
        shape((HEAD, rows), bf16),
        in_specs=[SMEM, SMEM, HBM, HBM],
        scratch_shapes=[pltpu.VMEM((kbins, rows), jnp.int32), pltpu.VMEM((kbins, rows), bf16), dma(2)],
    )(me, own_zone, sun_bins.T, sun_rad.T)
    far = exchange(packed, "hour", 2)

    tiles = (windows // LANES, LANES)
    message = pl.cdiv(5 * zones, LANES) * LANES
    coef, zone_sums, zone2, area2, openness2 = call(
        fetch_kernel(zones),
        "fetch",
        [shape((nbins, width), bf16), shape((1, message), f32)]
        + [shape(tiles, jnp.int32), shape(tiles, f32), shape(tiles, f32)],
        in_specs=[HBM] * 4,
        out_specs=[VMEM] * 5,
        scratch_shapes=[dma(4)],
    )(sun_coef, zone_of.reshape(tiles), area.reshape(tiles), openness.reshape(tiles))

    both = call(join_kernel, "join", shape((2 * HEAD, rows), bf16), in_specs=[ANY] + [VMEM] * 2)(zone_sums, packed, far)
    near = exchange(both, "hour", 1)

    assert width // LANES <= TAIL

    def sun(sources, *heads):
        count = len(sources)
        scratch = [pltpu.VMEM((count * rows, width), f32)] + [pltpu.VMEM((count * rows, LANES), PATTERN)] * 2
        return call(
            sun_kernel(sources, kbins),
            "sun",
            [shape((width // LANES * rows + TAIL, LANES), jnp.int16)] * count,
            in_specs=[VMEM] * (1 + len(heads)),
            out_specs=[VMEM] * count,
            scratch_shapes=scratch,
        )(coef, *heads)

    codes = [None] * groups
    (codes[2],) = sun([(0, 0)], far)
    codes[1], codes[3] = sun([(0, 0), (0, HEAD)], near)
    (codes[0],) = sun([(0, 0)], packed)
    codes = [exchange(code, "hour", mask) if mask else code for mask, code in enumerate(codes)]

    base, closed, wanted = call(
        base_kernel,
        "base",
        [shape((rows, sensors), f32)] * 2 + [shape((rows, sensors), bf16)],
        in_specs=[ANY] + [HBM] * 4,
        out_specs=[VMEM] * 3,
        scratch_shapes=[
            pltpu.VMEM((patches, rows), bf16),
            pltpu.VMEM((patches, sensors), bf16),
            pltpu.VMEM((patches, sensors), bf16),
            dma(4),
        ],
    )(codes[0], sky.T, sky_open, sky_closed, target)
    first, second = [2, 0], [1, 3]
    block = shape((rows, width), f32)
    *first_crosses, first_sums = call(
        first_kernel(first),
        "first",
        [block] * len(first) + [shape((2, 8, width), f32)],
        in_specs=[SMEM] + [VMEM] * (3 + len(first)),
        out_specs=[VMEM] * (1 + len(first)),
    )(me, base, closed, wanted, *[codes[mask] for mask in first])
    *second_crosses, sent = call(
        second_kernel(second, zones),
        "second",
        [block] * len(second) + [shape((zones * groups, 1, message), f32)],
        in_specs=[SMEM] * 2 + [VMEM] * (5 + len(second)),
        out_specs=[VMEM] * (1 + len(second)),
    )(me, own_zone, base, closed, wanted, first_sums, zone_sums, *[codes[mask] for mask in second])
    crosses = dict(zip(first + second, first_crosses + second_crosses))
    heard = lax.all_to_all(sent, ("hour", "sens"), 0, 0)
    illuminance, new_openness = call(
        last_kernel(groups, zones, windows * zones),
        "last",
        [shape((rows, sensors), bf16), shape(tiles, f32)],
        in_specs=[SMEM] * 2 + [VMEM] * (5 + groups),
    )(me, own_zone, heard, zone2, area2, openness2, closed, *[crosses[mask] for mask in range(groups)])
    return (illuminance, new_openness.reshape(-1))


def solution(mesh):
    in_specs = (
        P("hour", None),
        P(None, "sens"),
        P(None, "sens"),
        P(None, ("sens", "hour")),
        P("hour", None),
        P("hour", None),
        P("hour", "sens"),
        P("sens", None),
        P("sens"),
        P("sens"),
    )
    out_specs = (P("hour", "sens"), P("sens"))
    return jax.shard_map(local, mesh=mesh, in_specs=in_specs, out_specs=out_specs, check_vma=False)
```

```python
import jax
import jax.numpy as jnp
from jax import lax
from jax.experimental import pallas as pl
from jax.experimental.pallas import tpu as pltpu
from jax.sharding import PartitionSpec as P

LANES = 128
CHUNK = 16
HEAD = 16
TAIL = 8
PATTERN = jnp.bfloat16
LEVELS = 65000.0
VMEM_BYTES = 12 * 1024 * 1024
ANY = pl.BlockSpec(memory_space=pl.ANY)
HBM = pl.BlockSpec(memory_space=pltpu.HBM)
SMEM = pl.BlockSpec(memory_space=pltpu.SMEM)
VMEM = pl.BlockSpec(memory_space=pltpu.VMEM)


def call(kernel, name, out_shape, flops=0, moved=0, **more):
    run = pl.pallas_call(
        kernel,
        out_shape=out_shape,
        name=name,
        compiler_params=pltpu.CompilerParams(vmem_limit_bytes=VMEM_BYTES),
        cost_estimate=pl.CostEstimate(flops=flops, bytes_accessed=moved, transcendentals=0),
        **more,
    )
    specs = more["in_specs"]
    return lambda *args: run(
        *[pltpu.with_memory_space_constraint(x, pltpu.HBM) if s is HBM else x for x, s in zip(args, specs)]
    )


def exchange(x, axis, mask):
    return lax.ppermute(x, axis, [(i, i ^ mask) for i in range(lax.axis_size(axis))])


def fetch(pairs, sems):
    copies = [pltpu.make_async_copy(source, place, sems.at[i]) for i, (source, place) in enumerate(pairs)]
    for c in copies:
        c.start()
    return copies


def pack_kernel(me_ref, own_ref, bins_hbm, rad_hbm, out_ref, bins_ref, rad_ref, sems):
    for c in fetch([(bins_hbm, bins_ref), (rad_hbm, rad_ref)], sems):
        c.wait()
    bins = bins_ref[:]
    kbins = bins.shape[0]
    fill = jnp.zeros((HEAD - 3 * kbins, bins.shape[1]), jnp.float32)
    parts = [rad_ref[:].astype(jnp.float32), (bins // LANES).astype(jnp.float32), (bins % LANES).astype(jnp.float32)]
    out_ref[:] = jnp.concatenate(parts + [fill], axis=0).astype(jnp.bfloat16)


def fetch_kernel(zones):
    def kernel(coef_hbm, zone_hbm, area_hbm, openness_hbm, coef_ref, sums_ref, zone_ref, area_ref, openness_ref, sems):
        pairs = [(zone_hbm, zone_ref), (area_hbm, area_ref), (openness_hbm, openness_ref)]
        copies = fetch(pairs + [(coef_hbm, coef_ref)], sems)
        for c in copies[:3]:
            c.wait()
        zone, area = zone_ref[:], area_ref[:]
        lane = lax.broadcasted_iota(jnp.int32, sums_ref.shape, 1)
        values = [area * openness_ref[:], area, area * area]
        row = jnp.zeros(sums_ref.shape, jnp.float32)
        for z in range(zones):
            member = zone == z
            for k, value in enumerate(values):
                total = jnp.sum(jnp.where(member, value, 0.0), keepdims=True)
                row = jnp.where(lane == (2 + k) * zones + z, total, row)
        sums_ref[:] = row
        copies[3].wait()

    return kernel


def join_kernel(token, one_ref, two_ref, out_ref):
    out_ref[:HEAD] = one_ref[:]
    out_ref[HEAD:] = two_ref[:]


def sun_kernel(sources, kbins):
    count = len(sources)
    inputs = 1 + max(operand for operand, _ in sources)

    def kernel(coef_ref, *refs):
        heads, outs, (acc, pattern, block) = refs[:inputs], refs[inputs : inputs + count], refs[inputs + count :]
        rows = heads[0].shape[1]
        nbins = coef_ref.shape[0]
        step = CHUNK * LANES
        spans = [(first, min(first + step, nbins)) for first in range(0, nbins, step)]
        lane = lax.broadcasted_iota(jnp.int32, (rows, LANES), 1)
        for g in range(count):
            operand, offset = sources[g]
            small = heads[operand][offset : offset + HEAD].astype(jnp.float32).T
            value = jnp.zeros((rows, LANES), jnp.float32)
            where = jnp.zeros((rows, LANES), jnp.float32)
            for k in range(kbins):
                low = small[:, 2 * kbins + k : 2 * kbins + k + 1].astype(jnp.int32)
                hit = lane == low
                value = jnp.where(hit, small[:, k : k + 1], value)
                where = jnp.where(hit, small[:, kbins + k : kbins + k + 1], where)
            pattern[g * rows : (g + 1) * rows] = value.astype(pattern.dtype)
            block[g * rows : (g + 1) * rows] = where.astype(block.dtype)

        for first, end in spans:
            parts = []
            for c in range(first // LANES, pl.cdiv(end, LANES)):
                here = block[:] == jnp.asarray(c, block.dtype)
                parts.append(jnp.where(here, pattern[:], jnp.zeros_like(pattern)).astype(jnp.bfloat16))
            weights = jnp.concatenate(parts, axis=1) if len(parts) > 1 else parts[0]
            part = jnp.dot(weights[:, : end - first], coef_ref[first:end], preferred_element_type=jnp.float32)
            acc[:] = part if first == 0 else acc[:] + part

        for g in range(count):
            sun = acc[g * rows : (g + 1) * rows]
            power = jnp.ceil(jnp.log2(jnp.maximum(jnp.max(sun, axis=0, keepdims=True), 1e-30)))
            code = jnp.round(sun * (LEVELS / jnp.exp2(power)) - 0.5 * LEVELS)
            code = code.astype(jnp.int32).astype(jnp.int16)
            cuts = [slice(c, c + LANES) for c in range(0, code.shape[1], LANES)]
            for c, cut in enumerate(cuts):
                outs[g][c * rows : (c + 1) * rows] = code[:, cut]
            tail = [power[:, cut] for cut in cuts] + [jnp.zeros((TAIL - len(cuts), LANES), jnp.float32)]
            outs[g][len(cuts) * rows :] = jnp.concatenate(tail, axis=0).astype(jnp.int32).astype(jnp.int16)

    return kernel


def base_kernel(
    token, sky_hbm, open_hbm, closed_hbm, target_hbm, cross_ref, closed_out, target_out, sky_ref, open_ref, closed_ref, sems
):
    pairs = [(sky_hbm, sky_ref), (open_hbm, open_ref), (closed_hbm, closed_ref), (target_hbm, target_out)]
    copies = fetch(pairs, sems)
    for c in copies[:3]:
        c.wait()
    over = (((0,), (0,)), ((), ()))
    closed = lax.dot_general(sky_ref[:], closed_ref[:], over, preferred_element_type=jnp.float32)
    opened = lax.dot_general(sky_ref[:], open_ref[:], over, preferred_element_type=jnp.float32)
    closed_out[:] = closed
    cross_ref[:] = opened - closed
    copies[3].wait()


def place(me_ref, mask, width):
    return pl.ds(pl.multiple_of((me_ref[0] ^ mask) * width, LANES), width)


def cross_of(codes, base):
    rows, width = base.shape
    columns = width // LANES
    scales = jnp.exp2(codes[columns * rows :].astype(jnp.int32).astype(jnp.float32)) / LEVELS
    suns = []
    for c in range(columns):
        code = codes[c * rows : (c + 1) * rows].astype(jnp.int32).astype(jnp.float32)
        suns.append((code + 0.5 * LEVELS) * scales[c : c + 1])
    return base + jnp.concatenate(suns, axis=1)


def grad_terms(me_ref, base_ref, closed_ref, target_ref, codes, crosses, masks, linear, square):
    rows, width = base_ref.shape[0], linear.shape[1]
    for mask, code, cross_ref in zip(masks, codes, crosses):
        at = place(me_ref, mask, width)
        cross = cross_of(code, base_ref[:, at])
        cross_ref[:] = cross
        apart = closed_ref[:, at] - target_ref[:, at].astype(jnp.float32)
        linear = linear + jnp.sum((apart * cross).reshape(rows // 8, 8, width), axis=0)
        square = square + jnp.sum((cross * cross).reshape(rows // 8, 8, width), axis=0)
    return linear, square


def first_kernel(masks):
    count = len(masks)

    def kernel(me_ref, base_ref, closed_ref, target_ref, *refs):
        codes, crosses, out_ref = refs[:count], refs[count : 2 * count], refs[-1]
        zero = jnp.zeros(out_ref.shape[1:], jnp.float32)
        out_ref[0], out_ref[1] = grad_terms(
            me_ref, base_ref, closed_ref, target_ref, codes, crosses, masks, zero, zero
        )

    return kernel


def second_kernel(masks, zones):
    count = len(masks)

    def kernel(me_ref, own_ref, base_ref, closed_ref, target_ref, first_ref, sums_ref, *refs):
        codes, crosses, out_ref = refs[:count], refs[count : 2 * count], refs[-1]
        linear, square = grad_terms(
            me_ref, base_ref, closed_ref, target_ref, codes, crosses, masks, first_ref[0], first_ref[1]
        )
        lane = lax.broadcasted_iota(jnp.int32, sums_ref.shape, 1)
        row = jnp.where(lane == own_ref[0], 2.0 * jnp.sum(linear, keepdims=True), sums_ref[:])
        row = jnp.where(lane == own_ref[0] + zones, 2.0 * jnp.sum(square, keepdims=True), row)
        out_ref[:] = jnp.broadcast_to(row[None], out_ref.shape)

    return kernel


def last_kernel(groups, zones, windows):
    def kernel(place_ref, own_ref, heard_ref, zone_ref, area_ref, openness_ref, closed_ref, *refs):
        crosses, (lit_ref, step_ref) = refs[:groups], refs[groups:]
        total = jnp.sum(heard_ref[:], axis=0)
        linear, quadratic, num, den, squares = [total[:, i * zones : (i + 1) * zones] for i in range(5)]
        share = num / den
        lane = lax.broadcasted_iota(jnp.int32, share.shape, 1)
        own_share = jnp.sum(jnp.where(lane == own_ref[0], share, 0.0), keepdims=True)
        width = closed_ref.shape[1] // groups
        for mask in range(groups):
            at = place(place_ref, mask, width)
            lit = closed_ref[:, at] + own_share * crosses[mask][:]
            lit_ref[:, at] = lit.astype(jnp.bfloat16)
        ratio = groups * (linear + share * quadratic) / den
        rms = jnp.sqrt(jnp.sum(ratio * ratio * squares, keepdims=True) / (windows * groups) + 1e-06)
        zone = zone_ref[:]
        chosen = jnp.zeros(zone.shape, jnp.float32)
        for z in range(zones):
            chosen = jnp.where(zone == z, ratio[:, z : z + 1], chosen)
        step_ref[:] = jnp.clip(openness_ref[:] - 0.25 * (area_ref[:] * chosen) / rms, 0.0, 1.0)

    return kernel


def local(sky, sky_open, sky_closed, sun_coef, sun_bins, sun_rad, target, zone_of, area, openness):
    zones = lax.axis_size("sens")
    groups = lax.axis_size("hour")
    me = lax.axis_index("hour").astype(jnp.int32)[None]
    own_zone = lax.axis_index("sens").astype(jnp.int32)[None]
    rows, patches = sky.shape
    kbins = sun_bins.shape[1]
    nbins, width = sun_coef.shape
    hours = rows * groups
    sensors = groups * width
    windows = area.shape[0]
    assert nbins % LANES == 0 or nbins % LANES >= 2 * kbins
    assert nbins <= 256 * LANES and width % LANES == 0 and windows % LANES == 0 and 3 * kbins <= HEAD
    assert groups == 4 and rows % 16 == 0
    shape = jax.ShapeDtypeStruct
    f32, bf16 = jnp.float32, jnp.bfloat16
    dma = lambda n: pltpu.SemaphoreType.DMA((n,))

    packed = call(
        pack_kernel,
        "pack",
        shape((HEAD, rows), bf16),
        in_specs=[SMEM, SMEM, HBM, HBM],
        scratch_shapes=[pltpu.VMEM((kbins, rows), jnp.int32), pltpu.VMEM((kbins, rows), bf16), dma(2)],
    )(me, own_zone, sun_bins.T, sun_rad.T)
    far = exchange(packed, "hour", 2)

    tiles = (windows // LANES, LANES)
    message = pl.cdiv(5 * zones, LANES) * LANES
    coef, zone_sums, zone2, area2, openness2 = call(
        fetch_kernel(zones),
        "fetch",
        [shape((nbins, width), bf16), shape((1, message), f32)]
        + [shape(tiles, jnp.int32), shape(tiles, f32), shape(tiles, f32)],
        in_specs=[HBM] * 4,
        out_specs=[VMEM] * 5,
        scratch_shapes=[dma(4)],
    )(sun_coef, zone_of.reshape(tiles), area.reshape(tiles), openness.reshape(tiles))

    both = call(join_kernel, "join", shape((2 * HEAD, rows), bf16), in_specs=[ANY] + [VMEM] * 2)(zone_sums, packed, far)
    near = exchange(both, "hour", 1)

    assert width // LANES <= TAIL

    def sun(sources, *heads):
        count = len(sources)
        scratch = [pltpu.VMEM((count * rows, width), f32)] + [pltpu.VMEM((count * rows, LANES), PATTERN)] * 2
        return call(
            sun_kernel(sources, kbins),
            "sun",
            [shape((width // LANES * rows + TAIL, LANES), jnp.int16)] * count,
            in_specs=[VMEM] * (1 + len(heads)),
            out_specs=[VMEM] * count,
            scratch_shapes=scratch,
        )(coef, *heads)

    codes = [None] * groups
    (codes[2],) = sun([(0, 0)], far)
    codes[1], codes[3] = sun([(0, 0), (0, HEAD)], near)
    (codes[0],) = sun([(0, 0)], packed)
    codes = [exchange(code, "hour", mask) if mask else code for mask, code in enumerate(codes)]

    base, closed, wanted = call(
        base_kernel,
        "base",
        [shape((rows, sensors), f32)] * 2 + [shape((rows, sensors), bf16)],
        in_specs=[ANY] + [HBM] * 4,
        out_specs=[VMEM] * 3,
        scratch_shapes=[
            pltpu.VMEM((patches, rows), bf16),
            pltpu.VMEM((patches, sensors), bf16),
            pltpu.VMEM((patches, sensors), bf16),
            dma(4),
        ],
    )(codes[0], sky.T, sky_open, sky_closed, target)
    first, second = [2, 0], [3, 1]
    block = shape((rows, width), f32)
    *first_crosses, first_sums = call(
        first_kernel(first),
        "first",
        [block] * len(first) + [shape((2, 8, width), f32)],
        in_specs=[SMEM] + [VMEM] * (3 + len(first)),
        out_specs=[VMEM] * (1 + len(first)),
    )(me, base, closed, wanted, *[codes[mask] for mask in first])
    *second_crosses, sent = call(
        second_kernel(second, zones),
        "second",
        [block] * len(second) + [shape((zones * groups, 1, message), f32)],
        in_specs=[SMEM] * 2 + [VMEM] * (5 + len(second)),
        out_specs=[VMEM] * (1 + len(second)),
    )(me, own_zone, base, closed, wanted, first_sums, zone_sums, *[codes[mask] for mask in second])
    crosses = dict(zip(first + second, first_crosses + second_crosses))
    heard = lax.all_to_all(sent, ("hour", "sens"), 0, 0)
    illuminance, new_openness = call(
        last_kernel(groups, zones, windows * zones),
        "last",
        [shape((rows, sensors), bf16), shape(tiles, f32)],
        in_specs=[SMEM] * 2 + [VMEM] * (5 + groups),
    )(me, own_zone, heard, zone2, area2, openness2, closed, *[crosses[mask] for mask in range(groups)])
    return (illuminance, new_openness.reshape(-1))


def solution(mesh):
    in_specs = (
        P("hour", None),
        P(None, "sens"),
        P(None, "sens"),
        P(None, ("sens", "hour")),
        P("hour", None),
        P("hour", None),
        P("hour", "sens"),
        P("sens", None),
        P("sens"),
        P("sens"),
    )
    out_specs = (P("hour", "sens"), P("sens"))
    return jax.shard_map(local, mesh=mesh, in_specs=in_specs, out_specs=out_specs, check_vma=False)
```

```python
import jax
import jax.numpy as jnp
from jax import lax
from jax.experimental import pallas as pl
from jax.experimental.pallas import tpu as pltpu
from jax.sharding import PartitionSpec as P

LANES = 128
CHUNK = 8
HEAD = 16
TAIL = 8
PATTERN = jnp.bfloat16
LEVELS = 65000.0
VMEM_BYTES = 12 * 1024 * 1024
ANY = pl.BlockSpec(memory_space=pl.ANY)
HBM = pl.BlockSpec(memory_space=pltpu.HBM)
SMEM = pl.BlockSpec(memory_space=pltpu.SMEM)
VMEM = pl.BlockSpec(memory_space=pltpu.VMEM)


def call(kernel, name, out_shape, flops=0, moved=0, **more):
    run = pl.pallas_call(
        kernel,
        out_shape=out_shape,
        name=name,
        compiler_params=pltpu.CompilerParams(vmem_limit_bytes=VMEM_BYTES),
        cost_estimate=pl.CostEstimate(flops=flops, bytes_accessed=moved, transcendentals=0),
        **more,
    )
    specs = more["in_specs"]
    return lambda *args: run(
        *[pltpu.with_memory_space_constraint(x, pltpu.HBM) if s is HBM else x for x, s in zip(args, specs)]
    )


def exchange(x, axis, mask):
    return lax.ppermute(x, axis, [(i, i ^ mask) for i in range(lax.axis_size(axis))])


def fetch(pairs, sems):
    copies = [pltpu.make_async_copy(source, place, sems.at[i]) for i, (source, place) in enumerate(pairs)]
    for c in copies:
        c.start()
    return copies


def pack_kernel(me_ref, own_ref, bins_hbm, rad_hbm, out_ref, bins_ref, rad_ref, sems):
    for c in fetch([(bins_hbm, bins_ref), (rad_hbm, rad_ref)], sems):
        c.wait()
    bins = bins_ref[:]
    kbins = bins.shape[0]
    fill = jnp.zeros((HEAD - 3 * kbins, bins.shape[1]), jnp.float32)
    parts = [rad_ref[:].astype(jnp.float32), (bins // LANES).astype(jnp.float32), (bins % LANES).astype(jnp.float32)]
    out_ref[:] = jnp.concatenate(parts + [fill], axis=0).astype(jnp.bfloat16)


def fetch_kernel(zones):
    def kernel(coef_hbm, zone_hbm, area_hbm, openness_hbm, coef_ref, sums_ref, zone_ref, area_ref, openness_ref, sems):
        pairs = [(zone_hbm, zone_ref), (area_hbm, area_ref), (openness_hbm, openness_ref)]
        copies = fetch(pairs + [(coef_hbm, coef_ref)], sems)
        for c in copies[:3]:
            c.wait()
        zone, area = zone_ref[:], area_ref[:]
        lane = lax.broadcasted_iota(jnp.int32, sums_ref.shape, 1)
        values = [area * openness_ref[:], area, area * area]
        row = jnp.zeros(sums_ref.shape, jnp.float32)
        for z in range(zones):
            member = zone == z
            for k, value in enumerate(values):
                total = jnp.sum(jnp.where(member, value, 0.0), keepdims=True)
                row = jnp.where(lane == (2 + k) * zones + z, total, row)
        sums_ref[:] = row
        copies[3].wait()

    return kernel


def join_kernel(token, one_ref, two_ref, out_ref):
    out_ref[:HEAD] = one_ref[:]
    out_ref[HEAD:] = two_ref[:]


def sun_kernel(sources, kbins):
    count = len(sources)
    inputs = 1 + max(operand for operand, _ in sources)

    def kernel(coef_ref, *refs):
        heads, outs, (acc, pattern, block) = refs[:inputs], refs[inputs : inputs + count], refs[inputs + count :]
        rows = heads[0].shape[1]
        nbins = coef_ref.shape[0]
        step = CHUNK * LANES
        spans = [(first, min(first + step, nbins)) for first in range(0, nbins, step)]
        lane = lax.broadcasted_iota(jnp.int32, (rows, LANES), 1)
        for g in range(count):
            operand, offset = sources[g]
            small = heads[operand][offset : offset + HEAD].astype(jnp.float32).T
            value = jnp.zeros((rows, LANES), jnp.float32)
            where = jnp.zeros((rows, LANES), jnp.float32)
            for k in range(kbins):
                low = small[:, 2 * kbins + k : 2 * kbins + k + 1].astype(jnp.int32)
                hit = lane == low
                value = jnp.where(hit, small[:, k : k + 1], value)
                where = jnp.where(hit, small[:, kbins + k : kbins + k + 1], where)
            pattern[g * rows : (g + 1) * rows] = value.astype(pattern.dtype)
            block[g * rows : (g + 1) * rows] = where.astype(block.dtype)

        for first, end in spans:
            parts = []
            for c in range(first // LANES, pl.cdiv(end, LANES)):
                here = block[:] == jnp.asarray(c, block.dtype)
                parts.append(jnp.where(here, pattern[:], jnp.zeros_like(pattern)).astype(jnp.bfloat16))
            weights = jnp.concatenate(parts, axis=1) if len(parts) > 1 else parts[0]
            part = jnp.dot(weights[:, : end - first], coef_ref[first:end], preferred_element_type=jnp.float32)
            acc[:] = part if first == 0 else acc[:] + part

        for g in range(count):
            sun = acc[g * rows : (g + 1) * rows]
            power = jnp.ceil(jnp.log2(jnp.maximum(jnp.max(sun, axis=0, keepdims=True), 1e-30)))
            code = jnp.round(sun * (LEVELS / jnp.exp2(power)) - 0.5 * LEVELS)
            code = code.astype(jnp.int32).astype(jnp.int16)
            cuts = [slice(c, c + LANES) for c in range(0, code.shape[1], LANES)]
            for c, cut in enumerate(cuts):
                outs[g][c * rows : (c + 1) * rows] = code[:, cut]
            tail = [power[:, cut] for cut in cuts] + [jnp.zeros((TAIL - len(cuts), LANES), jnp.float32)]
            outs[g][len(cuts) * rows :] = jnp.concatenate(tail, axis=0).astype(jnp.int32).astype(jnp.int16)

    return kernel


def base_kernel(
    token, sky_hbm, open_hbm, closed_hbm, target_hbm, cross_ref, closed_out, target_out, sky_ref, open_ref, closed_ref, sems
):
    pairs = [(sky_hbm, sky_ref), (open_hbm, open_ref), (closed_hbm, closed_ref), (target_hbm, target_out)]
    copies = fetch(pairs, sems)
    for c in copies[:3]:
        c.wait()
    over = (((0,), (0,)), ((), ()))
    closed = lax.dot_general(sky_ref[:], closed_ref[:], over, preferred_element_type=jnp.float32)
    opened = lax.dot_general(sky_ref[:], open_ref[:], over, preferred_element_type=jnp.float32)
    closed_out[:] = closed
    cross_ref[:] = opened - closed
    copies[3].wait()


def place(me_ref, mask, width):
    return pl.ds(pl.multiple_of((me_ref[0] ^ mask) * width, LANES), width)


def cross_of(codes, base):
    rows, width = base.shape
    columns = width // LANES
    scales = jnp.exp2(codes[columns * rows :].astype(jnp.int32).astype(jnp.float32)) / LEVELS
    suns = []
    for c in range(columns):
        code = codes[c * rows : (c + 1) * rows].astype(jnp.int32).astype(jnp.float32)
        suns.append((code + 0.5 * LEVELS) * scales[c : c + 1])
    return base + jnp.concatenate(suns, axis=1)


def grad_terms(me_ref, base_ref, closed_ref, target_ref, codes, crosses, masks, linear, square):
    rows, width = base_ref.shape[0], linear.shape[1]
    for mask, code, cross_ref in zip(masks, codes, crosses):
        at = place(me_ref, mask, width)
        cross = cross_of(code, base_ref[:, at])
        cross_ref[:] = cross
        apart = closed_ref[:, at] - target_ref[:, at].astype(jnp.float32)
        linear = linear + jnp.sum((apart * cross).reshape(rows // 8, 8, width), axis=0)
        square = square + jnp.sum((cross * cross).reshape(rows // 8, 8, width), axis=0)
    return linear, square


def first_kernel(masks):
    count = len(masks)

    def kernel(me_ref, base_ref, closed_ref, target_ref, *refs):
        codes, crosses, out_ref = refs[:count], refs[count : 2 * count], refs[-1]
        zero = jnp.zeros(out_ref.shape[1:], jnp.float32)
        out_ref[0], out_ref[1] = grad_terms(
            me_ref, base_ref, closed_ref, target_ref, codes, crosses, masks, zero, zero
        )

    return kernel


def second_kernel(masks, zones):
    count = len(masks)

    def kernel(me_ref, own_ref, base_ref, closed_ref, target_ref, first_ref, sums_ref, *refs):
        codes, crosses, out_ref = refs[:count], refs[count : 2 * count], refs[-1]
        linear, square = grad_terms(
            me_ref, base_ref, closed_ref, target_ref, codes, crosses, masks, first_ref[0], first_ref[1]
        )
        lane = lax.broadcasted_iota(jnp.int32, sums_ref.shape, 1)
        row = jnp.where(lane == own_ref[0], 2.0 * jnp.sum(linear, keepdims=True), sums_ref[:])
        row = jnp.where(lane == own_ref[0] + zones, 2.0 * jnp.sum(square, keepdims=True), row)
        out_ref[:] = jnp.broadcast_to(row[None], out_ref.shape)

    return kernel


def last_kernel(groups, zones, windows):
    def kernel(place_ref, own_ref, heard_ref, zone_ref, area_ref, openness_ref, closed_ref, *refs):
        crosses, (lit_hbm, step_ref, lit_ref, sems) = refs[:groups], refs[groups:]
        total = jnp.sum(heard_ref[:], axis=0)
        linear, quadratic, num, den, squares = [total[:, i * zones : (i + 1) * zones] for i in range(5)]
        share = num / den
        lane = lax.broadcasted_iota(jnp.int32, share.shape, 1)
        own_share = jnp.sum(jnp.where(lane == own_ref[0], share, 0.0), keepdims=True)
        width = closed_ref.shape[1] // groups
        part = closed_ref.shape[0] // groups
        copies = []
        for r in range(groups):
            some = pl.ds(r * part, part)
            for mask in range(groups):
                at = place(place_ref, mask, width)
                lit = closed_ref[some, at] + own_share * crosses[mask][some]
                lit_ref[some, at] = lit.astype(jnp.bfloat16)
            copies.append(pltpu.make_async_copy(lit_ref.at[some], lit_hbm.at[some], sems.at[r]))
            copies[r].start()
        ratio = groups * (linear + share * quadratic) / den
        rms = jnp.sqrt(jnp.sum(ratio * ratio * squares, keepdims=True) / (windows * groups) + 1e-06)
        zone = zone_ref[:]
        chosen = jnp.zeros(zone.shape, jnp.float32)
        for z in range(zones):
            chosen = jnp.where(zone == z, ratio[:, z : z + 1], chosen)
        step_ref[:] = jnp.clip(openness_ref[:] - 0.25 * (area_ref[:] * chosen) / rms, 0.0, 1.0)
        for c in copies:
            c.wait()

    return kernel


def local(sky, sky_open, sky_closed, sun_coef, sun_bins, sun_rad, target, zone_of, area, openness):
    zones = lax.axis_size("sens")
    groups = lax.axis_size("hour")
    me = lax.axis_index("hour").astype(jnp.int32)[None]
    own_zone = lax.axis_index("sens").astype(jnp.int32)[None]
    rows, patches = sky.shape
    kbins = sun_bins.shape[1]
    nbins, width = sun_coef.shape
    hours = rows * groups
    sensors = groups * width
    windows = area.shape[0]
    assert nbins % LANES == 0 or nbins % LANES >= 2 * kbins
    assert nbins <= 256 * LANES and width % LANES == 0 and windows % LANES == 0 and 3 * kbins <= HEAD
    assert groups == 4 and rows % (16 * groups) == 0
    shape = jax.ShapeDtypeStruct
    f32, bf16 = jnp.float32, jnp.bfloat16
    dma = lambda n: pltpu.SemaphoreType.DMA((n,))

    packed = call(
        pack_kernel,
        "pack",
        shape((HEAD, rows), bf16),
        in_specs=[SMEM, SMEM, HBM, HBM],
        scratch_shapes=[pltpu.VMEM((kbins, rows), jnp.int32), pltpu.VMEM((kbins, rows), bf16), dma(2)],
    )(me, own_zone, sun_bins.T, sun_rad.T)
    far = exchange(packed, "hour", 2)

    tiles = (windows // LANES, LANES)
    message = pl.cdiv(5 * zones, LANES) * LANES
    coef, zone_sums, zone2, area2, openness2 = call(
        fetch_kernel(zones),
        "fetch",
        [shape((nbins, width), bf16), shape((1, message), f32)]
        + [shape(tiles, jnp.int32), shape(tiles, f32), shape(tiles, f32)],
        in_specs=[HBM] * 4,
        out_specs=[VMEM] * 5,
        scratch_shapes=[dma(4)],
    )(sun_coef, zone_of.reshape(tiles), area.reshape(tiles), openness.reshape(tiles))

    both = call(join_kernel, "join", shape((2 * HEAD, rows), bf16), in_specs=[ANY] + [VMEM] * 2)(zone_sums, packed, far)
    near = exchange(both, "hour", 1)

    assert width // LANES <= TAIL

    def sun(sources, *heads):
        count = len(sources)
        scratch = [pltpu.VMEM((count * rows, width), f32)] + [pltpu.VMEM((count * rows, LANES), PATTERN)] * 2
        return call(
            sun_kernel(sources, kbins),
            "sun",
            [shape((width // LANES * rows + TAIL, LANES), jnp.int16)] * count,
            in_specs=[VMEM] * (1 + len(heads)),
            out_specs=[VMEM] * count,
            scratch_shapes=scratch,
        )(coef, *heads)

    codes = [None] * groups
    (codes[2],) = sun([(0, 0)], far)
    codes[1], codes[3] = sun([(0, 0), (0, HEAD)], near)
    (codes[0],) = sun([(0, 0)], packed)
    codes = [exchange(code, "hour", mask) if mask else code for mask, code in enumerate(codes)]

    base, closed, wanted = call(
        base_kernel,
        "base",
        [shape((rows, sensors), f32)] * 2 + [shape((rows, sensors), bf16)],
        in_specs=[ANY] + [HBM] * 4,
        out_specs=[VMEM] * 3,
        scratch_shapes=[
            pltpu.VMEM((patches, rows), bf16),
            pltpu.VMEM((patches, sensors), bf16),
            pltpu.VMEM((patches, sensors), bf16),
            dma(4),
        ],
    )(codes[0], sky.T, sky_open, sky_closed, target)
    first, second = [2, 0], [1, 3]
    block = shape((rows, width), f32)
    *first_crosses, first_sums = call(
        first_kernel(first),
        "first",
        [block] * len(first) + [shape((2, 8, width), f32)],
        in_specs=[SMEM] + [VMEM] * (3 + len(first)),
        out_specs=[VMEM] * (1 + len(first)),
    )(me, base, closed, wanted, *[codes[mask] for mask in first])
    *second_crosses, sent = call(
        second_kernel(second, zones),
        "second",
        [block] * len(second) + [shape((zones * groups, 1, message), f32)],
        in_specs=[SMEM] * 2 + [VMEM] * (5 + len(second)),
        out_specs=[VMEM] * (1 + len(second)),
    )(me, own_zone, base, closed, wanted, first_sums, zone_sums, *[codes[mask] for mask in second])
    crosses = dict(zip(first + second, first_crosses + second_crosses))
    heard = lax.all_to_all(sent, ("hour", "sens"), 0, 0)
    illuminance, new_openness = call(
        last_kernel(groups, zones, windows * zones),
        "last",
        [shape((rows, sensors), bf16), shape(tiles, f32)],
        in_specs=[SMEM] * 2 + [VMEM] * (5 + groups),
        out_specs=[HBM, VMEM],
        scratch_shapes=[pltpu.VMEM((rows, sensors), bf16), dma(groups)],
    )(me, own_zone, heard, zone2, area2, openness2, closed, *[crosses[mask] for mask in range(groups)])
    return (illuminance, new_openness.reshape(-1))


def solution(mesh):
    in_specs = (
        P("hour", None),
        P(None, "sens"),
        P(None, "sens"),
        P(None, ("sens", "hour")),
        P("hour", None),
        P("hour", None),
        P("hour", "sens"),
        P("sens", None),
        P("sens"),
        P("sens"),
    )
    out_specs = (P("hour", "sens"), P("sens"))
    return jax.shard_map(local, mesh=mesh, in_specs=in_specs, out_specs=out_specs, check_vma=False)
```
